32 devices in a mesh: row: 4 (over y, x), col: 8 (over z, core).
Axes of the slice: x: 2, y: 2, z: 4, core: 2. Of those that a mesh axis runs over, the one named last changes fastest.
Arguments:
- block_input: bfloat16 [4, 10240, 1088], P(None, ('row', 'col')), may hold values from -6 to 6
- paths: int32 [2, 4, 10240], P(None, None, 'row'), may hold values from 0 to 12, as said below
- ln1_gain: float32 [1088], replicated, may hold values from 0.1 to 1.9
- ln1_bias: float32 [1088], replicated, may hold values from -3 to 3
- w_qkv: bfloat16 [1088, 3264], P('row', 'col'), may hold values from -0.1875 to 0.1875
- q_bias: float32 [1088], replicated, may hold values from -3 to 3
- v_bias: float32 [1088], replicated, may hold values from -0.3 to 0.3
- w_out: bfloat16 [1088, 1088], P('row', 'col'), may hold values from -3 to 3
- out_bias: float32 [1088], replicated, may hold values from -3 to 3
- ln2_gain: float32 [1088], replicated, may hold values from 0.1 to 1.9
- ln2_bias: float32 [1088], replicated, may hold values from -3 to 3
- w_up: bfloat16 [1088, 4352], P('row', 'col'), may hold values from -0.1875 to 0.1875
- up_bias: float32 [4352], replicated, may hold values from -3 to 3
- w_down: bfloat16 [4352, 1088], P('col', 'row'), may hold values from -0.09375 to 0.09375
- down_bias: float32 [1088], replicated, may hold values from -3 to 3
- cotangent: bfloat16 [4, 10240, 1088], P(None, ('row', 'col')), may hold values from -6 to 6
Outputs:
- result: bfloat16 [4, 10240, 1088], P(None, ('row', 'col'))
- input_grad: bfloat16 [4, 10240, 1088], P(None, ('row', 'col'))
- ln1_gain_grad: float32 [1088], replicated
- ln1_bias_grad: float32 [1088], replicated
- w_qkv_grad: float32 [1088, 3264], P('row', 'col')
- q_bias_grad: float32 [1088], replicated
- v_bias_grad: float32 [1088], replicated
- w_out_grad: float32 [1088, 1088], P('row', 'col')
- out_bias_grad: float32 [1088], replicated
- ln2_gain_grad: float32 [1088], replicated
- ln2_bias_grad: float32 [1088], replicated
- w_up_grad: float32 [1088, 4352], P('row', 'col')
- up_bias_grad: float32 [4352], replicated
- w_down_grad: float32 [4352, 1088], P('col', 'row')
- down_bias_grad: float32 [1088], replicated
The draws below stay inside these ranges and needn't reach their ends.
Inputs may be any that keep to these rules, and one draw needn't show every extreme that they name: Within each tree, segment 0 is the trunk and takes the first 1024 rows; the remaining rows form 4 groups of three consecutive segments of 128 rows each: one branch (a segment b from 1 to 4) and its two leaves (segments 2b + 3 and 2b + 4, so 5 to 12), in an order within the group that may differ from group to group; the branch may stand before, between or after its leaves. paths[1] is 0 for the trunk and for branches, and a leaf's branch for a leaf. Every tree holds all 13 segments.
All inputs are finite; a program needn't handle non-finite values.
Results may differ from the reference program's by a relative error of at most 0.013.
Values may be sent and summed in bfloat16 or wider, within the bound.
A program may use at most 704 MiB of HBM per device.

```python
import jax
import jax.numpy as jnp
from jax import lax

HEAD_DIM = 64
D = 1088
FF = 4352
TRUNK = 1024
SEG = 128
BRANCHES = 4
MICRO = 4
TREE_LEN = 2560
ROWS = 10240


def draw_paths(key, part):
    key = jax.random.fold_in(key, 11)
    trees = MICRO * (ROWS // TREE_LEN)
    order_keys = jax.random.split(key, trees)
    orders = jax.vmap(lambda single: jax.random.permutation(single, BRANCHES))(order_keys)
    flips = jax.random.randint(jax.random.fold_in(key, 5), (trees, BRANCHES), 0, 2)
    slots = jax.random.randint(jax.random.fold_in(key, 7), (trees, BRANCHES), 0, 3)
    place = jnp.arange(TREE_LEN, dtype=jnp.int32)
    offset = jnp.maximum(place - TRUNK, 0) // SEG
    group = offset // 3
    within = offset % 3
    branch = orders[:, group].astype(jnp.int32)
    flip = flips[:, group].astype(jnp.int32)
    slot = slots[:, group].astype(jnp.int32)
    trunk = (place < TRUNK)[None, :]
    is_branch = within[None, :] == slot
    rank = jnp.where(within[None, :] > slot, within[None, :] - 1, within[None, :])
    leaf = BRANCHES + 1 + 2 * branch + jnp.where(rank == 0, flip, 1 - flip)
    own = jnp.where(trunk, 0, jnp.where(is_branch, branch + 1, leaf))
    parent = jnp.where(trunk | is_branch, 0, branch + 1)
    return jnp.stack([own, parent]).reshape(2, MICRO, ROWS).astype(jnp.int32)


def levels(own_key, shape, cuts, least, high):
    def one(dim, parts):
        steps = jax.random.uniform(jax.random.fold_in(jax.random.fold_in(own_key, 6), dim), (parts,), jnp.float32, least / len(cuts), high / len(cuts))
        return jnp.repeat(jnp.exp(steps), shape[dim] // parts).reshape((-1,) + (1,) * (len(shape) - dim - 1))

    factor_of = one(*cuts[0])
    for cut in cuts[1:]:
        factor_of = factor_of * one(*cut)
    return factor_of


def bell_draw(stream_key, dims, scale, bound, cuts=(), held_as=jnp.bfloat16):
    entries = jax.random.normal(stream_key, dims, jnp.float32) * scale
    if len(cuts) > 0:
        entries = levels(stream_key, dims, cuts, -0.22, 0.18) * entries
    return jnp.clip(entries, min=-bound, max=bound).astype(held_as)


def setup_inputs(seed: int = 0) -> dict:
    seeds = jax.random.split(jax.random.key(seed), 17)
    block_input = bell_draw(seeds[0], (MICRO, ROWS, D), 1.0, 6.0, ((1, 32),))
    paths = draw_paths(jax.random.fold_in(seeds[16], 71), 0)
    ln1_gain = jnp.clip(1.0 + 0.18 * jax.random.normal(seeds[2], (D,), jnp.float32), 0.1, 1.9)
    ln1_bias = bell_draw(seeds[3], (D,), 0.3, 3.0, (), jnp.float32)
    w_qkv = bell_draw(seeds[4], (D, 3 * D), D ** -0.5, 0.1875, ((0, 4), (1, 8)))
    q_bias = bell_draw(seeds[5], (D,), 0.5, 3.0, (), jnp.float32)
    v_bias = bell_draw(seeds[6], (D,), 0.05, 0.3, (), jnp.float32)
    w_out = bell_draw(seeds[7], (D, D), (max(D // 256, 1)) ** -0.5, 3.0, ((0, 4), (1, 8)))
    out_bias = bell_draw(seeds[8], (D,), 0.3, 3.0, (), jnp.float32)
    ln2_gain = jnp.clip(1.0 + 0.18 * jax.random.normal(seeds[9], (D,), jnp.float32), 0.1, 1.9)
    ln2_bias = bell_draw(seeds[10], (D,), 0.3, 3.0, (), jnp.float32)
    w_up = bell_draw(seeds[11], (D, FF), D ** -0.5, 0.1875, ((0, 4), (1, 8)))
    up_bias = bell_draw(seeds[12], (FF,), 0.3, 3.0, (), jnp.float32)
    w_down = bell_draw(seeds[13], (FF, D), FF ** -0.5, 0.09375, ((0, 8), (1, 4)))
    down_bias = bell_draw(seeds[14], (D,), 0.3, 3.0, (), jnp.float32)
    cotangent = bell_draw(seeds[15], (MICRO, ROWS, D), 1.0, 6.0, ((1, 32),))
    return dict(block_input=block_input, paths=paths, ln1_gain=ln1_gain, ln1_bias=ln1_bias, w_qkv=w_qkv, q_bias=q_bias, v_bias=v_bias, w_out=w_out, out_bias=out_bias, ln2_gain=ln2_gain, ln2_bias=ln2_bias, w_up=w_up, up_bias=up_bias, w_down=w_down, down_bias=down_bias, cotangent=cotangent)


HIGH = lax.Precision.HIGHEST

@jax.custom_vjp
def low(v):
    return lax.optimization_barrier(v.astype(jnp.bfloat16)).astype(jnp.float32)

@jax.custom_vjp
def low_back(v):
    return v

def low_keep(v):
    return (low(v), None)

def low_pass(kept, grad):
    return (grad,)

def back_keep(v):
    return (v, None)

def back_low(kept, grad):
    return (low(grad),)
low.defvjp(low_keep, low_pass)
low_back.defvjp(back_keep, back_low)

def product(left, right):
    return jnp.dot(left, right, precision=HIGH, preferred_element_type=jnp.float32)

def layer_norm(value, gain, bias):
    center = value - lax.optimization_barrier(jnp.mean(value, axis=-1, keepdims=True))
    spread = lax.optimization_barrier(jnp.mean(center * center, axis=-1, keepdims=True))
    return center * lax.rsqrt(spread + 1e-05) * gain + bias

def attention(query, keys, values, own, parent):
    length = query.shape[0]
    block = 512 if length % 512 == 0 else length
    heads = query.shape[1] // HEAD_DIM
    scale = HEAD_DIM ** (-0.5)
    query_blocks = query.reshape(length // block, block, heads, HEAD_DIM)
    keys_heads = keys.reshape(length, heads, HEAD_DIM)
    values_heads = values.reshape(length, heads, HEAD_DIM)
    own_blocks = own.reshape(length // block, block)
    parent_blocks = parent.reshape(length // block, block)
    places = jnp.arange(length, dtype=jnp.int32)
    place_blocks = places.reshape(length // block, block)

    def one_block(items):
        query_block, own_block, parent_block, place_block = items
        scores = jnp.einsum('qhd,khd->hqk', query_block, keys_heads, precision=HIGH) * scale
        visible = (places[None, :] <= place_block[:, None]) & ((own[None, :] == 0) | (own[None, :] == own_block[:, None]) | (own[None, :] == parent_block[:, None]))
        scores = jnp.where(visible[None], scores, -1e+30)
        scores = low_back(scores)
        shares = low(jax.nn.softmax(scores, axis=-1))
        mixed = jnp.einsum('hqk,khd->qhd', shares, values_heads, precision=HIGH)
        return mixed.reshape(block, heads * HEAD_DIM)
    mixed = lax.map(jax.checkpoint(one_block), (query_blocks, own_blocks, parent_blocks, place_blocks))
    return mixed.reshape(length, heads * HEAD_DIM)

def block_forward(inputs, own, parent, params):
    ln1_gain, ln1_bias, w_qkv, q_bias, v_bias, w_out, out_bias, ln2_gain, ln2_bias, w_up, up_bias, w_down, down_bias = params
    width = inputs.shape[1]
    first = low(layer_norm(inputs, ln1_gain, ln1_bias))
    triple_bias = jnp.concatenate([q_bias, jnp.zeros_like(q_bias), v_bias])
    triple = low_back(low(product(first, w_qkv) + triple_bias))
    mixed = attention(triple[:, :width], triple[:, width:2 * width], triple[:, 2 * width:], own, parent)
    mixed = low_back(low(mixed))
    attended = low_back(low(product(mixed, w_out) + out_bias))
    middle = inputs + attended
    second = low(layer_norm(middle, ln2_gain, ln2_bias))
    widened = low_back(product(second, w_up) + up_bias)
    activated = low(jax.nn.gelu(widened, approximate=False))
    return middle + product(activated, w_down) + down_bias

def reference(block_input, paths, ln1_gain, ln1_bias, w_qkv, q_bias, v_bias, w_out, out_bias, ln2_gain, ln2_bias, w_up, up_bias, w_down, down_bias, cotangent):
    trees = MICRO * (ROWS // TREE_LEN)
    inputs = block_input.astype(jnp.float32).reshape(trees, TREE_LEN, D)
    upstream = cotangent.astype(jnp.float32).reshape(trees, TREE_LEN, D)
    own = paths[0].reshape(trees, TREE_LEN)
    parent = paths[1].reshape(trees, TREE_LEN)
    params = (ln1_gain.astype(jnp.float32), ln1_bias.astype(jnp.float32), w_qkv.astype(jnp.float32), q_bias.astype(jnp.float32), v_bias.astype(jnp.float32), w_out.astype(jnp.float32), out_bias.astype(jnp.float32), ln2_gain.astype(jnp.float32), ln2_bias.astype(jnp.float32), w_up.astype(jnp.float32), up_bias.astype(jnp.float32), w_down.astype(jnp.float32), down_bias.astype(jnp.float32))
    zeros = jax.tree.map(jnp.zeros_like, params)

    def step(totals, items):
        tree_in, tree_own, tree_parent, tree_up = items

        def forward(value, weights):
            return block_forward(value, tree_own, tree_parent, weights)
        output, pullback = jax.vjp(forward, tree_in, params)
        grad_in, grad_params = pullback(tree_up)
        totals = jax.tree.map(jnp.add, totals, grad_params)
        return (totals, (output.astype(jnp.bfloat16), grad_in.astype(jnp.bfloat16)))
    totals, (outputs, grads) = lax.scan(step, zeros, (inputs, own, parent, upstream))
    result = outputs.reshape(MICRO, ROWS, D)
    input_grad = grads.reshape(MICRO, ROWS, D)
    return (result, input_grad, totals[0], totals[1], totals[2], totals[3], totals[4], totals[5], totals[6], totals[7], totals[8], totals[9], totals[10], totals[11], totals[12])
```

```python
import math
from functools import partial

import jax
import jax.numpy as jnp
import numpy as np
from jax import lax
from jax.experimental import pallas as pl
from jax.experimental.pallas import tpu as pltpu
from jax.sharding import PartitionSpec as P

HEAD_DIM = 64
TRUNK = 1024
GROUP = 384
QT = 256
LOG2E = 1.4426950408889634
LN2 = 0.6931471805599453


def dot_nn(a, b):
    return jnp.dot(a, b, preferred_element_type=jnp.float32)


def dot_nt(a, b):
    return lax.dot_general(a, b, (((1,), (1,)), ((), ())), preferred_element_type=jnp.float32)


def dot_tn(a, b):
    return lax.dot_general(a, b, (((0,), (0,)), ((), ())), preferred_element_type=jnp.float32)


def lane_masks(head):
    lane = lax.broadcasted_iota(jnp.int32, (1, 128), 1)
    inside = (lane // HEAD_DIM) == head
    return inside, inside.astype(jnp.float32).astype(jnp.bfloat16), lane % HEAD_DIM


def fill_trunk(parts, own_ref, other_ref, out_ref):
    own = TRUNK // parts
    for tile in range(own // QT):
        for part in range(parts):
            rows = (
                own_ref[tile * QT : (tile + 1) * QT, :]
                if part == 0
                else other_ref[(part - 1) * own + tile * QT : (part - 1) * own + (tile + 1) * QT, :]
            )
            start = (tile * parts + part) * QT
            out_ref[start : start + QT, :] = rows


def fwd_kernel(parts, heads, start, extra, q_ref, k_ref, v_ref, ko_ref, vo_ref, mt_ref, mg_ref, *refs):
    o_ref, lse_ref, kt, vt, va = refs[extra:]
    pair = start + pl.program_id(0)
    own = TRUNK // parts
    tiles = own // QT
    groups = (TRUNK // 256) // parts
    fill_trunk(parts, k_ref, ko_ref, kt)
    fill_trunk(parts, v_ref, vo_ref, vt)
    o_ref[...] = jnp.zeros_like(o_ref)
    lse_ref[...] = jnp.zeros_like(lse_ref)

    def finish(rows, top, total, inside):
        turned = pltpu.roll(total, HEAD_DIM, 1)
        o_ref[rows, :] += jnp.where(inside, total / turned, 0.0).astype(jnp.bfloat16)
        lse_ref[rows, :] += jnp.where(inside, 0.0, top + jnp.log2(total))

    def head_body(head, carry):
        inside, hm, _ = lane_masks(head)
        rest = 1 - hm
        va[...] = vt[...] * hm + rest
        for tile in range(tiles):
            rows = pl.ds(tile * QT, QT)
            q = q_ref[rows, :] * hm
            near = tile * parts * QT
            s_near = dot_nt(q, kt[near : near + parts * QT, :]) + mt_ref[tile]
            top = jnp.max(s_near, axis=1, keepdims=True)
            if tile > 0:
                s_far = dot_nt(q, kt[:near, :])
                top = jnp.maximum(top, jnp.max(s_far, axis=1, keepdims=True))
            p_near = jnp.exp2(s_near - top).astype(jnp.bfloat16)
            total = dot_nn(p_near, va[near : near + parts * QT, :])
            if tile > 0:
                total += dot_nn(jnp.exp2(s_far - top).astype(jnp.bfloat16), va[:near, :])
            finish(rows, top, total, inside)

        def group_body(group, carry):
            rows = pl.ds(pl.multiple_of(own + group * GROUP, 128), GROUP)
            q = q_ref[rows, :] * hm
            s_near = dot_nt(q, k_ref[rows, :]) + mg_ref[group]
            s_far = dot_nt(q, kt[...])
            top = jnp.maximum(
                jnp.max(s_near, axis=1, keepdims=True), jnp.max(s_far, axis=1, keepdims=True)
            )
            near = v_ref[rows, :] * hm + rest
            total = dot_nn(jnp.exp2(s_near - top).astype(jnp.bfloat16), near)
            total += dot_nn(jnp.exp2(s_far - top).astype(jnp.bfloat16), va[...])
            finish(rows, top, total, inside)
            return carry

        return lax.fori_loop(0, groups, group_body, carry)

    lax.fori_loop(0, jnp.minimum(2, heads - 2 * pair), head_body, 0)


def attention_forward(parts, heads, triple, others, mask_trunk, mask_group, start, stop, deps=()):
    rows = triple.shape[0]
    pairs = triple.shape[1] // (3 * 128)
    extra = others.shape[0]
    block = lambda count, shift: pl.BlockSpec((count, 128), lambda i: (0, i + shift))
    whole = lambda shape: pl.BlockSpec(shape, lambda i: (0,) * len(shape))
    return pl.pallas_call(
        partial(fwd_kernel, parts, heads, start, len(deps)),
        grid=(stop - start,),
        in_specs=[
            block(rows, start),
            block(rows, start + pairs),
            block(rows, start + 2 * pairs),
            block(extra, start),
            block(extra, start + pairs),
            whole(mask_trunk.shape),
            whole(mask_group.shape),
        ]
        + [pl.BlockSpec(memory_space=pl.ANY)] * len(deps),
        out_specs=[block(rows, 0), block(rows, 0)],
        out_shape=[
            jax.ShapeDtypeStruct((rows, (stop - start) * 128), jnp.bfloat16),
            jax.ShapeDtypeStruct((rows, (stop - start) * 128), jnp.float32),
        ],
        scratch_shapes=[
            pltpu.VMEM((TRUNK, 128), jnp.bfloat16),
            pltpu.VMEM((TRUNK, 128), jnp.bfloat16),
            pltpu.VMEM((TRUNK, 128), jnp.bfloat16),
        ],
        compiler_params=pltpu.CompilerParams(vmem_limit_bytes=48 * 1024 * 1024),
        cost_estimate=pl.CostEstimate(
            flops=(stop - start) * rows * 6_800_000, bytes_accessed=rows * pairs * 2000, transcendentals=0
        ),
        name="attention_forward",
    )(triple, triple, triple, others, others, mask_trunk, mask_group, *deps)


def split_three(value, place, outside):
    high = value.astype(jnp.bfloat16)
    left = value - high.astype(jnp.float32)
    middle = left.astype(jnp.bfloat16)
    low = (left - middle.astype(jnp.float32)).astype(jnp.bfloat16)
    high, middle, low = (v.astype(jnp.float32) for v in (high, middle, low))
    picked = jnp.where(place == 0, high, jnp.where(place == 1, middle, jnp.where(place == 2, low, 0.0)))
    return jnp.where(outside, picked, 0.0).astype(jnp.bfloat16)


def bwd_kernel(
    parts, heads, start, extra, q_ref, k_ref, v_ref, ko_ref, vo_ref, o_ref, do_ref, lse_ref, mt_ref, mg_ref,
    *refs,
):
    dq_ref, dk_ref, dv_ref, dko_ref, dvo_ref = refs[extra : extra + 5]
    kt, vt, ka, va, qa, da, qm, dm, dkt, dvt, dkg, dvg, dqs = refs[extra + 5 :]
    pair = start + pl.program_id(0)
    own = TRUNK // parts
    tiles = own // QT
    groups = (TRUNK // 256) // parts
    rows_all = own + groups * GROUP
    fill_trunk(parts, k_ref, ko_ref, kt)
    fill_trunk(parts, v_ref, vo_ref, vt)
    dkt[...] = jnp.zeros_like(dkt)
    dvt[...] = jnp.zeros_like(dvt)
    dkg[...] = jnp.zeros_like(dkg)
    dvg[...] = jnp.zeros_like(dvg)
    dqs[...] = jnp.zeros_like(dqs)

    def head_body(head, carry):
        inside, hm, place = lane_masks(head)
        rest = 1 - hm
        outside = jnp.logical_not(inside)
        ka[:TRUNK, :] = kt[...] * hm + rest
        va[:TRUNK, :] = vt[...] * hm + rest
        ka[TRUNK:, :] = k_ref[own:, :] * hm + rest
        va[TRUNK:, :] = v_ref[own:, :] * hm + rest

        def prepare(step, carry):
            rows = pl.ds(pl.multiple_of(step * 128, 128), 128)
            q = q_ref[rows, :] * hm
            d = do_ref[rows, :] * hm
            qm[rows, :] = q
            dm[rows, :] = d
            qa[rows, :] = q - split_three(lse_ref[rows, :], place, outside)
            delta = jnp.sum(
                d.astype(jnp.float32) * o_ref[rows, :].astype(jnp.float32), axis=1, keepdims=True
            )
            da[rows, :] = d - split_three(jnp.broadcast_to(delta, (128, 128)), place, outside)
            return carry

        lax.fori_loop(0, rows_all // 128, prepare, 0)

        def step(rows, keys, mask, keep, dk, dv):
            st = dot_nt(ka[keys, :], qa[rows, :])
            if mask is not None:
                st = st + mask
            p = jnp.exp2(st)
            dp = dot_nt(va[keys, :], da[rows, :])
            ds = (p * dp).astype(jnp.bfloat16)
            dv[keep, :] += dot_nn(p.astype(jnp.bfloat16), dm[rows, :])
            dk[keep, :] += dot_nn(ds, qm[rows, :])
            dqs[rows, :] += jnp.where(inside, dot_tn(ds, ka[keys, :]), 0.0)

        span = parts * QT
        for tile in range(tiles):
            rows = pl.ds(tile * QT, QT)
            for near in range(tile + 1):
                keys = pl.ds(near * span, span)
                step(rows, keys, mt_ref[tile] if near == tile else None, keys, dkt, dvt)
        count = QT if (groups * GROUP) % QT == 0 else 128

        def far_body(index, carry):
            rows = pl.ds(pl.multiple_of(own + index * count, 128), count)
            keys = pl.ds(0, TRUNK)
            step(rows, keys, None, keys, dkt, dvt)
            return carry

        lax.fori_loop(0, groups * GROUP // count, far_body, 0)

        def near_body(group, carry):
            rows = pl.ds(pl.multiple_of(own + group * GROUP, 128), GROUP)
            keys = pl.ds(pl.multiple_of(TRUNK + group * GROUP, 128), GROUP)
            keep = pl.ds(pl.multiple_of(group * GROUP, 128), GROUP)
            step(rows, keys, mg_ref[group], keep, dkg, dvg)
            return carry

        return lax.fori_loop(0, groups, near_body, carry)

    lax.fori_loop(0, jnp.minimum(2, heads - 2 * pair), head_body, 0)
    dq_ref[...] = (dqs[...] * HEAD_DIM**-0.5).astype(jnp.bfloat16)
    dk_ref[own:, :] = dkg[...] * LN2
    dv_ref[own:, :] = dvg[...]
    for tile in range(tiles):
        for part in range(parts):
            source = pl.ds((tile * parts + part) * QT, QT)
            if part == 0:
                dk_ref[tile * QT : (tile + 1) * QT, :] = dkt[source, :] * LN2
                dv_ref[tile * QT : (tile + 1) * QT, :] = dvt[source, :]
            else:
                start = (part - 1) * own + tile * QT
                dko_ref[start : start + QT, :] = (dkt[source, :] * LN2).astype(jnp.bfloat16)
                dvo_ref[start : start + QT, :] = dvt[source, :].astype(jnp.bfloat16)


def attention_backward(
    parts, heads, triple, others, mixed, mixed_grad, lse, mask_trunk, mask_group, start, stop, deps=()
):
    rows = triple.shape[0]
    pairs = triple.shape[1] // (3 * 128)
    extra = others.shape[0]
    block = lambda count, shift: pl.BlockSpec((count, 128), lambda i: (0, i + shift))
    whole = lambda shape: pl.BlockSpec(shape, lambda i: (0,) * len(shape))
    near = rows - TRUNK // parts
    return pl.pallas_call(
        partial(bwd_kernel, parts, heads, start, len(deps)),
        grid=(stop - start,),
        in_specs=[
            block(rows, start),
            block(rows, start + pairs),
            block(rows, start + 2 * pairs),
            block(extra, start),
            block(extra, start + pairs),
            block(rows, start),
            block(rows, start),
            block(rows, start),
            whole(mask_trunk.shape),
            whole(mask_group.shape),
        ]
        + [pl.BlockSpec(memory_space=pl.ANY)] * len(deps),
        out_specs=[block(rows, 0), block(rows, 0), block(rows, 0), block(extra, 0), block(extra, 0)],
        out_shape=[
            jax.ShapeDtypeStruct((rows, (stop - start) * 128), jnp.bfloat16),
            jax.ShapeDtypeStruct((rows, (stop - start) * 128), jnp.float32),
            jax.ShapeDtypeStruct((rows, (stop - start) * 128), jnp.float32),
            jax.ShapeDtypeStruct((extra, (stop - start) * 128), jnp.bfloat16),
            jax.ShapeDtypeStruct((extra, (stop - start) * 128), jnp.bfloat16),
        ],
        scratch_shapes=[
            pltpu.VMEM((TRUNK, 128), jnp.bfloat16),
            pltpu.VMEM((TRUNK, 128), jnp.bfloat16),
            pltpu.VMEM((TRUNK + near, 128), jnp.bfloat16),
            pltpu.VMEM((TRUNK + near, 128), jnp.bfloat16),
            pltpu.VMEM((rows, 128), jnp.bfloat16),
            pltpu.VMEM((rows, 128), jnp.bfloat16),
            pltpu.VMEM((rows, 128), jnp.bfloat16),
            pltpu.VMEM((rows, 128), jnp.bfloat16),
            pltpu.VMEM((TRUNK, 128), jnp.float32),
            pltpu.VMEM((TRUNK, 128), jnp.float32),
            pltpu.VMEM((near, 128), jnp.float32),
            pltpu.VMEM((near, 128), jnp.float32),
            pltpu.VMEM((rows, 128), jnp.float32),
        ],
        compiler_params=pltpu.CompilerParams(vmem_limit_bytes=56 * 1024 * 1024),
        cost_estimate=pl.CostEstimate(
            flops=(stop - start) * rows * 12_200_000, bytes_accessed=rows * pairs * 4000, transcendentals=0
        ),
        name="attention_backward",
    )(triple, triple, triple, others, others, mixed, mixed_grad, lse, mask_trunk, mask_group, *deps)


ERF_TOP = (
    -2.72614225801306e-10, 2.77068142495902e-08, -2.10102402082508e-06, -5.69250639462346e-05,
    -7.34990630326855e-04, -2.95459980854025e-03, -1.60960333262415e-02,
)
ERF_LOW = (
    -1.45660718464996e-05, -2.13374055278905e-04, -1.68282697438203e-03, -7.37332916720468e-03,
    -1.42647390514189e-02,
)


def erf_float(value):
    value = jnp.clip(value, -3.832506856900711, 3.832506856900711)
    square = value * value
    top = jnp.full_like(value, ERF_TOP[0])
    for c in ERF_TOP[1:]:
        top = top * square + c
    low = jnp.full_like(value, ERF_LOW[0])
    for c in ERF_LOW[1:]:
        low = low * square + c
    return value * top / low


FF_BLOCK = 256
ROW_CHUNK = 640


def ffn_kernel(
    sizes, outs, chunk, scalars, *refs,
):
    count = len(sizes)
    mine, theirs = refs[:count], refs[count : 2 * count]
    second, second_t, seed, seed_t, bias = refs[2 * count : 2 * count + 5]
    edge = 2 * count + 8
    lowered, second_grad, bias_grad = refs[2 * count + 5 : edge]
    mine_grads, theirs_grads = refs[edge : edge + outs], refs[edge + outs : edge + 2 * outs]
    up, down, act, wide, up_grad, down_grad = refs[edge + 2 * outs :]
    step = pl.program_id(0)
    role = scalars[0]

    def place(first_part, second_part):
        for index, size in enumerate(sizes):
            rows = pl.ds(pl.multiple_of(scalars[1 + index], 16), size)
            up[rows, :] = first_part[index][...]
            down[rows, :] = second_part[index][...]

    @pl.when(role == 0)
    def _():
        place(mine, theirs)

    @pl.when(role != 0)
    def _():
        place(theirs, mine)

    @pl.when(step == 0)
    def _():
        lowered[...] = jnp.zeros_like(lowered)
        second_grad[...] = jnp.zeros_like(second_grad)

    total = jnp.zeros((1, FF_BLOCK), jnp.float32)
    for start in range(0, second.shape[0], chunk):
        rows = pl.ds(start, chunk)
        wide_in = dot_nn(second[rows, :], up[...]) + bias[...]
        hidden = dot_nn(seed[rows, :], down[...])
        share = 0.5 + 0.5 * erf_float(wide_in * 0.7071067811865476)
        act_now = (wide_in * share).astype(jnp.bfloat16)
        slope = share + wide_in * (jnp.exp(-0.5 * wide_in * wide_in) * 0.3989422804014327)
        wide_now = (hidden * slope).astype(jnp.bfloat16)
        total += jnp.sum(wide_now.astype(jnp.float32), axis=0, keepdims=True)
        act[rows, :] = act_now
        wide[rows, :] = wide_now
        lowered[rows, :] += dot_nt(act_now, down[...])
        second_grad[rows, :] += dot_nt(wide_now, up[...])
    bias_grad[...] = total
    up_grad[...] = dot_nn(second_t[...], wide[...]).astype(jnp.bfloat16)
    down_grad[...] = dot_nn(seed_t[...], act[...]).astype(jnp.bfloat16)

    def deliver(first_grad, second_grad):
        for index in range(outs):
            size = mine_grads[index].shape[0]
            rows = pl.ds(pl.multiple_of(scalars[1 + index], 16), size)
            mine_grads[index][...] = first_grad[rows, :]
            theirs_grads[index][...] = second_grad[rows, :]

    @pl.when(role == 0)
    def _():
        deliver(up_grad, down_grad)

    @pl.when(role != 0)
    def _():
        deliver(down_grad, up_grad)


def feed_forward(scalars, mine, theirs, second, seed, bias, outs):
    rows, width = second.shape
    hidden = mine[0].shape[1]
    sizes = tuple(piece.shape[0] for piece in mine)
    piece_specs = [pl.BlockSpec((size, FF_BLOCK), lambda j, s: (0, j)) for size in sizes]
    whole = lambda shape: pl.BlockSpec(shape, lambda j, s: (0, 0))
    grad_spec = pl.BlockSpec((width // outs, FF_BLOCK), lambda j, s: (0, j))
    grad_shape = jax.ShapeDtypeStruct((width // outs, hidden), jnp.bfloat16)
    line = pl.BlockSpec((1, FF_BLOCK), lambda j, s: (0, j))
    chunk = ROW_CHUNK if rows % ROW_CHUNK == 0 else rows // 2
    return pl.pallas_call(
        partial(ffn_kernel, sizes, outs, chunk),
        grid_spec=pltpu.PrefetchScalarGridSpec(
            num_scalar_prefetch=1,
            grid=(hidden // FF_BLOCK,),
            in_specs=piece_specs * 2 + [
                whole((rows, width)), whole((width, rows)), whole((rows, width)), whole((width, rows)), line,
            ],
            out_specs=[whole((rows, width)), whole((rows, width)), line] + [grad_spec] * (2 * outs),
            scratch_shapes=[
                pltpu.VMEM((width, FF_BLOCK), jnp.bfloat16),
                pltpu.VMEM((width, FF_BLOCK), jnp.bfloat16),
                pltpu.VMEM((rows, FF_BLOCK), jnp.bfloat16),
                pltpu.VMEM((rows, FF_BLOCK), jnp.bfloat16),
                pltpu.VMEM((width, FF_BLOCK), jnp.bfloat16),
                pltpu.VMEM((width, FF_BLOCK), jnp.bfloat16),
            ],
        ),
        out_shape=[
            jax.ShapeDtypeStruct((rows, width), jnp.float32),
            jax.ShapeDtypeStruct((rows, width), jnp.float32),
            jax.ShapeDtypeStruct((1, hidden), jnp.float32),
        ]
        + [grad_shape] * (2 * outs),
        compiler_params=pltpu.CompilerParams(vmem_limit_bytes=60 * 1024 * 1024),
        cost_estimate=pl.CostEstimate(
            flops=24 * rows * width * hidden, bytes_accessed=8 * width * hidden + 20 * rows * width,
            transcendentals=rows * hidden,
        ),
        name="feed_forward",
    )(scalars, *mine, *theirs, second, second.T, seed, seed.T, bias.reshape(1, hidden))


def layer_norm(value, gain, bias):
    center = value - jnp.mean(value, axis=-1, keepdims=True)
    spread = jnp.mean(center * center, axis=-1, keepdims=True)
    return center * lax.rsqrt(spread + 1e-05) * gain + bias


def own_rows(parts, part):
    blocks = TRUNK // (128 * parts)
    starts = []
    for k in range(blocks):
        base = (k // 2) * 2 * parts
        starts.append(128 * (base + (part if k % 2 == 0 else 2 * parts - 1 - part)))
    rows = [np.arange(128) + s for s in starts]
    groups = (TRUNK // 256) // parts
    rows.append(TRUNK + part * groups * GROUP + np.arange(groups * GROUP))
    return np.concatenate(rows)


def spread_kernel(grain, table, *refs):
    pieces, out = refs[:-1], refs[-1]
    each = pieces[0].shape[0] // grain
    for index, piece in enumerate(pieces):
        for i in range(each):
            target = table[index * each + i]

            @pl.when(target >= 0)
            def _():
                rows = pl.ds(pl.multiple_of(target * grain, grain), grain)
                out[rows, :] = piece[i * grain : (i + 1) * grain, :]


def spread(table, pieces, grain, count):
    width = pieces[0].shape[1]
    whole = lambda rows: pl.BlockSpec((rows, width), lambda i, s: (0, 0))
    return pl.pallas_call(
        partial(spread_kernel, grain),
        grid_spec=pltpu.PrefetchScalarGridSpec(
            num_scalar_prefetch=1,
            grid=(1,),
            in_specs=[whole(p.shape[0]) for p in pieces],
            out_specs=whole(count),
        ),
        out_shape=jax.ShapeDtypeStruct((count, width), pieces[0].dtype),
        compiler_params=pltpu.CompilerParams(vmem_limit_bytes=48 * 1024 * 1024),
        cost_estimate=pl.CostEstimate(flops=0, bytes_accessed=6 * count * width, transcendentals=0),
        name="spread_rows",
    )(table, *pieces)


def collect_kernel(grain, count, table, *refs):
    sources, outs = refs[:-count], refs[-count:]
    each = outs[0].shape[0] // grain
    for index, out in enumerate(outs):
        for i in range(each):
            owner = table[2 * (index * each + i)]
            start = table[2 * (index * each + i) + 1]
            for which, source in enumerate(sources):

                @pl.when(owner == which)
                def _():
                    rows = pl.ds(pl.multiple_of(start * grain, grain), grain)
                    out[i * grain : (i + 1) * grain, :] = source[rows, :]


def collect(table, sources, grain, count, length):
    width = sources[0].shape[1]
    whole = lambda rows: pl.BlockSpec((rows, width), lambda i, s: (0, 0))
    return pl.pallas_call(
        partial(collect_kernel, grain, count),
        grid_spec=pltpu.PrefetchScalarGridSpec(
            num_scalar_prefetch=1,
            grid=(1,),
            in_specs=[whole(s.shape[0]) for s in sources],
            out_specs=[whole(length)] * count,
        ),
        out_shape=[jax.ShapeDtypeStruct((length, width), sources[0].dtype)] * count,
        compiler_params=pltpu.CompilerParams(vmem_limit_bytes=48 * 1024 * 1024),
        cost_estimate=pl.CostEstimate(flops=0, bytes_accessed=6 * count * length * width, transcendentals=0),
        name="collect_rows",
    )(table, *sources)


class Place:
    def __init__(self, micro, tree):
        self.columns = lax.axis_size("col")
        self.micro = micro
        self.parts = self.columns // micro
        self.tree = tree
        self.length = tree // self.columns
        self.grain = math.gcd(self.length, 128)
        me = lax.axis_index("col")
        self.quarter, self.part = me // self.parts, me % self.parts
        self.own = np.stack([own_rows(self.parts, part) for part in range(self.parts)])
        self.count = self.own.shape[1]

    def quarter_perm(self, shift):
        p = self.parts
        return [(c, ((c // p) ^ shift) * p + c % p) for c in range(self.columns)]

    def part_perm(self, shift):
        return [(c, c ^ shift) for c in range(self.columns)]

    def swap_quarters(self, value):
        groups = [
            [q * self.parts + part for q in range(self.micro)] for part in range(self.parts)
        ]
        return lax.all_to_all(value, "col", 0, 0, axis_index_groups=groups, tiled=True)

    def to_tree_sources(self, value):
        mine = self.swap_quarters(value).reshape(self.micro * self.length, value.shape[2])
        return [mine] + [lax.ppermute(mine, "col", self.part_perm(e)) for e in range(1, self.parts)]

    def to_tree(self, sources):
        grain, each = self.grain, self.length // self.grain
        table = np.full((self.parts, self.tree // grain), -1, np.int32)
        for part in range(self.parts):
            table[part, self.own[part, ::grain] // grain] = np.arange(self.count // grain)
        mine = lax.dynamic_index_in_dim(jnp.asarray(table), self.part, 0, keepdims=False)
        e, rest = np.divmod(np.arange(self.tree // grain, dtype=np.int32), self.micro * each)
        quarter, inside = np.divmod(rest, each)
        chunk = (quarter * self.parts + (self.part ^ e)) * each + inside
        return spread(mine[chunk], sources, grain, self.count)

    def from_tree_sources(self, value):
        return [value] + [lax.ppermute(value, "col", self.part_perm(e)) for e in range(1, self.parts)]

    def from_tree_parts(self, sources):
        grain, each, parts = self.grain, self.length // self.grain, self.parts
        owner = np.zeros(self.tree // grain, np.int32)
        local = np.zeros(self.tree // grain, np.int32)
        for part in range(parts):
            owner[self.own[part, ::grain] // grain] = part
            local[self.own[part, ::grain] // grain] = np.arange(self.count // grain)
        quarter, inside = np.divmod(np.arange(self.micro * each, dtype=np.int32), each)
        chunk = (quarter * parts + self.part) * each + inside
        table = jnp.stack([jnp.asarray(owner)[chunk] ^ self.part, jnp.asarray(local)[chunk]], axis=1)
        (out,) = collect(table.reshape(-1), sources, grain, 1, self.micro * self.length)
        return out.reshape(self.micro, self.length, sources[0].shape[1])

    def masks(self, own_ids, parent_ids):
        parts = self.parts
        own = jnp.asarray(self.own, jnp.int32)
        mine = lax.dynamic_index_in_dim(own, self.part, 0, keepdims=False)
        trunk_rows = TRUNK // parts
        tiles = trunk_rows // QT
        trunk = []
        for tile in range(tiles):
            span = slice(tile * QT, (tile + 1) * QT)
            keys = jnp.concatenate(
                [
                    lax.dynamic_index_in_dim(own, self.part ^ e, 0, keepdims=False)[span]
                    for e in range(parts)
                ]
            )
            trunk.append(jnp.where(keys[None, :] <= mine[span][:, None], 0.0, -1e30))
        group = []
        groups = (TRUNK // 256) // parts
        places = jnp.arange(GROUP)
        for g in range(groups):
            start = TRUNK + (self.part * groups + g) * GROUP
            ids = lax.dynamic_slice_in_dim(own_ids, start, GROUP)
            parent = lax.dynamic_slice_in_dim(parent_ids, start, GROUP)
            seen = (places[None, :] <= places[:, None]) & (
                (ids[None, :] == 0) | (ids[None, :] == ids[:, None]) | (ids[None, :] == parent[:, None])
            )
            group.append(jnp.where(seen, 0.0, -1e30))
        return jnp.stack(trunk).astype(jnp.float32), jnp.stack(group).astype(jnp.float32)


BOTH = ("row", "col")
ROW_CUT = 144


def plain_gather(block):
    full = lax.all_gather(block, BOTH, axis=0, tiled=False)
    full = full.reshape(lax.axis_size("row"), lax.axis_size("col"), *block.shape)
    return full.transpose(0, 2, 1, 3).reshape(full.shape[0] * full.shape[2], full.shape[1] * full.shape[3])


def plain_scatter(grad):
    rows, cols = lax.axis_size("row"), lax.axis_size("col")
    blocks = grad.astype(jnp.bfloat16).reshape(rows, grad.shape[0] // rows, cols, grad.shape[1] // cols)
    blocks = blocks.transpose(0, 2, 1, 3).reshape(rows * cols, grad.shape[0] // rows, grad.shape[1] // cols)
    return lax.psum_scatter(blocks, BOTH, scatter_dimension=0, tiled=False).astype(jnp.float32)


def across(value, shift):
    return lax.ppermute(value, "row", [(r, r ^ shift) for r in range(lax.axis_size("row"))])


def row_gather(block):
    beside = across(block, 1)
    below = across(block, 2)
    return [block, beside, below, across(beside[:ROW_CUT], 2), across(below[ROW_CUT:], 1)]


def row_starts(rows):
    me = lax.axis_index("row")
    far = (me ^ 3) * rows
    return [me * rows, (me ^ 1) * rows, (me ^ 2) * rows, far, far + ROW_CUT]


def core_swap(place, value):
    return lax.ppermute(value, "col", place.part_perm(1))


def far_sums(own, swapped):
    f32, bf16 = jnp.float32, jnp.bfloat16
    add = lambda d, part: (own[d][part].astype(f32) + swapped[d][part].astype(f32)).astype(bf16)
    top, bottom = slice(0, ROW_CUT), slice(ROW_CUT, None)
    return add(3, top), add(3, bottom), add(1, bottom), add(2, top)


def far_sends(sums):
    return across(sums[0], 2), across(sums[1], 1), across(sums[2], 1), across(sums[3], 2)


def near_sums(own, swapped, received):
    f32 = jnp.float32
    beside = own[1][:ROW_CUT].astype(f32) + swapped[1][:ROW_CUT].astype(f32) + received[0].astype(f32)
    below = own[2][ROW_CUT:].astype(f32) + swapped[2][ROW_CUT:].astype(f32) + received[1].astype(f32)
    return beside.astype(jnp.bfloat16), below.astype(jnp.bfloat16)


def near_sends(sums):
    return across(sums[0], 1), across(sums[1], 2)


def row_total(own, swapped, received, last):
    f32 = jnp.float32
    base = own[0].astype(f32) + swapped[0].astype(f32)
    beside = jnp.concatenate([last[0], received[2]], axis=0).astype(f32)
    below = jnp.concatenate([received[3], last[1]], axis=0).astype(f32)
    return (base + beside + below).astype(jnp.bfloat16)


def column_scatter(place, pick):
    total = pick(0)
    for d in range(1, place.micro):
        total = total + lax.ppermute(
            pick(d).astype(jnp.bfloat16), "col", place.quarter_perm(d)
        ).astype(jnp.float32)
    return total


def sum_all(values):
    sizes = [v.shape[0] for v in values]
    flat = jnp.concatenate(values)
    flat = jnp.pad(flat, (0, -flat.shape[0] % 1024)).reshape(-1, 128)
    for axis in ("col", "row"):
        size = lax.axis_size(axis)
        shift = 1
        while shift < size:
            flat = flat + lax.ppermute(flat, axis, [(i, i ^ shift) for i in range(size)])
            shift *= 2
    flat = flat.reshape(-1)
    out, start = [], 0
    for size in sizes:
        out.append(flat[start : start + size])
        start += size
    return out


def assemble_kernel(sizes, edge, scalars, *refs):
    count = len(sizes)
    mine, theirs = refs[:count], refs[count : 2 * count]
    triple, out = refs[2 * count :]
    step = pl.program_id(0)
    use_mine = (step < edge) == (scalars[0] == 0)
    total = sum(sizes)

    def fill(target, pieces):
        for index, size in enumerate(sizes):
            rows = pl.ds(pl.multiple_of(scalars[1 + index], 16), size)
            target[rows, :] = pieces[index][...]

    for own in (True, False):
        for low in (True, False):

            @pl.when(jnp.logical_and(use_mine == own, (step < edge + edge // 2) == low))
            def _():
                fill(triple if low else out, mine if own else theirs)

    @pl.when(step >= edge + edge // 2)
    def _():
        out[total:, :] = jnp.zeros((out.shape[0] - total, out.shape[1]), out.dtype)


def assemble(scalars, mine, theirs, padded):
    block = 384
    edge = 2 * padded // block
    sizes = tuple(piece.shape[0] for piece in mine)
    width = sum(sizes)

    def source(own):
        def index(j, s):
            first = (s[0] == 0) if own else (s[0] != 0)
            return (0, jnp.where(first, jnp.minimum(j, edge - 1), jnp.maximum(j - edge, 0)))

        return [pl.BlockSpec((size, block), index) for size in sizes]

    return pl.pallas_call(
        partial(assemble_kernel, sizes, edge),
        grid_spec=pltpu.PrefetchScalarGridSpec(
            num_scalar_prefetch=1,
            grid=(2 * edge,),
            in_specs=source(True) + source(False),
            out_specs=[
                pl.BlockSpec((width, block), lambda j, s: (0, jnp.minimum(j, 3 * edge // 2 - 1))),
                pl.BlockSpec((padded, block), lambda j, s: (0, jnp.maximum(j - 3 * edge // 2, 0))),
            ],
        ),
        out_shape=[
            jax.ShapeDtypeStruct((width, 3 * padded), jnp.bfloat16),
            jax.ShapeDtypeStruct((padded, padded), jnp.bfloat16),
        ],
        compiler_params=pltpu.CompilerParams(vmem_limit_bytes=48 * 1024 * 1024),
        cost_estimate=pl.CostEstimate(flops=0, bytes_accessed=16 * width * padded, transcendentals=0),
        name="assemble_weights",
    )(scalars, *mine, *theirs)


class QuickWeights:
    def __init__(self, place, w_qkv, w_out, w_up, w_down, padded):
        self.place, self.padded = place, padded
        self.rows = w_qkv.shape[0]
        self.cols = place.columns
        self.width = w_out.shape[1] * self.cols
        self.qkv_cols, self.out_cols, self.up_cols = w_qkv.shape[1], w_out.shape[1], w_up.shape[1]
        self.main = self.up_cols // 256 * 256
        self.rest = self.up_cols - self.main
        starts = row_starts(self.rows)
        self.role = place.part
        self.scalars = jnp.stack([self.role] + starts).astype(jnp.int32)
        pad = padded - self.width

        pack = jnp.concatenate([w_qkv, w_out], axis=1)
        full = lax.all_gather(pack, "col", axis=0, tiled=False).transpose(1, 0, 2)
        qkv = full[:, :, : self.qkv_cols].reshape(self.rows, 3, self.width)
        out = full[:, :, self.qkv_cols :].reshape(self.rows, 1, self.width)
        four = jnp.pad(jnp.concatenate([qkv, out], axis=1), ((0, 0), (0, 0), (0, pad)))
        mine = jnp.where(self.role == 0, four[:, :2], four[:, 2:]).reshape(self.rows, 2 * padded)
        mine = row_gather(mine)
        theirs = [core_swap(place, piece) for piece in mine]
        self.triple, self.out = assemble(self.scalars, mine, theirs, padded)

        main = self.main
        down = w_down.T
        pack = jnp.concatenate([w_up[:, :main], down[:, :main], w_up[:, main:], down[:, main:]], axis=1)
        full = lax.all_gather(pack, "col", axis=0, tiled=False)
        rest = self.rest

        def role_part(role):
            body = full[:, :, role * main : (role + 1) * main].transpose(1, 0, 2)
            tail = full[:, :, 2 * main + role * rest : 2 * main + (role + 1) * rest].transpose(1, 0, 2)
            return jnp.concatenate(
                [body.reshape(self.rows, self.cols * main), tail.reshape(self.rows, self.cols * rest)], axis=1
            )

        self.mine = row_gather(jnp.where(self.role == 0, role_part(0), role_part(1)))
        self.theirs = [core_swap(place, piece) for piece in self.mine]

    def bias_order(self, bias):
        blocks = bias.reshape(self.cols, self.up_cols)
        return jnp.concatenate([blocks[:, : self.main].reshape(-1), blocks[:, self.main :].reshape(-1)])

    def bias_back(self, grad):
        edge = self.cols * self.main
        return jnp.concatenate(
            [grad[:edge].reshape(self.cols, self.main), grad[edge:].reshape(self.cols, self.rest)], axis=1
        ).reshape(-1)

    def pair_total(self, total):
        place = self.place
        other = core_swap(place, total)
        edge = self.cols * self.main

        def pick(d):
            shard = (place.quarter ^ d) * place.parts + place.part
            out = []
            for start, size in ((0, self.main), (edge, self.rest)):
                for value in (total, other):
                    out.append(lax.dynamic_slice_in_dim(value, start + shard * size, size, 1))
            return jnp.concatenate(out, axis=1).astype(jnp.float32)

        final = column_scatter(place, pick)
        main, rest = self.main, self.rest
        own = jnp.concatenate([final[:, :main], final[:, 2 * main : 2 * main + rest]], axis=1)
        far = jnp.concatenate([final[:, main : 2 * main], final[:, 2 * main + rest :]], axis=1)
        up = jnp.where(self.role == 0, own, far)
        down = jnp.where(self.role == 0, far, own)
        return up, down.T

    def first_pieces(self, triple_grad, out_grad):
        padded, rows = self.padded, self.rows
        low = triple_grad[:, : 2 * padded]
        high = jnp.concatenate([triple_grad[:, 2 * padded :], out_grad], axis=1)
        mine = jnp.where(self.role == 0, low, high)
        theirs = jnp.where(self.role == 0, high, low)
        me = lax.axis_index("row")
        cut = lambda value: [
            lax.dynamic_slice_in_dim(value, (me ^ d) * rows, rows, 0) for d in range(4)
        ]
        return cut(mine), cut(theirs)

    def first_total(self, total):
        place, padded, width = self.place, self.padded, self.width
        other = core_swap(place, total)
        low = jnp.where(self.role == 0, total, other).reshape(self.rows, 2, padded)
        high = jnp.where(self.role == 0, other, total).reshape(self.rows, 2, padded)
        four = jnp.concatenate([low, high], axis=1)[:, :, :width]
        qkv = four[:, :3].reshape(self.rows, self.cols, self.qkv_cols)
        out = four[:, 3].reshape(self.rows, self.cols, self.out_cols)
        blocks = jnp.concatenate([qkv, out], axis=2).transpose(1, 0, 2)

        def pick(d):
            shard = (place.quarter ^ d) * place.parts + place.part
            return lax.dynamic_index_in_dim(blocks, shard, 0, keepdims=False).astype(jnp.float32)

        final = column_scatter(place, pick)
        return final[:, : self.qkv_cols], final[:, self.qkv_cols :]


class PlainWeights:
    def __init__(self, place, w_qkv, w_out, w_up, w_down, padded):
        self.place, self.padded = place, padded
        qkv, out = plain_gather(w_qkv), plain_gather(w_out)
        self.width = width = out.shape[1]
        pad = padded - width
        self.triple = jnp.pad(qkv.reshape(width, 3, width), ((0, 0), (0, 0), (0, pad))).reshape(
            width, 3 * padded
        )
        self.out = jnp.pad(out, ((0, pad), (0, pad)))
        self.mine = [plain_gather(w_up)]
        self.theirs = [plain_gather(w_down.T)]
        self.scalars = jnp.zeros((2,), jnp.int32)

    def bias_order(self, bias):
        return bias

    def bias_back(self, grad):
        return grad

    def scatter_pair(self, mine, theirs):
        return plain_scatter(mine), plain_scatter(theirs).T

    def scatter_first(self, triple_grad, out_grad):
        width, padded = self.width, self.padded
        qkv = triple_grad.reshape(width, 3, padded)[:, :, :width].reshape(width, 3 * width)
        return plain_scatter(qkv), plain_scatter(out_grad[:, :width])


def cuts_of(pairs, count):
    edges = [round(i * pairs / count) for i in range(count + 1)]
    return list(zip(edges[:-1], edges[1:]))


def local(
    block_input, paths, ln1_gain, ln1_bias, w_qkv, q_bias, v_bias, w_out, out_bias,
    ln2_gain, ln2_bias, w_up, up_bias, w_down, down_bias, cotangent,
):
    micro, _, width = block_input.shape
    place = Place(micro, paths.shape[2])
    parts = place.parts
    heads = width // HEAD_DIM
    padded = (heads + 1) // 2 * 128
    pairs = padded // 128
    pad = padded - width
    own_trunk = TRUNK // parts
    f32, bf16 = jnp.float32, jnp.bfloat16

    quick = lax.axis_size("row") == 4 and parts == 2 and w_qkv.shape[0] == 272
    weights = (QuickWeights if quick else PlainWeights)(place, w_qkv, w_out, w_up, w_down, padded)

    own_ids = lax.dynamic_index_in_dim(paths[0], place.quarter, 0, keepdims=False)
    parent_ids = lax.dynamic_index_in_dim(paths[1], place.quarter, 0, keepdims=False)
    mask_trunk, mask_group = place.masks(own_ids, parent_ids)

    rows_in = place.to_tree(place.to_tree_sources(block_input)).astype(f32)
    seed_rows = place.to_tree(place.to_tree_sources(cotangent))

    q_scale = HEAD_DIM**-0.5 * LOG2E
    triple_bias = jnp.concatenate(
        [jnp.pad(q_bias * q_scale, (0, pad)), jnp.zeros((padded,), f32), jnp.pad(v_bias, (0, pad))]
    )
    triple_scale = jnp.concatenate([jnp.full((padded,), q_scale, f32), jnp.ones((2 * padded,), f32)])
    first = layer_norm(rows_in, ln1_gain, ln1_bias).astype(bf16)
    triple = (dot_nn(first, weights.triple) * triple_scale + triple_bias).astype(bf16)
    shared = triple[:own_trunk, padded:]
    others = jnp.concatenate(
        [lax.ppermute(shared, "col", place.part_perm(e)) for e in range(1, parts)], axis=0
    )
    forward_cuts, backward_cuts = cuts_of(pairs, 3), cuts_of(pairs, 4)
    mixed, lse = [], []
    for start, stop in forward_cuts:
        one, two = attention_forward(
            parts, heads, triple, others, mask_trunk, mask_group, start, stop
        )
        mixed.append(one)
        lse.append(two)
    mixed, lse = jnp.concatenate(mixed, axis=1), jnp.concatenate(lse, axis=1)
    out_weight = weights.out[:, :width]
    attended = (dot_nn(mixed, out_weight) + out_bias).astype(bf16)
    middle = rows_in + attended.astype(f32)
    second = layer_norm(middle, ln2_gain, ln2_bias).astype(bf16)
    seed = seed_rows.astype(f32)
    outs = 4 if quick else 1
    lowered, second_grad, up_bias_grad, *pair_grads = feed_forward(
        weights.scalars, weights.mine, weights.theirs, second, seed_rows, weights.bias_order(up_bias), outs
    )
    pair_mine, pair_theirs = pair_grads[:outs], pair_grads[outs:]
    up_bias_grad = weights.bias_back(up_bias_grad.reshape(-1))
    result = (middle + lowered + down_bias).astype(bf16)

    down_bias_grad = jnp.sum(seed, axis=0)
    norm_grad, gain_two, shift_two = jax.vjp(layer_norm, middle, ln2_gain, ln2_bias)[1](second_grad)
    middle_grad = seed + norm_grad
    attended_grad = middle_grad.astype(bf16)
    out_bias_grad = jnp.sum(attended_grad.astype(f32), axis=0)
    out_weight_grad = dot_tn(mixed, attended_grad)[:width].astype(bf16)
    mixed_grad = dot_nt(attended_grad, out_weight).astype(bf16)
    early = sum_all([out_bias_grad, gain_two, shift_two, up_bias_grad, down_bias_grad])

    turned = jnp.swapaxes(mask_trunk, 1, 2), jnp.swapaxes(mask_group, 1, 2)
    result_sources = place.from_tree_sources(result)
    if quick:
        pair_swapped = {d: core_swap(place, pair_theirs[d]) for d in (3, 1, 2, 0)}
        sums = far_sums(pair_mine, pair_swapped)
    grads = []
    for index, (start, stop) in enumerate(backward_cuts):
        deps = ()
        if quick and index == 0:
            deps = sums
            received = far_sends(sums)
        if index == 1:
            result_parts = place.from_tree_parts(result_sources)
            deps = (result_parts,)
            result_out = place.swap_quarters(result_parts)
            if quick:
                sums = near_sums(pair_mine, pair_swapped, received)
                deps = deps + sums
                last = near_sends(sums)
        if quick and index == 3:
            total = row_total(pair_mine, pair_swapped, received, last)
            deps = (total,)
        grads.append(
            attention_backward(
                parts, heads, triple, others, mixed, mixed_grad, lse, *turned, start, stop, deps
            )
        )
    if quick:
        up_grad, down_grad = weights.pair_total(total)
    else:
        up_grad, down_grad = weights.scatter_pair(pair_mine[0], pair_theirs[0])
    dq, dk, dv, dko, dvo = (jnp.concatenate(part, axis=1) for part in zip(*grads))
    both = jnp.concatenate([dko, dvo], axis=1)
    key_value = jnp.concatenate([dk, dv], axis=1)
    for e in range(1, parts):
        block = both[(e - 1) * own_trunk : e * own_trunk]
        key_value = key_value.at[:own_trunk].add(
            lax.ppermute(block, "col", place.part_perm(e)).astype(f32)
        )
    triple_grad = jnp.concatenate([dq, key_value.astype(bf16)], axis=1)
    first_grad = dot_nt(triple_grad, weights.triple)
    q_bias_grad = jnp.sum(triple_grad[:, :width].astype(f32), axis=0)
    v_bias_grad = jnp.sum(triple_grad[:, 2 * padded : 2 * padded + width].astype(f32), axis=0)
    norm_grad, gain_one, shift_one = jax.vjp(layer_norm, rows_in, ln1_gain, ln1_bias)[1](first_grad)
    input_grad = (middle_grad + norm_grad).astype(bf16)
    input_grad_out = place.swap_quarters(place.from_tree_parts(place.from_tree_sources(input_grad)))
    triple_weight_grad = dot_tn(first, triple_grad).astype(bf16)
    out_padded = jnp.pad(out_weight_grad, ((0, 0), (0, pad)))
    if quick:
        mine, theirs = weights.first_pieces(triple_weight_grad, out_padded)
        swapped = {d: core_swap(place, theirs[d]) for d in (3, 1, 2, 0)}
        received = far_sends(far_sums(mine, swapped))
        last = near_sends(near_sums(mine, swapped, received))
        qkv_grad, out_grad = weights.first_total(row_total(mine, swapped, received, last))
    else:
        qkv_grad, out_grad = weights.scatter_first(triple_weight_grad, out_padded)
    late = sum_all([gain_one, shift_one, q_bias_grad, v_bias_grad])
    return (
        result_out, input_grad_out, late[0], late[1], qkv_grad, late[2], late[3],
        out_grad, early[0], early[1], early[2], up_grad, early[3], down_grad, early[4],
    )


def solution(mesh):
    rows = P(None, BOTH, None)
    placed = (
        rows, P(None, None, "row"), P(), P(), P("row", "col"), P(), P(), P("row", "col"), P(),
        P(), P(), P("row", "col"), P(), P("col", "row"), P(), rows,
    )
    out = (
        rows, rows, P(), P(), P("row", "col"), P(), P(), P("row", "col"), P(),
        P(), P(), P("row", "col"), P(), P("col", "row"), P(),
    )
    return jax.shard_map(local, mesh=mesh, in_specs=placed, out_specs=out, check_vma=False)
```

```python
import math
from functools import partial

import jax
import jax.numpy as jnp
import numpy as np
from jax import lax
from jax.experimental import pallas as pl
from jax.experimental.pallas import tpu as pltpu
from jax.sharding import PartitionSpec as P

HEAD_DIM = 64
TRUNK = 1024
GROUP = 384
QT = 256
LOG2E = 1.4426950408889634
LN2 = 0.6931471805599453


def dot_nn(a, b):
    return jnp.dot(a, b, preferred_element_type=jnp.float32)


def dot_nt(a, b):
    return lax.dot_general(a, b, (((1,), (1,)), ((), ())), preferred_element_type=jnp.float32)


def dot_tn(a, b):
    return lax.dot_general(a, b, (((0,), (0,)), ((), ())), preferred_element_type=jnp.float32)


def lane_masks(head):
    lane = lax.broadcasted_iota(jnp.int32, (1, 128), 1)
    inside = (lane // HEAD_DIM) == head
    return inside, inside.astype(jnp.float32).astype(jnp.bfloat16), lane % HEAD_DIM


def fill_trunk(parts, own_ref, other_ref, out_ref):
    own = TRUNK // parts
    for tile in range(own // QT):
        for part in range(parts):
            rows = (
                own_ref[tile * QT : (tile + 1) * QT, :]
                if part == 0
                else other_ref[(part - 1) * own + tile * QT : (part - 1) * own + (tile + 1) * QT, :]
            )
            start = (tile * parts + part) * QT
            out_ref[start : start + QT, :] = rows


def fwd_kernel(parts, heads, start, extra, q_ref, k_ref, v_ref, ko_ref, vo_ref, mt_ref, mg_ref, *refs):
    o_ref, lse_ref, kt, vt, va = refs[extra:]
    pair = start + pl.program_id(0)
    own = TRUNK // parts
    tiles = own // QT
    groups = (TRUNK // 256) // parts
    fill_trunk(parts, k_ref, ko_ref, kt)
    fill_trunk(parts, v_ref, vo_ref, vt)
    o_ref[...] = jnp.zeros_like(o_ref)
    lse_ref[...] = jnp.zeros_like(lse_ref)

    def finish(rows, top, total, inside):
        turned = pltpu.roll(total, HEAD_DIM, 1)
        o_ref[rows, :] += jnp.where(inside, total / turned, 0.0).astype(jnp.bfloat16)
        lse_ref[rows, :] += jnp.where(inside, 0.0, top + jnp.log2(total))

    def head_body(head, carry):
        inside, hm, _ = lane_masks(head)
        rest = 1 - hm
        va[...] = vt[...] * hm + rest
        for tile in range(tiles):
            rows = pl.ds(tile * QT, QT)
            q = q_ref[rows, :] * hm
            near = tile * parts * QT
            s_near = dot_nt(q, kt[near : near + parts * QT, :]) + mt_ref[tile]
            top = jnp.max(s_near, axis=1, keepdims=True)
            if tile > 0:
                s_far = dot_nt(q, kt[:near, :])
                top = jnp.maximum(top, jnp.max(s_far, axis=1, keepdims=True))
            p_near = jnp.exp2(s_near - top).astype(jnp.bfloat16)
            total = dot_nn(p_near, va[near : near + parts * QT, :])
            if tile > 0:
                total += dot_nn(jnp.exp2(s_far - top).astype(jnp.bfloat16), va[:near, :])
            finish(rows, top, total, inside)

        def group_body(group, carry):
            rows = pl.ds(pl.multiple_of(own + group * GROUP, 128), GROUP)
            q = q_ref[rows, :] * hm
            s_near = dot_nt(q, k_ref[rows, :]) + mg_ref[group]
            s_far = dot_nt(q, kt[...])
            top = jnp.maximum(
                jnp.max(s_near, axis=1, keepdims=True), jnp.max(s_far, axis=1, keepdims=True)
            )
            near = v_ref[rows, :] * hm + rest
            total = dot_nn(jnp.exp2(s_near - top).astype(jnp.bfloat16), near)
            total += dot_nn(jnp.exp2(s_far - top).astype(jnp.bfloat16), va[...])
            finish(rows, top, total, inside)
            return carry

        return lax.fori_loop(0, groups, group_body, carry)

    lax.fori_loop(0, jnp.minimum(2, heads - 2 * pair), head_body, 0)


def attention_forward(parts, heads, triple, others, mask_trunk, mask_group, start, stop, deps=()):
    rows = triple.shape[0]
    pairs = triple.shape[1] // (3 * 128)
    extra = others.shape[0]
    block = lambda count, shift: pl.BlockSpec((count, 128), lambda i: (0, i + shift))
    whole = lambda shape: pl.BlockSpec(shape, lambda i: (0,) * len(shape))
    return pl.pallas_call(
        partial(fwd_kernel, parts, heads, start, len(deps)),
        grid=(stop - start,),
        in_specs=[
            block(rows, start),
            block(rows, start + pairs),
            block(rows, start + 2 * pairs),
            block(extra, start),
            block(extra, start + pairs),
            whole(mask_trunk.shape),
            whole(mask_group.shape),
        ]
        + [pl.BlockSpec(memory_space=pl.ANY)] * len(deps),
        out_specs=[block(rows, 0), block(rows, 0)],
        out_shape=[
            jax.ShapeDtypeStruct((rows, (stop - start) * 128), jnp.bfloat16),
            jax.ShapeDtypeStruct((rows, (stop - start) * 128), jnp.float32),
        ],
        scratch_shapes=[
            pltpu.VMEM((TRUNK, 128), jnp.bfloat16),
            pltpu.VMEM((TRUNK, 128), jnp.bfloat16),
            pltpu.VMEM((TRUNK, 128), jnp.bfloat16),
        ],
        compiler_params=pltpu.CompilerParams(vmem_limit_bytes=48 * 1024 * 1024),
        cost_estimate=pl.CostEstimate(
            flops=(stop - start) * rows * 6_800_000, bytes_accessed=rows * pairs * 2000, transcendentals=0
        ),
        name="attention_forward",
    )(triple, triple, triple, others, others, mask_trunk, mask_group, *deps)


def split_three(value, place, outside):
    high = value.astype(jnp.bfloat16)
    left = value - high.astype(jnp.float32)
    middle = left.astype(jnp.bfloat16)
    low = (left - middle.astype(jnp.float32)).astype(jnp.bfloat16)
    high, middle, low = (v.astype(jnp.float32) for v in (high, middle, low))
    picked = jnp.where(place == 0, high, jnp.where(place == 1, middle, jnp.where(place == 2, low, 0.0)))
    return jnp.where(outside, picked, 0.0).astype(jnp.bfloat16)


def bwd_kernel(
    parts, heads, start, extra, q_ref, k_ref, v_ref, ko_ref, vo_ref, o_ref, do_ref, lse_ref, mt_ref, mg_ref,
    *refs,
):
    dq_ref, dk_ref, dv_ref, dko_ref, dvo_ref = refs[extra : extra + 5]
    kt, vt, ka, va, qa, da, qm, dm, dkt, dvt, dkg, dvg, dqs = refs[extra + 5 :]
    pair = start + pl.program_id(0)
    own = TRUNK // parts
    tiles = own // QT
    groups = (TRUNK // 256) // parts
    rows_all = own + groups * GROUP
    fill_trunk(parts, k_ref, ko_ref, kt)
    fill_trunk(parts, v_ref, vo_ref, vt)
    dkt[...] = jnp.zeros_like(dkt)
    dvt[...] = jnp.zeros_like(dvt)
    dkg[...] = jnp.zeros_like(dkg)
    dvg[...] = jnp.zeros_like(dvg)
    dqs[...] = jnp.zeros_like(dqs)

    def head_body(head, carry):
        inside, hm, place = lane_masks(head)
        rest = 1 - hm
        outside = jnp.logical_not(inside)
        ka[:TRUNK, :] = kt[...] * hm + rest
        va[:TRUNK, :] = vt[...] * hm + rest
        ka[TRUNK:, :] = k_ref[own:, :] * hm + rest
        va[TRUNK:, :] = v_ref[own:, :] * hm + rest

        def prepare(step, carry):
            rows = pl.ds(pl.multiple_of(step * 128, 128), 128)
            q = q_ref[rows, :] * hm
            d = do_ref[rows, :] * hm
            qm[rows, :] = q
            dm[rows, :] = d
            qa[rows, :] = q - split_three(lse_ref[rows, :], place, outside)
            delta = jnp.sum(
                d.astype(jnp.float32) * o_ref[rows, :].astype(jnp.float32), axis=1, keepdims=True
            )
            da[rows, :] = d - split_three(jnp.broadcast_to(delta, (128, 128)), place, outside)
            return carry

        lax.fori_loop(0, rows_all // 128, prepare, 0)

        def step(rows, keys, mask, keep, dk, dv):
            st = dot_nt(ka[keys, :], qa[rows, :])
            if mask is not None:
                st = st + mask
            p = jnp.exp2(st)
            dp = dot_nt(va[keys, :], da[rows, :])
            ds = (p * dp).astype(jnp.bfloat16)
            dv[keep, :] += dot_nn(p.astype(jnp.bfloat16), dm[rows, :])
            dk[keep, :] += dot_nn(ds, qm[rows, :])
            dqs[rows, :] += jnp.where(inside, dot_tn(ds, ka[keys, :]), 0.0)

        span = parts * QT
        for tile in range(tiles):
            rows = pl.ds(tile * QT, QT)
            for near in range(tile + 1):
                keys = pl.ds(near * span, span)
                step(rows, keys, mt_ref[tile] if near == tile else None, keys, dkt, dvt)
        count = QT if (groups * GROUP) % QT == 0 else 128

        def far_body(index, carry):
            rows = pl.ds(pl.multiple_of(own + index * count, 128), count)
            keys = pl.ds(0, TRUNK)
            step(rows, keys, None, keys, dkt, dvt)
            return carry

        lax.fori_loop(0, groups * GROUP // count, far_body, 0)

        def near_body(group, carry):
            rows = pl.ds(pl.multiple_of(own + group * GROUP, 128), GROUP)
            keys = pl.ds(pl.multiple_of(TRUNK + group * GROUP, 128), GROUP)
            keep = pl.ds(pl.multiple_of(group * GROUP, 128), GROUP)
            step(rows, keys, mg_ref[group], keep, dkg, dvg)
            return carry

        return lax.fori_loop(0, groups, near_body, carry)

    lax.fori_loop(0, jnp.minimum(2, heads - 2 * pair), head_body, 0)
    dq_ref[...] = (dqs[...] * HEAD_DIM**-0.5).astype(jnp.bfloat16)
    dk_ref[own:, :] = (dkg[...] * LN2).astype(jnp.bfloat16)
    dv_ref[own:, :] = dvg[...].astype(jnp.bfloat16)
    for tile in range(tiles):
        for part in range(parts):
            source = pl.ds((tile * parts + part) * QT, QT)
            if part == 0:
                dk_ref[tile * QT : (tile + 1) * QT, :] = (dkt[source, :] * LN2).astype(jnp.bfloat16)
                dv_ref[tile * QT : (tile + 1) * QT, :] = dvt[source, :].astype(jnp.bfloat16)
            else:
                start = (part - 1) * own + tile * QT
                dko_ref[start : start + QT, :] = (dkt[source, :] * LN2).astype(jnp.bfloat16)
                dvo_ref[start : start + QT, :] = dvt[source, :].astype(jnp.bfloat16)


def attention_backward(
    parts, heads, triple, others, mixed, mixed_grad, lse, mask_trunk, mask_group, start, stop, before=(), deps=()
):
    fixed = 10
    aliases = {fixed + index: index for index in range(len(before))}
    deps = tuple(before) + tuple(deps)
    rows = triple.shape[0]
    pairs = triple.shape[1] // (3 * 128)
    extra = others.shape[0]
    block = lambda count, shift: pl.BlockSpec((count, 128), lambda i: (0, i + shift))
    whole = lambda shape: pl.BlockSpec(shape, lambda i: (0,) * len(shape))
    near = rows - TRUNK // parts
    return pl.pallas_call(
        partial(bwd_kernel, parts, heads, start, len(deps)),
        grid=(stop - start,),
        in_specs=[
            block(rows, start),
            block(rows, start + pairs),
            block(rows, start + 2 * pairs),
            block(extra, start),
            block(extra, start + pairs),
            block(rows, start),
            block(rows, start),
            block(rows, start),
            whole(mask_trunk.shape),
            whole(mask_group.shape),
        ]
        + [pl.BlockSpec(memory_space=pl.ANY)] * len(deps),
        out_specs=[block(rows, start)] * 3 + [block(extra, start)] * 2,
        input_output_aliases=aliases,
        out_shape=[
            jax.ShapeDtypeStruct((rows, pairs * 128), jnp.bfloat16),
            jax.ShapeDtypeStruct((rows, pairs * 128), jnp.bfloat16),
            jax.ShapeDtypeStruct((rows, pairs * 128), jnp.bfloat16),
            jax.ShapeDtypeStruct((extra, pairs * 128), jnp.bfloat16),
            jax.ShapeDtypeStruct((extra, pairs * 128), jnp.bfloat16),
        ],
        scratch_shapes=[
            pltpu.VMEM((TRUNK, 128), jnp.bfloat16),
            pltpu.VMEM((TRUNK, 128), jnp.bfloat16),
            pltpu.VMEM((TRUNK + near, 128), jnp.bfloat16),
            pltpu.VMEM((TRUNK + near, 128), jnp.bfloat16),
            pltpu.VMEM((rows, 128), jnp.bfloat16),
            pltpu.VMEM((rows, 128), jnp.bfloat16),
            pltpu.VMEM((rows, 128), jnp.bfloat16),
            pltpu.VMEM((rows, 128), jnp.bfloat16),
            pltpu.VMEM((TRUNK, 128), jnp.float32),
            pltpu.VMEM((TRUNK, 128), jnp.float32),
            pltpu.VMEM((near, 128), jnp.float32),
            pltpu.VMEM((near, 128), jnp.float32),
            pltpu.VMEM((rows, 128), jnp.float32),
        ],
        compiler_params=pltpu.CompilerParams(vmem_limit_bytes=56 * 1024 * 1024),
        cost_estimate=pl.CostEstimate(
            flops=(stop - start) * rows * 12_200_000, bytes_accessed=rows * pairs * 4000, transcendentals=0
        ),
        name="attention_backward",
    )(triple, triple, triple, others, others, mixed, mixed_grad, lse, mask_trunk, mask_group, *deps)


ERF_TOP = (
    -2.72614225801306e-10, 2.77068142495902e-08, -2.10102402082508e-06, -5.69250639462346e-05,
    -7.34990630326855e-04, -2.95459980854025e-03, -1.60960333262415e-02,
)
ERF_LOW = (
    -1.45660718464996e-05, -2.13374055278905e-04, -1.68282697438203e-03, -7.37332916720468e-03,
    -1.42647390514189e-02,
)


def erf_float(value):
    value = jnp.clip(value, -3.832506856900711, 3.832506856900711)
    square = value * value
    top = jnp.full_like(value, ERF_TOP[0])
    for c in ERF_TOP[1:]:
        top = top * square + c
    low = jnp.full_like(value, ERF_LOW[0])
    for c in ERF_LOW[1:]:
        low = low * square + c
    return value * top / low


FF_BLOCK = 256
ROW_CHUNK = 640


def ffn_kernel(outs, chunk, scalars, *refs):
    up_main, down_main, tails, second, seed, bias = refs[:6]
    lowered, second_grad, bias_grad = refs[6:9]
    mine_grads, theirs_grads = refs[9 : 9 + outs], refs[9 + outs : 9 + 2 * outs]
    up, down, act, wide, up_grad, down_grad, second_t, seed_t = refs[9 + 2 * outs :]
    step = pl.program_id(0)
    role = scalars[0]
    is_rest = step == pl.num_programs(0) - 1

    @pl.when(jnp.logical_not(is_rest))
    def _():
        height = up_main.shape[2]
        for index in range(up_main.shape[0]):
            rows = pl.ds(index * height, height)
            up[rows, :] = up_main[index, 0]
            down[rows, :] = down_main[index, 0]

    @pl.when(is_rest)
    def _():
        height, columns = tails.shape[2], tails.shape[1]
        rest = FF_BLOCK // columns
        for index in range(tails.shape[0]):
            rows = pl.ds(index * height, height)
            slabs = [tails[index, c].astype(jnp.float32) for c in range(columns)]
            for shift, target in ((0, up), (rest, down)):
                joined = jnp.concatenate([slab[:, shift : shift + rest] for slab in slabs], axis=1)
                target[rows, :] = joined.astype(jnp.bfloat16)

    @pl.when(step == 0)
    def _():
        lowered[...] = jnp.zeros_like(lowered)
        second_grad[...] = jnp.zeros_like(second_grad)
        for start in range(0, second.shape[0], 128):
            rows = pl.ds(start, 128)
            second_t[:, rows] = second[rows, :].T
            seed_t[:, rows] = seed[rows, :].T

    total = jnp.zeros((1, FF_BLOCK), jnp.float32)
    for start in range(0, second.shape[0], chunk):
        rows = pl.ds(start, chunk)
        wide_in = dot_nn(second[rows, :], up[...]) + bias[...]
        hidden = dot_nn(seed[rows, :], down[...])
        share = 0.5 + 0.5 * erf_float(wide_in * 0.7071067811865476)
        act_now = (wide_in * share).astype(jnp.bfloat16)
        slope = share + wide_in * (jnp.exp(-0.5 * wide_in * wide_in) * 0.3989422804014327)
        wide_now = (hidden * slope).astype(jnp.bfloat16)
        total += jnp.sum(wide_now.astype(jnp.float32), axis=0, keepdims=True)
        act[rows, :] = act_now
        wide[rows, :] = wide_now
        lowered[rows, :] += dot_nt(act_now, down[...])
        second_grad[rows, :] += dot_nt(wide_now, up[...])
    bias_grad[...] = total
    up_grad[...] = dot_nn(second_t[...], wide[...]).astype(jnp.bfloat16)
    down_grad[...] = dot_nn(seed_t[...], act[...]).astype(jnp.bfloat16)

    def deliver(first_grad, second_grad):
        for index in range(outs):
            size = mine_grads[index].shape[0]
            rows = pl.ds(pl.multiple_of(scalars[1 + index], 16), size)
            mine_grads[index][...] = first_grad[rows, :]
            theirs_grads[index][...] = second_grad[rows, :]

    @pl.when(role == 0)
    def _():
        deliver(up_grad, down_grad)

    @pl.when(role != 0)
    def _():
        deliver(down_grad, up_grad)


def feed_forward(scalars, main, second, seed, bias, outs):
    rows, width = second.shape
    hidden = bias.shape[0]
    last = hidden // FF_BLOCK - 2
    per = (last + 1) // main.shape[1]

    def main_spec(shift):
        def index(j, s):
            j = jnp.minimum(j, last)
            return (0, j // per, 0, j % per + shift)

        return pl.BlockSpec((main.shape[0], 1, main.shape[2], FF_BLOCK), index)

    tail_spec = pl.BlockSpec(main.shape[:3] + (128,), lambda j, s: (0, 0, 0, 4 * per))
    whole = lambda shape: pl.BlockSpec(shape, lambda j, s: (0, 0))
    grad_spec = pl.BlockSpec((width // outs, FF_BLOCK), lambda j, s: (0, j))
    grad_shape = jax.ShapeDtypeStruct((width // outs, hidden), jnp.bfloat16)
    line = pl.BlockSpec((1, FF_BLOCK), lambda j, s: (0, j))
    chunk = ROW_CHUNK if rows % ROW_CHUNK == 0 else rows // 2
    return pl.pallas_call(
        partial(ffn_kernel, outs, chunk),
        grid_spec=pltpu.PrefetchScalarGridSpec(
            num_scalar_prefetch=1,
            grid=(hidden // FF_BLOCK,),
            in_specs=[
                main_spec(0), main_spec(per), tail_spec,
                whole((rows, width)), whole((rows, width)), line,
            ],
            out_specs=[whole((rows, width)), whole((rows, width)), line] + [grad_spec] * (2 * outs),
            scratch_shapes=[
                pltpu.VMEM((width, FF_BLOCK), jnp.bfloat16),
                pltpu.VMEM((width, FF_BLOCK), jnp.bfloat16),
                pltpu.VMEM((rows, FF_BLOCK), jnp.bfloat16),
                pltpu.VMEM((rows, FF_BLOCK), jnp.bfloat16),
                pltpu.VMEM((width, FF_BLOCK), jnp.bfloat16),
                pltpu.VMEM((width, FF_BLOCK), jnp.bfloat16),
                pltpu.VMEM((width, rows), jnp.bfloat16),
                pltpu.VMEM((width, rows), jnp.bfloat16),
            ],
        ),
        out_shape=[
            jax.ShapeDtypeStruct((rows, width), jnp.float32),
            jax.ShapeDtypeStruct((rows, width), jnp.float32),
            jax.ShapeDtypeStruct((1, hidden), jnp.float32),
        ]
        + [grad_shape] * (2 * outs),
        compiler_params=pltpu.CompilerParams(vmem_limit_bytes=60 * 1024 * 1024),
        cost_estimate=pl.CostEstimate(
            flops=24 * rows * width * hidden, bytes_accessed=8 * width * hidden + 20 * rows * width,
            transcendentals=rows * hidden,
        ),
        name="feed_forward",
    )(scalars, main, main, main, second, seed, bias.reshape(1, hidden))


MESH = pl.DeviceIdType.MESH
HOLD = pl.BlockSpec(memory_space=pl.ANY)


def greet(peers):
    barrier = pltpu.get_barrier_semaphore()
    for peer in peers:
        pl.semaphore_signal(barrier, inc=1, device_id=peer, device_id_type=MESH)
    pl.semaphore_wait(barrier, len(peers))


def remote(source, target, send, receive, device):
    return pltpu.make_async_remote_copy(
        src_ref=source, dst_ref=target, send_sem=send, recv_sem=receive,
        device_id=device, device_id_type=MESH,
    )


def chunk_home(chunk):
    block = chunk // 2
    turn = block % 4
    in_trunk = chunk < 16
    owner = jnp.where(in_trunk, ((turn + 1) // 2) % 2, (chunk - 16) // 12)
    spot = jnp.where(
        in_trunk, 2 * (2 * (block // 4) + turn // 2) + chunk % 2, 8 + (chunk - 16) % 12
    )
    return owner, spot


def start_kernel(grain, pack, later_pack, value, full, rows, later_out, z_send, z_recv, r_send, r_recv, c_send, c_recv,
                 x_send, x_recv, own_sem, later_sem):
    row, col = lax.axis_index("row"), lax.axis_index("col")
    z, core = col // 2, col % 2
    at = lambda r, c: (r, c)
    peers = [at(row, (col + shift) % 8) for shift in range(1, 8)] + [at(row ^ 1, col), at(row ^ 2, col)]
    greet(peers)
    later_copy = pltpu.make_async_copy(later_pack, later_out, later_sem)
    later_copy.start()
    here = full.at[core, row, z]
    own = pltpu.make_async_copy(pack, here, own_sem)
    own.start()
    sends = []
    for d in range(1, 4):
        copy = remote(pack, here, z_send.at[d - 1], z_recv.at[d - 1], at(row, (z ^ d) * 2 + core))
        copy.start()
        sends.append(copy)
    own.wait()
    for copy in sends:
        copy.wait_recv()
    later = []

    def pass_on(index, ref, device, send=r_send, receive=r_recv):
        copy = remote(ref, ref, send.at[index], receive.at[index], device)
        copy.start()
        later.append(copy)
        return copy

    beside = pass_on(0, full.at[core, row], at(row ^ 1, col))
    below = pass_on(1, full.at[core, row], at(row ^ 2, col))
    swaps = [pass_on(0, full.at[core, row], at(row, col ^ 1), c_send, c_recv)]

    each = value.shape[1] // grain

    def each_chunk(act_remote, act_own):
        for m in range(4):
            for i in range(each):
                owner, spot = chunk_home(col * each + i)
                source = value.at[m, pl.ds(i * grain, grain), :]
                target = rows.at[pl.ds(pl.multiple_of(spot * grain, grain), grain), :]
                same = jnp.logical_and(z == m, owner == core)
                index = m * each + i

                @pl.when(jnp.logical_not(same))
                def _():
                    act_remote(
                        remote(source, target, x_send.at[index], x_recv, at(row, 2 * m + owner))
                    )

                if act_own:

                    @pl.when(same)
                    def _():
                        pltpu.make_async_copy(source, target, x_recv).start()

    each_chunk(lambda copy: copy.start(), True)
    beside.wait_recv()
    far_a = pass_on(2, full.at[core, row ^ 1, pl.ds(0, 2)], at(row ^ 2, col))
    swaps.append(pass_on(1, full.at[core, row ^ 1], at(row, col ^ 1), c_send, c_recv))
    below.wait_recv()
    far_b = pass_on(3, full.at[core, row ^ 2, pl.ds(2, 2)], at(row ^ 1, col))
    swaps.append(pass_on(2, full.at[core, row ^ 2], at(row, col ^ 1), c_send, c_recv))
    far_a.wait_recv()
    far_b.wait_recv()
    swaps.append(pass_on(3, full.at[core, row ^ 3], at(row, col ^ 1), c_send, c_recv))
    for copy in swaps:
        copy.wait_recv()
    pltpu.make_async_copy(rows, rows, x_recv).wait()
    later_copy.wait()
    for copy in sends + later:
        copy.wait_send()
    each_chunk(lambda copy: copy.wait_send(), False)


def start_exchange(pack, later_pack, value, count):
    grain = 64
    height, lanes = pack.shape
    copies = 4 * (value.shape[1] // grain)
    dma = lambda n: pltpu.SemaphoreType.DMA((n,))
    return pl.pallas_call(
        partial(start_kernel, grain),
        in_specs=[HOLD] * 3,
        out_specs=[HOLD] * 3,
        out_shape=[
            jax.ShapeDtypeStruct((2, 4, 4, height, lanes), pack.dtype),
            jax.ShapeDtypeStruct((count, value.shape[2]), value.dtype),
            jax.ShapeDtypeStruct(later_pack.shape, later_pack.dtype),
        ],
        scratch_shapes=[
            dma(3), dma(3), dma(4), dma(4), dma(4), dma(4), dma(copies),
            pltpu.SemaphoreType.DMA, pltpu.SemaphoreType.DMA, pltpu.SemaphoreType.DMA,
        ],
        compiler_params=pltpu.CompilerParams(collective_id=0, has_side_effects=True),
        cost_estimate=pl.CostEstimate(flops=100_000_000_000, bytes_accessed=0, transcendentals=0),
        name="start_exchange",
    )(pack, later_pack, value)


def end_kernel(
    grain, grads, small, rows, *refs,
):
    final, small_out, tokens, mine, swapped, far, beside, below, tail, small_col, small_row, part = refs[-26:-14]
    own_sem, c_send, c_recv, r_send, r_recv, z_send, z_recv, s_send, s_recv, t_send, t_recv, _, x_send, x_recv = refs[-14:]
    row, col = lax.axis_index("row"), lax.axis_index("col")
    z, core = col // 2, col % 2
    at = lambda r, c: (r, c)
    peers = [at(row, (col + shift) % 8) for shift in range(1, 8)]
    peers += [at(row ^ d, col) for d in range(1, 4)]
    greet(peers)
    own = pltpu.make_async_copy(grads.at[core], mine, own_sem)
    own.start()
    sends = []
    for d in (3, 1, 2, 0):
        copy = remote(
            grads.at[1 - core, row ^ d], swapped.at[row ^ d], c_send.at[d], c_recv.at[d], at(row, col ^ 1)
        )
        copy.start()
        sends.append(copy)
    for shift in range(1, 8):
        copy = remote(
            small, small_col.at[col], s_send.at[shift - 1], s_recv.at[7 - shift], at(row, (col + shift) % 8)
        )
        copy.start()
        sends.append(copy)
    small_col[col] = small[...]
    own.wait()
    f32 = jnp.float32
    each = tokens.shape[1] // grain

    def each_chunk(act_remote, act_own):
        for local in range(rows.shape[0] // grain):
            pair = local // 2
            turn = 4 * (pair // 2) + (core if pair % 2 == 0 else 3 - core)
            chunk = 2 * turn + local % 2 if local < 8 else 16 + 12 * core + local - 8
            shard = chunk // each
            source = rows.at[pl.ds(local * grain, grain), :]
            start = pl.multiple_of((chunk % each) * grain, grain)
            target = tokens.at[z, pl.ds(start, grain), :]

            @pl.when(shard != col)
            def _():
                act_remote(remote(source, target, x_send.at[local], x_recv, at(row, shard)))

            if act_own:

                @pl.when(shard == col)
                def _():
                    pltpu.make_async_copy(source, target, x_recv).start()

    each_chunk(lambda copy: copy.start(), True)

    def add(target, source):
        target[...] = (target[...].astype(f32) + source[...].astype(f32)).astype(target.dtype)

    def add_swapped(position):
        sends[position].wait_recv()
        d = (3, 1, 2, 0)[position]
        for q in range(4):
            add(mine.at[row ^ d, q], swapped.at[row ^ d, q])

    def send(index, source, target, device):
        copy = remote(source, target, r_send.at[index], r_recv.at[index], device)
        copy.start()
        sends.append(copy)
        return copy

    add_swapped(0)
    far_a = send(0, mine.at[row ^ 3, pl.ds(0, 2)], far.at[pl.ds(0, 2)], at(row ^ 2, col))
    far_b = send(1, mine.at[row ^ 3, pl.ds(2, 2)], far.at[pl.ds(2, 2)], at(row ^ 1, col))
    add_swapped(1)
    x_b = send(2, mine.at[row ^ 1, pl.ds(2, 2)], beside.at[pl.ds(2, 2)], at(row ^ 1, col))
    add_swapped(2)
    y_a = send(3, mine.at[row ^ 2, pl.ds(0, 2)], below.at[pl.ds(0, 2)], at(row ^ 2, col))
    add_swapped(3)
    for shift in range(1, 8):
        sends[3 + shift].wait_recv()
    part[...] = small_col[0]
    for c in range(1, 8):
        part[...] += small_col[c]
    rounds = []
    for d in range(1, 4):
        copy = remote(part, small_row.at[row], t_send.at[d - 1], t_recv.at[d - 1], at(row ^ d, col))
        copy.start()
        rounds.append(copy)
    small_row[row] = part[...]
    far_a.wait_recv()
    for q in (0, 1):
        add(mine.at[row ^ 1, q], far.at[q])
    x_a = send(4, mine.at[row ^ 1, pl.ds(0, 2)], beside.at[pl.ds(0, 2)], at(row ^ 1, col))
    far_b.wait_recv()
    for q in (2, 3):
        add(mine.at[row ^ 2, q], far.at[q])
    y_b = send(5, mine.at[row ^ 2, pl.ds(2, 2)], below.at[pl.ds(2, 2)], at(row ^ 2, col))
    for copy in (x_b, y_a, x_a, y_b):
        copy.wait_recv()

    def total(q):
        return (
            mine[row, q].astype(f32) + beside[q].astype(f32) + below[q].astype(f32)
        )

    lasts = []
    for d in range(1, 4):
        q = z ^ d
        mine[row, q] = total(q).astype(mine.dtype)
        copy = remote(
            mine.at[row, q], tail.at[d - 1], z_send.at[d - 1], z_recv.at[d - 1], at(row, q * 2 + core)
        )
        copy.start()
        lasts.append(copy)
    result = total(z)
    for d in range(1, 4):
        lasts[d - 1].wait_recv()
        result = result + tail[d - 1].astype(f32)
    final[...] = result
    for copy in rounds:
        copy.wait_recv()
    pltpu.make_async_copy(tokens, tokens, x_recv).wait()
    each_chunk(lambda copy: copy.wait_send(), False)
    small_out[...] = small_row[0] + small_row[1] + small_row[2] + small_row[3]
    for copy in sends + lasts + rounds:
        copy.wait_send()


def end_exchange(grads, small, rows, shape, deps):
    grain = 64
    height, lanes = grads.shape[3:]
    slab = lambda *n: pltpu.VMEM(n + (height, lanes), grads.dtype)
    dma = lambda n: pltpu.SemaphoreType.DMA((n,))
    return pl.pallas_call(
        partial(end_kernel, grain),
        in_specs=[HOLD, pl.BlockSpec(memory_space=pltpu.VMEM), HOLD] + [HOLD] * len(deps),
        out_specs=[pl.BlockSpec(memory_space=pltpu.VMEM)] * 2 + [HOLD],
        out_shape=[
            jax.ShapeDtypeStruct((height, lanes), jnp.float32),
            jax.ShapeDtypeStruct(small.shape, jnp.float32),
            jax.ShapeDtypeStruct(shape, rows.dtype),
        ],
        scratch_shapes=[
            slab(4, 4), slab(4, 4), slab(4), slab(4), slab(4), slab(3),
            pltpu.VMEM((8,) + small.shape, jnp.float32), pltpu.VMEM((4,) + small.shape, jnp.float32),
            pltpu.VMEM(small.shape, jnp.float32),
            pltpu.SemaphoreType.DMA, dma(4), dma(4), dma(6), dma(6), dma(3), dma(3),
            dma(7), dma(7), dma(3), dma(3), dma(1), dma(rows.shape[0] // grain), pltpu.SemaphoreType.DMA,
        ],
        compiler_params=pltpu.CompilerParams(
            collective_id=1, has_side_effects=True, vmem_limit_bytes=40 * 1024 * 1024
        ),
        cost_estimate=pl.CostEstimate(flops=100_000_000_000, bytes_accessed=0, transcendentals=0),
        name="end_exchange",
    )(grads, small, rows, *deps)


def lane_runs(width, padded, columns, qkv_cols, out_cols):
    runs = []
    for c in range(columns):
        start = c * qkv_cols
        while start < (c + 1) * qkv_cols:
            third = start // width
            stop = min((c + 1) * qkv_cols, (third + 1) * width)
            runs.append((0, third * padded + start - third * width, c, start - c * qkv_cols, stop - start))
            start = stop
        runs.append((1, c * out_cols, c, qkv_cols, out_cols))
    return runs


def assemble_kernel(runs, width, padded, full, triple, out):
    step = pl.program_id(0)
    height = full.shape[3]
    columns = 2 * full.shape[2]
    slabs = [full[c % 2, 0, c // 2].astype(jnp.float32) for c in range(columns)]
    piece = lambda run: slabs[run[2]][:, run[3] : run[3] + run[4]]
    gap = jnp.zeros((height, padded - width), jnp.float32)

    def line(which, third):
        low, high = third * padded, third * padded + padded
        chosen = [r for r in runs if r[0] == which and low <= r[1] < high]
        return jnp.concatenate([piece(r) for r in chosen] + [gap], axis=1).astype(triple.dtype)

    for third in range(3):
        triple[:, third * padded : (third + 1) * padded] = line(0, third)

    @pl.when(step == 0)
    def _():
        out[width:, :] = jnp.zeros((padded - width, padded), out.dtype)

    out[pl.ds(pl.multiple_of(step * height, 16), height), :] = line(1, 0)


def assemble(full, width, padded, qkv_cols):
    height, lanes = full.shape[3:]
    runs = lane_runs(width, padded, 2 * full.shape[2], qkv_cols, lanes - qkv_cols)
    return pl.pallas_call(
        partial(assemble_kernel, runs, width, padded),
        grid=(full.shape[1],),
        in_specs=[pl.BlockSpec((2, 1, full.shape[2], height, lanes), lambda r: (0, r, 0, 0, 0))],
        out_specs=[
            pl.BlockSpec((height, 3 * padded), lambda r: (r, 0)),
            pl.BlockSpec((padded, padded), lambda r: (0, 0)),
        ],
        out_shape=[
            jax.ShapeDtypeStruct((width, 3 * padded), full.dtype),
            jax.ShapeDtypeStruct((padded, padded), full.dtype),
        ],
        compiler_params=pltpu.CompilerParams(vmem_limit_bytes=48 * 1024 * 1024),
        cost_estimate=pl.CostEstimate(flops=12_000_000_000, bytes_accessed=0, transcendentals=0),
        name="assemble_weights",
    )(full)


def divide_kernel(runs, triple, out, full):
    wide = triple[...].astype(jnp.float32)
    last = out[...].astype(jnp.float32)
    for c in range(2 * full.shape[2]):
        parts = [
            (wide, last)[r[0]][:, r[1] : r[1] + r[4]] for r in runs if r[2] == c
        ]
        full[c % 2, 0, c // 2] = jnp.concatenate(parts, axis=1).astype(full.dtype)


def divide(triple, out, width, padded, qkv_cols, out_cols, columns, rows):
    height, lanes = width // rows, qkv_cols + out_cols
    runs = lane_runs(width, padded, columns, qkv_cols, out_cols)
    return pl.pallas_call(
        partial(divide_kernel, runs),
        grid=(rows,),
        in_specs=[
            pl.BlockSpec((height, 3 * padded), lambda r: (r, 0)),
            pl.BlockSpec((height, out.shape[1]), lambda r: (r, 0)),
        ],
        out_specs=pl.BlockSpec((2, 1, columns // 2, height, lanes), lambda r: (0, r, 0, 0, 0)),
        out_shape=jax.ShapeDtypeStruct((2, rows, columns // 2, height, lanes), jnp.bfloat16),
        compiler_params=pltpu.CompilerParams(vmem_limit_bytes=48 * 1024 * 1024),
        cost_estimate=pl.CostEstimate(flops=12_000_000_000, bytes_accessed=0, transcendentals=0),
        name="divide_gradients",
    )(triple, out)


def finish_kernel(own_trunk, dq, dk, dv, other_k, other_v, *refs):
    total, sums = refs[-2:]
    step = pl.program_id(0)
    each = pl.num_programs(0) // 3

    def deliver(value):
        total[...] = value
        sums[...] = jnp.sum(value.astype(jnp.float32), axis=0, keepdims=True)

    @pl.when(step < each)
    def _():
        deliver(dq[...])

    for index, (near, far) in enumerate(((dk, other_k), (dv, other_v))):

        @pl.when(step // each == index + 1)
        def _():
            value = near[:own_trunk, :].astype(jnp.float32)
            for start in range(0, far.shape[0], own_trunk):
                value = value + far[start : start + own_trunk, :].astype(jnp.float32)
            deliver(jnp.concatenate([value.astype(total.dtype), near[own_trunk:, :]], axis=0))


def finish_gradients(own_trunk, dq, dk, dv, other_k, other_v, deps):
    rows, padded = dq.shape
    block = 384
    each = padded // block

    def spec(count, third):
        return pl.BlockSpec((count, block), lambda j: (0, jnp.clip(j - third * each, 0, each - 1)))

    return pl.pallas_call(
        partial(finish_kernel, own_trunk),
        grid=(3 * each,),
        in_specs=[
            spec(rows, 0), spec(rows, 1), spec(rows, 2), spec(other_k.shape[0], 1), spec(other_v.shape[0], 2),
        ]
        + [HOLD] * len(deps),
        out_specs=[
            pl.BlockSpec((rows, block), lambda j: (0, j)), pl.BlockSpec((1, block), lambda j: (0, j)),
        ],
        out_shape=[
            jax.ShapeDtypeStruct((rows, 3 * padded), jnp.bfloat16),
            jax.ShapeDtypeStruct((1, 3 * padded), jnp.float32),
        ],
        compiler_params=pltpu.CompilerParams(vmem_limit_bytes=48 * 1024 * 1024),
        cost_estimate=pl.CostEstimate(flops=8_000_000_000, bytes_accessed=0, transcendentals=0),
        name="finish_gradients",
    )(dq, dk, dv, other_k, other_v, *deps)


def norm_parts(value):
    center = value - jnp.mean(value, axis=-1, keepdims=True)
    scale = lax.rsqrt(jnp.mean(center * center, axis=-1, keepdims=True) + 1e-05)
    return center * scale, scale


def norm_back(grad, value, gain):
    unit, scale = norm_parts(value)
    scaled = grad * gain
    back = scaled - jnp.mean(scaled, axis=-1, keepdims=True)
    back = scale * (back - unit * jnp.mean(scaled * unit, axis=-1, keepdims=True))
    return back, jnp.sum(grad * unit, axis=0, keepdims=True), jnp.sum(grad, axis=0, keepdims=True)


def out_kernel(mixed, weight, bias, rows, gain, shift, middle, second):
    width = rows.shape[1]
    attended = dot_nn(mixed[...], weight[...])[:, :width] + bias[...]
    total = rows[...].astype(jnp.float32) + attended.astype(jnp.bfloat16).astype(jnp.float32)
    middle[...] = total
    unit, _ = norm_parts(total)
    second[...] = (unit * gain[...] + shift[...]).astype(jnp.bfloat16)


def by_rows(kernel, name, count, chunked, fixed, outs, sums=(), scratch=(), flops=0):
    chunk = count // 5
    block = lambda width: pl.BlockSpec((chunk, width), lambda i: (i, 0))
    whole = lambda shape: pl.BlockSpec(shape, lambda i: (0,) * len(shape))
    return pl.pallas_call(
        kernel,
        grid=(5,),
        in_specs=[block(v.shape[1]) for v in chunked] + [whole(v.shape) for v in fixed],
        out_specs=[block(width) for width, _ in outs] + [whole(shape) for shape, _ in sums],
        out_shape=[jax.ShapeDtypeStruct((count, width), dtype) for width, dtype in outs]
        + [jax.ShapeDtypeStruct(shape, dtype) for shape, dtype in sums],
        scratch_shapes=list(scratch),
        compiler_params=pltpu.CompilerParams(vmem_limit_bytes=56 * 1024 * 1024),
        cost_estimate=pl.CostEstimate(flops=flops, bytes_accessed=0, transcendentals=0),
        name=name,
    )(*chunked, *fixed)


def project_out(mixed, rows, weight, bias, gain, shift):
    width = rows.shape[1]

    def kernel(mixed, rows, weight, bias, gain, shift, middle, second):
        out_kernel(mixed, weight, bias, rows, gain, shift, middle, second)

    line = lambda v: v.reshape(1, width)
    return by_rows(
        kernel, "project_out", rows.shape[0], (mixed, rows), (weight, line(bias), line(gain), line(shift)),
        ((width, jnp.float32), (width, jnp.bfloat16)), flops=12_000_000_000,
    )


def middle_kernel(second_grad, lowered, middle, seed, mixed, weight, gain, down_bias,
                  result, middle_grad, mixed_grad, sums, out_grad, total):
    step = pl.program_id(0)
    width = middle.shape[1]
    value, up = middle[...], seed[...].astype(jnp.float32)
    result[...] = (value + lowered[...] + down_bias[...]).astype(jnp.bfloat16)
    back, gain_sum, shift_sum = norm_back(second_grad[...], value, gain[...])
    grad = up + back
    middle_grad[...] = grad
    low = grad.astype(jnp.bfloat16)
    mixed_grad[...] = dot_nt(low, weight[:, :width]).astype(jnp.bfloat16)
    part = dot_tn(mixed[...], low)
    low_sum = jnp.sum(low.astype(jnp.float32), axis=0, keepdims=True)
    up_sum = jnp.sum(up, axis=0, keepdims=True)
    lines = jnp.concatenate([low_sum, gain_sum, shift_sum, up_sum], axis=0)

    @pl.when(step == 0)
    def _():
        sums[...] = lines
        total[...] = part

    @pl.when(step > 0)
    def _():
        sums[...] += lines
        total[...] += part

    @pl.when(step == pl.num_programs(0) - 1)
    def _():
        out_grad[:, :width] = total[:width, :].astype(jnp.bfloat16)
        out_grad[:, width:] = jnp.zeros((width, out_grad.shape[1] - width), jnp.bfloat16)


def middle_back(second_grad, lowered, middle, seed, mixed, weight, gain, down_bias):
    rows, width = middle.shape
    padded = weight.shape[0]
    line = lambda v: v.reshape(1, width)
    return by_rows(
        middle_kernel, "middle_back", rows, (second_grad, lowered, middle, seed, mixed),
        (weight, line(gain), line(down_bias)),
        ((width, jnp.bfloat16), (width, jnp.float32), (padded, jnp.bfloat16)),
        (((4, width), jnp.float32), ((width, padded), jnp.bfloat16)),
        (pltpu.VMEM((padded, width), jnp.float32),), flops=25_000_000_000,
    )


def first_kernel(triple_grad, rows, middle_grad, weight, gain, input_grad, sums):
    step = pl.program_id(0)
    grad = dot_nt(triple_grad[...], weight[...])
    back, gain_sum, shift_sum = norm_back(grad, rows[...].astype(jnp.float32), gain[...])
    input_grad[...] = (middle_grad[...] + back).astype(jnp.bfloat16)
    lines = jnp.concatenate([gain_sum, shift_sum], axis=0)

    @pl.when(step == 0)
    def _():
        sums[...] = lines

    @pl.when(step > 0)
    def _():
        sums[...] += lines


def first_back(triple_grad, rows, middle_grad, weight, gain):
    count, width = rows.shape
    return by_rows(
        first_kernel, "first_back", count, (triple_grad, rows, middle_grad), (weight, gain.reshape(1, width)),
        ((width, jnp.bfloat16),), (((2, width), jnp.float32),), flops=25_000_000_000,
    )


def blocks_kernel(rest, core, total, other, total_tail, other_tail, out):
    quarter = pl.program_id(0)
    main = total.shape[1]
    out[0, :, :main] = total[...]
    out[0, :, main : 2 * main] = other[...]
    for shard in range(8):

        @pl.when(2 * quarter + core[0] == shard)
        def _():
            cut = slice(shard * rest, (shard + 1) * rest)
            out[0, :, 2 * main : 2 * main + rest] = total_tail[:, cut]
            out[0, :, 2 * main + rest :] = other_tail[:, cut]


def pair_blocks(core, total, other, main, rest):
    rows = total.shape[0]
    spec = pl.BlockSpec((rows, main), lambda q, s: (0, 2 * q + s[0]))
    tail = pl.BlockSpec((rows, 8 * rest), lambda q, s: (0, main // rest))
    return pl.pallas_call(
        partial(blocks_kernel, rest),
        grid_spec=pltpu.PrefetchScalarGridSpec(
            num_scalar_prefetch=1,
            grid=(4,),
            in_specs=[spec, spec, tail, tail],
            out_specs=pl.BlockSpec((1, rows, 2 * (main + rest)), lambda q, s: (q, 0, 0)),
        ),
        out_shape=jax.ShapeDtypeStruct((4, rows, 2 * (main + rest)), total.dtype),
        cost_estimate=pl.CostEstimate(flops=5_000_000_000, bytes_accessed=0, transcendentals=0),
        name="pair_blocks",
    )(core, total, other, total, other)


def after(value, *deps):
    def kernel(*refs):
        pass

    return pl.pallas_call(
        kernel,
        in_specs=[HOLD] * (1 + len(deps)),
        out_specs=HOLD,
        out_shape=jax.ShapeDtypeStruct(value.shape, value.dtype),
        input_output_aliases={0: 0},
        name="after",
    )(value, *deps)


def layer_norm(value, gain, bias):
    center = value - jnp.mean(value, axis=-1, keepdims=True)
    spread = jnp.mean(center * center, axis=-1, keepdims=True)
    return center * lax.rsqrt(spread + 1e-05) * gain + bias


def own_rows(parts, part):
    blocks = TRUNK // (128 * parts)
    starts = []
    for k in range(blocks):
        base = (k // 2) * 2 * parts
        starts.append(128 * (base + (part if k % 2 == 0 else 2 * parts - 1 - part)))
    rows = [np.arange(128) + s for s in starts]
    groups = (TRUNK // 256) // parts
    rows.append(TRUNK + part * groups * GROUP + np.arange(groups * GROUP))
    return np.concatenate(rows)


def spread_kernel(grain, table, *refs):
    pieces, out = refs[:-1], refs[-1]
    each = pieces[0].shape[0] // grain
    for index, piece in enumerate(pieces):
        for i in range(each):
            target = table[index * each + i]

            @pl.when(target >= 0)
            def _():
                rows = pl.ds(pl.multiple_of(target * grain, grain), grain)
                out[rows, :] = piece[i * grain : (i + 1) * grain, :]


def spread(table, pieces, grain, count):
    width = pieces[0].shape[1]
    whole = lambda rows: pl.BlockSpec((rows, width), lambda i, s: (0, 0))
    return pl.pallas_call(
        partial(spread_kernel, grain),
        grid_spec=pltpu.PrefetchScalarGridSpec(
            num_scalar_prefetch=1,
            grid=(1,),
            in_specs=[whole(p.shape[0]) for p in pieces],
            out_specs=whole(count),
        ),
        out_shape=jax.ShapeDtypeStruct((count, width), pieces[0].dtype),
        compiler_params=pltpu.CompilerParams(vmem_limit_bytes=48 * 1024 * 1024),
        cost_estimate=pl.CostEstimate(flops=0, bytes_accessed=6 * count * width, transcendentals=0),
        name="spread_rows",
    )(table, *pieces)


def collect_kernel(grain, count, table, *refs):
    sources, outs = refs[:-count], refs[-count:]
    each = outs[0].shape[0] // grain
    for index, out in enumerate(outs):
        for i in range(each):
            owner = table[2 * (index * each + i)]
            start = table[2 * (index * each + i) + 1]
            for which, source in enumerate(sources):

                @pl.when(owner == which)
                def _():
                    rows = pl.ds(pl.multiple_of(start * grain, grain), grain)
                    out[i * grain : (i + 1) * grain, :] = source[rows, :]


def collect(table, sources, grain, count, length):
    width = sources[0].shape[1]
    whole = lambda rows: pl.BlockSpec((rows, width), lambda i, s: (0, 0))
    return pl.pallas_call(
        partial(collect_kernel, grain, count),
        grid_spec=pltpu.PrefetchScalarGridSpec(
            num_scalar_prefetch=1,
            grid=(1,),
            in_specs=[whole(s.shape[0]) for s in sources],
            out_specs=[whole(length)] * count,
        ),
        out_shape=[jax.ShapeDtypeStruct((length, width), sources[0].dtype)] * count,
        compiler_params=pltpu.CompilerParams(vmem_limit_bytes=48 * 1024 * 1024),
        cost_estimate=pl.CostEstimate(flops=0, bytes_accessed=6 * count * length * width, transcendentals=0),
        name="collect_rows",
    )(table, *sources)


class Place:
    def __init__(self, micro, tree):
        self.columns = lax.axis_size("col")
        self.micro = micro
        self.parts = self.columns // micro
        self.tree = tree
        self.length = tree // self.columns
        self.grain = math.gcd(self.length, 128)
        me = lax.axis_index("col")
        self.quarter, self.part = me // self.parts, me % self.parts
        self.own = np.stack([own_rows(self.parts, part) for part in range(self.parts)])
        self.count = self.own.shape[1]

    def quarter_perm(self, shift):
        p = self.parts
        return [(c, ((c // p) ^ shift) * p + c % p) for c in range(self.columns)]

    def part_perm(self, shift):
        return [(c, c ^ shift) for c in range(self.columns)]

    def swap_quarters(self, value):
        groups = [
            [q * self.parts + part for q in range(self.micro)] for part in range(self.parts)
        ]
        return lax.all_to_all(value, "col", 0, 0, axis_index_groups=groups, tiled=True)

    def tree_sources(self, value):
        mine = value.reshape(self.micro * self.length, value.shape[2])
        return [mine] + [lax.ppermute(mine, "col", self.part_perm(e)) for e in range(1, self.parts)]

    def to_tree(self, sources):
        grain, each = self.grain, self.length // self.grain
        table = np.full((self.parts, self.tree // grain), -1, np.int32)
        for part in range(self.parts):
            table[part, self.own[part, ::grain] // grain] = np.arange(self.count // grain)
        mine = lax.dynamic_index_in_dim(jnp.asarray(table), self.part, 0, keepdims=False)
        e, rest = np.divmod(np.arange(self.tree // grain, dtype=np.int32), self.micro * each)
        quarter, inside = np.divmod(rest, each)
        chunk = (quarter * self.parts + (self.part ^ e)) * each + inside
        return spread(mine[chunk], sources, grain, self.count)

    def from_tree_sources(self, value):
        return [value] + [lax.ppermute(value, "col", self.part_perm(e)) for e in range(1, self.parts)]

    def from_tree_parts(self, sources):
        grain, each, parts = self.grain, self.length // self.grain, self.parts
        owner = np.zeros(self.tree // grain, np.int32)
        local = np.zeros(self.tree // grain, np.int32)
        for part in range(parts):
            owner[self.own[part, ::grain] // grain] = part
            local[self.own[part, ::grain] // grain] = np.arange(self.count // grain)
        quarter, inside = np.divmod(np.arange(self.micro * each, dtype=np.int32), each)
        chunk = (quarter * parts + self.part) * each + inside
        table = jnp.stack([jnp.asarray(owner)[chunk] ^ self.part, jnp.asarray(local)[chunk]], axis=1)
        (out,) = collect(table.reshape(-1), sources, grain, 1, self.micro * self.length)
        return out.reshape(self.micro, self.length, sources[0].shape[1])

    def masks(self, own_ids, parent_ids):
        parts = self.parts
        own = jnp.asarray(self.own, jnp.int32)
        mine = lax.dynamic_index_in_dim(own, self.part, 0, keepdims=False)
        trunk_rows = TRUNK // parts
        tiles = trunk_rows // QT
        trunk = []
        for tile in range(tiles):
            span = slice(tile * QT, (tile + 1) * QT)
            keys = jnp.concatenate(
                [
                    lax.dynamic_index_in_dim(own, self.part ^ e, 0, keepdims=False)[span]
                    for e in range(parts)
                ]
            )
            trunk.append(jnp.where(keys[None, :] <= mine[span][:, None], 0.0, -1e30))
        group = []
        groups = (TRUNK // 256) // parts
        places = jnp.arange(GROUP)
        for g in range(groups):
            start = TRUNK + (self.part * groups + g) * GROUP
            ids = lax.dynamic_slice_in_dim(own_ids, start, GROUP)
            parent = lax.dynamic_slice_in_dim(parent_ids, start, GROUP)
            seen = (places[None, :] <= places[:, None]) & (
                (ids[None, :] == 0) | (ids[None, :] == ids[:, None]) | (ids[None, :] == parent[:, None])
            )
            group.append(jnp.where(seen, 0.0, -1e30))
        return jnp.stack(trunk).astype(jnp.float32), jnp.stack(group).astype(jnp.float32)


BOTH = ("row", "col")
ROW_CUT = 144


def plain_gather(block):
    full = lax.all_gather(block, BOTH, axis=0, tiled=False)
    full = full.reshape(lax.axis_size("row"), lax.axis_size("col"), *block.shape)
    return full.transpose(0, 2, 1, 3).reshape(full.shape[0] * full.shape[2], full.shape[1] * full.shape[3])


def plain_scatter(grad):
    rows, cols = lax.axis_size("row"), lax.axis_size("col")
    blocks = grad.astype(jnp.bfloat16).reshape(rows, grad.shape[0] // rows, cols, grad.shape[1] // cols)
    blocks = blocks.transpose(0, 2, 1, 3).reshape(rows * cols, grad.shape[0] // rows, grad.shape[1] // cols)
    return lax.psum_scatter(blocks, BOTH, scatter_dimension=0, tiled=False).astype(jnp.float32)


def across(value, shift):
    return lax.ppermute(value, "row", [(r, r ^ shift) for r in range(lax.axis_size("row"))])


def row_gather(block):
    beside = across(block, 1)
    below = across(block, 2)
    return [block, beside, below, across(beside[:ROW_CUT], 2), across(below[ROW_CUT:], 1)]


def row_starts(rows):
    me = lax.axis_index("row")
    far = (me ^ 3) * rows
    return [me * rows, (me ^ 1) * rows, (me ^ 2) * rows, far, far + ROW_CUT]


def core_swap(place, value):
    return lax.ppermute(value, "col", place.part_perm(1))


def far_sums(own, swapped):
    f32, bf16 = jnp.float32, jnp.bfloat16
    add = lambda d, part: (own[d][part].astype(f32) + swapped[d][part].astype(f32)).astype(bf16)
    top, bottom = slice(0, ROW_CUT), slice(ROW_CUT, None)
    return add(3, top), add(3, bottom), add(1, bottom), add(2, top)


def far_sends(sums):
    return across(sums[0], 2), across(sums[1], 1), across(sums[2], 1), across(sums[3], 2)


def near_sums(own, swapped, received):
    f32 = jnp.float32
    beside = own[1][:ROW_CUT].astype(f32) + swapped[1][:ROW_CUT].astype(f32) + received[0].astype(f32)
    below = own[2][ROW_CUT:].astype(f32) + swapped[2][ROW_CUT:].astype(f32) + received[1].astype(f32)
    return beside.astype(jnp.bfloat16), below.astype(jnp.bfloat16)


def near_sends(sums):
    return across(sums[0], 1), across(sums[1], 2)


def row_total(own, swapped, received, last):
    f32 = jnp.float32
    base = own[0].astype(f32) + swapped[0].astype(f32)
    beside = jnp.concatenate([last[0], received[2]], axis=0).astype(f32)
    below = jnp.concatenate([received[3], last[1]], axis=0).astype(f32)
    return (base + beside + below).astype(jnp.bfloat16)


def pack_pair(w_up, w_down):
    main = w_up.shape[1] // 256 * 256
    down = w_down.T
    return jnp.concatenate([w_up[:, :main], down[:, :main], w_up[:, main:], down[:, main:]], axis=1)


class QuickWeights:
    def __init__(self, place, w_qkv, w_out, w_up, w_down, padded):
        self.place, self.padded = place, padded
        self.rows = w_qkv.shape[0]
        self.cols = place.columns
        self.width = w_out.shape[1] * self.cols
        self.qkv_cols, self.out_cols, self.up_cols = w_qkv.shape[1], w_out.shape[1], w_up.shape[1]
        self.main = main = self.up_cols // 256 * 256
        self.rest = rest = self.up_cols - main
        self.role = place.part
        self.scalars = jnp.stack([self.role] + row_starts(self.rows)).astype(jnp.int32)
        self.pack = pack_pair(w_up, w_down)

    def start(self, w_qkv, w_out, value):
        full, rows, pack = start_exchange(
            jnp.concatenate([w_qkv, w_out], axis=1), self.pack, value, self.place.count
        )
        pair = lax.all_gather(pack, BOTH, axis=0, tiled=False)
        self.pair = pair.reshape(lax.axis_size("row"), self.cols, self.rows, 2 * self.up_cols)
        self.triple, self.out = assemble(full, self.width, self.padded, self.qkv_cols)
        return rows

    def end(self, triple_grad, out_grad, small, rows, shape, deps):
        blocks = divide(
            triple_grad, out_grad, self.width, self.padded, self.qkv_cols, self.out_cols, self.cols, 4
        )
        final, summed, tokens = end_exchange(blocks, small, rows, shape, deps)
        return final[:, : self.qkv_cols], final[:, self.qkv_cols :], summed, tokens

    def bias_order(self, bias):
        blocks = bias.reshape(self.cols, self.up_cols)
        return jnp.concatenate([blocks[:, : self.main].reshape(-1), blocks[:, self.main :].reshape(-1)])

    def bias_back(self, grad):
        edge = self.cols * self.main
        return jnp.concatenate(
            [grad[:edge].reshape(self.cols, self.main), grad[edge:].reshape(self.cols, self.rest)], axis=1
        ).reshape(-1)

    def pair_final(self, parts):
        final = jnp.sum(parts.astype(jnp.float32), axis=0)
        main, rest = self.main, self.rest
        own = jnp.concatenate([final[:, :main], final[:, 2 * main : 2 * main + rest]], axis=1)
        far = jnp.concatenate([final[:, main : 2 * main], final[:, 2 * main + rest :]], axis=1)
        up = jnp.where(self.role == 0, own, far)
        down = jnp.where(self.role == 0, far, own)
        return up, down.T


class PlainWeights:
    def __init__(self, place, w_qkv, w_out, w_up, w_down, padded):
        self.place, self.padded = place, padded
        qkv, out = plain_gather(w_qkv), plain_gather(w_out)
        self.width = width = out.shape[1]
        pad = padded - width
        self.triple = jnp.pad(qkv.reshape(width, 3, width), ((0, 0), (0, 0), (0, pad))).reshape(
            width, 3 * padded
        )
        self.out = jnp.pad(out, ((0, pad), (0, pad)))
        self.rows, self.cols, self.up_cols = w_qkv.shape[0], place.columns, w_up.shape[1]
        self.main = self.up_cols // 256 * 256
        self.rest = self.up_cols - self.main
        full = lax.all_gather(pack_pair(w_up, w_down), BOTH, axis=0, tiled=False)
        full = full.reshape(lax.axis_size("row"), self.cols, self.rows, 2 * self.up_cols)
        self.pair = full.transpose(1, 0, 2, 3).reshape(1, self.cols, width, 2 * self.up_cols)
        self.scalars = jnp.zeros((2,), jnp.int32)

    def bias_order(self, bias):
        blocks = bias.reshape(self.cols, self.up_cols)
        return jnp.concatenate([blocks[:, : self.main].reshape(-1), blocks[:, self.main :].reshape(-1)])

    def bias_back(self, grad):
        edge = self.cols * self.main
        return jnp.concatenate(
            [grad[:edge].reshape(self.cols, self.main), grad[edge:].reshape(self.cols, self.rest)], axis=1
        ).reshape(-1)

    def natural(self, grad):
        edge = self.cols * self.main
        cut = lambda value: value.reshape(grad.shape[0], self.cols, -1)
        return jnp.concatenate([cut(grad[:, :edge]), cut(grad[:, edge:])], axis=2).reshape(grad.shape)

    def scatter_pair(self, mine, theirs):
        return plain_scatter(self.natural(mine)), plain_scatter(self.natural(theirs)).T

    def scatter_first(self, triple_grad, out_grad):
        width, padded = self.width, self.padded
        qkv = triple_grad.reshape(width, 3, padded)[:, :, :width].reshape(width, 3 * width)
        return plain_scatter(qkv), plain_scatter(out_grad[:, :width])


def cuts_of(pairs, count):
    edges = [round(i * pairs / count) for i in range(count + 1)]
    return list(zip(edges[:-1], edges[1:]))


def local(
    block_input, paths, ln1_gain, ln1_bias, w_qkv, q_bias, v_bias, w_out, out_bias,
    ln2_gain, ln2_bias, w_up, up_bias, w_down, down_bias, cotangent,
):
    micro, _, width = block_input.shape
    place = Place(micro, paths.shape[2])
    parts = place.parts
    heads = width // HEAD_DIM
    padded = (heads + 1) // 2 * 128
    pairs = padded // 128
    pad = padded - width
    own_trunk = TRUNK // parts
    f32, bf16 = jnp.float32, jnp.bfloat16

    quick = lax.axis_size("row") == 4 and parts == 2 and w_qkv.shape[0] == 272
    if quick:
        weights = QuickWeights(place, w_qkv, w_out, w_up, w_down, padded)
        rows_low = weights.start(w_qkv, w_out, block_input)
    else:
        weights = PlainWeights(place, w_qkv, w_out, w_up, w_down, padded)
        rows_low = place.to_tree(place.tree_sources(place.swap_quarters(block_input)))
    rows_in = rows_low.astype(f32)

    own_ids = lax.dynamic_index_in_dim(paths[0], place.quarter, 0, keepdims=False)
    parent_ids = lax.dynamic_index_in_dim(paths[1], place.quarter, 0, keepdims=False)
    mask_trunk, mask_group = place.masks(own_ids, parent_ids)

    seed_moved = place.swap_quarters(cotangent)

    q_scale = HEAD_DIM**-0.5 * LOG2E
    triple_bias = jnp.concatenate(
        [jnp.pad(q_bias * q_scale, (0, pad)), jnp.zeros((padded,), f32), jnp.pad(v_bias, (0, pad))]
    )
    triple_scale = jnp.concatenate([jnp.full((padded,), q_scale, f32), jnp.ones((2 * padded,), f32)])
    first = layer_norm(rows_in, ln1_gain, ln1_bias).astype(bf16)
    triple = (dot_nn(first, weights.triple) * triple_scale + triple_bias).astype(bf16)
    shared = triple[:own_trunk, padded:]
    others = jnp.concatenate(
        [lax.ppermute(shared, "col", place.part_perm(e)) for e in range(1, parts)], axis=0
    )
    mixed, lse = attention_forward(parts, heads, triple, others, mask_trunk, mask_group, 0, pairs)
    seed_rows = place.to_tree(place.tree_sources(after(seed_moved, mixed)))
    middle, second = project_out(mixed, rows_low, weights.out, out_bias, ln2_gain, ln2_bias)
    outs = 4 if quick else 1
    lowered, second_grad, up_bias_grad, *pair_grads = feed_forward(
        weights.scalars, weights.pair, second, seed_rows, weights.bias_order(up_bias), outs
    )
    pair_mine, pair_theirs = pair_grads[:outs], pair_grads[outs:]
    up_bias_grad = weights.bias_back(up_bias_grad.reshape(-1))
    result, middle_grad, mixed_grad, sums, out_padded = middle_back(
        second_grad, lowered, middle, seed_rows, mixed, weights.out, ln2_gain, down_bias
    )
    out_bias_grad, gain_two, shift_two, down_bias_grad = sums[0], sums[1], sums[2], sums[3]

    turned = jnp.swapaxes(mask_trunk, 1, 2), jnp.swapaxes(mask_group, 1, 2)
    result_sources = place.from_tree_sources(result)
    if quick:
        pair_swapped = {d: core_swap(place, pair_theirs[d]) for d in (3, 1, 2, 0)}
        sums = far_sums(pair_mine, pair_swapped)
    grads = ()
    for index, (start, stop) in enumerate(cuts_of(pairs, 4)):
        deps = ()
        if quick and index == 0:
            deps = sums
            received = far_sends(sums)
        if index == 1:
            result_parts = place.from_tree_parts(result_sources)
            deps = (result_parts,)
            result_out = place.swap_quarters(result_parts)
            if quick:
                sums = near_sums(pair_mine, pair_swapped, received)
                deps = deps + sums
                last = near_sends(sums)
        if quick and index == 3:
            total = row_total(pair_mine, pair_swapped, received, last)
            deps = (total,)
        grads = attention_backward(
            parts, heads, triple, others, mixed, mixed_grad, lse, *turned, start, stop, grads, deps
        )
    deps = ()
    if quick:
        blocks = pair_blocks(
            place.part.reshape(1).astype(jnp.int32), total, core_swap(place, total), weights.main, weights.rest
        )
        pair_parts = place.swap_quarters(blocks)
        deps = (blocks,)
    else:
        up_grad, down_grad = weights.scatter_pair(pair_mine[0], pair_theirs[0])
    dq, dk, dv, dko, dvo = grads
    other_k, other_v = (
        jnp.concatenate(
            [
                lax.ppermute(part[(e - 1) * own_trunk : e * own_trunk], "col", place.part_perm(e))
                for e in range(1, parts)
            ],
            axis=0,
        )
        for part in (dko, dvo)
    )
    triple_grad, triple_sums = finish_gradients(own_trunk, dq, dk, dv, other_k, other_v, deps)
    q_bias_grad = triple_sums[0, :width]
    v_bias_grad = triple_sums[0, 2 * padded : 2 * padded + width]
    input_grad, sums = first_back(triple_grad, rows_low, middle_grad, weights.triple, ln1_gain)
    gain_one, shift_one = sums[0], sums[1]
    triple_weight_grad = dot_tn(first, triple_grad).astype(bf16)
    small = [
        gain_one, shift_one, q_bias_grad, v_bias_grad, out_bias_grad, gain_two, shift_two, up_bias_grad,
        down_bias_grad,
    ]
    if quick:
        up_grad, down_grad = weights.pair_final(pair_parts)
        flat = jnp.concatenate(small)
        flat = jnp.pad(flat, (0, -flat.shape[0] % 1024)).reshape(-1, 128)
        qkv_grad, out_grad, flat, input_grad_out = weights.end(
            triple_weight_grad, out_padded, flat, input_grad, block_input.shape, (up_grad, down_grad)
        )
        edges = np.cumsum([0] + [v.shape[0] for v in small])
        flat = flat.reshape(-1)
        small = [flat[low:high] for low, high in zip(edges[:-1], edges[1:])]
    else:
        qkv_grad, out_grad = weights.scatter_first(triple_weight_grad, out_padded)
        small = lax.psum(small, BOTH)
        input_grad_out = place.swap_quarters(
            place.from_tree_parts(place.from_tree_sources(input_grad))
        )
    return (
        result_out, input_grad_out, small[0], small[1], qkv_grad, small[2], small[3],
        out_grad, small[4], small[5], small[6], up_grad, small[7], down_grad, small[8],
    )


def solution(mesh):
    rows = P(None, BOTH, None)
    placed = (
        rows, P(None, None, "row"), P(), P(), P("row", "col"), P(), P(), P("row", "col"), P(),
        P(), P(), P("row", "col"), P(), P("col", "row"), P(), rows,
    )
    out = (
        rows, rows, P(), P(), P("row", "col"), P(), P(), P("row", "col"), P(),
        P(), P(), P("row", "col"), P(), P("col", "row"), P(),
    )
    return jax.shard_map(local, mesh=mesh, in_specs=placed, out_specs=out, check_vma=False)
```

```python
import math
from functools import partial

import jax
import jax.numpy as jnp
import numpy as np
from jax import lax
from jax.experimental import pallas as pl
from jax.experimental.pallas import tpu as pltpu
from jax.sharding import PartitionSpec as P

HEAD_DIM = 64
TRUNK = 1024
GROUP = 384
QT = 256
LOG2E = 1.4426950408889634
LN2 = 0.6931471805599453


def dot_nn(a, b):
    return jnp.dot(a, b, preferred_element_type=jnp.float32)


def dot_nt(a, b):
    return lax.dot_general(a, b, (((1,), (1,)), ((), ())), preferred_element_type=jnp.float32)


def dot_tn(a, b):
    return lax.dot_general(a, b, (((0,), (0,)), ((), ())), preferred_element_type=jnp.float32)


def lane_masks(head):
    lane = lax.broadcasted_iota(jnp.int32, (1, 128), 1)
    inside = (lane // HEAD_DIM) == head
    return inside, inside.astype(jnp.float32).astype(jnp.bfloat16), lane % HEAD_DIM


def fill_trunk(parts, own_ref, other_ref, out_ref):
    own = TRUNK // parts
    for tile in range(own // QT):
        for part in range(parts):
            rows = (
                own_ref[tile * QT : (tile + 1) * QT, :]
                if part == 0
                else other_ref[(part - 1) * own + tile * QT : (part - 1) * own + (tile + 1) * QT, :]
            )
            start = (tile * parts + part) * QT
            out_ref[start : start + QT, :] = rows


def fwd_kernel(parts, heads, start, extra, q_ref, k_ref, v_ref, ko_ref, vo_ref, mt_ref, mg_ref, *refs):
    o_ref, lse_ref, kt, vt, va = refs[extra:]
    pair = start + pl.program_id(0)
    own = TRUNK // parts
    tiles = own // QT
    groups = (TRUNK // 256) // parts
    fill_trunk(parts, k_ref, ko_ref, kt)
    fill_trunk(parts, v_ref, vo_ref, vt)
    o_ref[...] = jnp.zeros_like(o_ref)
    lse_ref[...] = jnp.zeros_like(lse_ref)

    def finish(rows, top, total, inside):
        turned = pltpu.roll(total, HEAD_DIM, 1)
        o_ref[rows, :] += jnp.where(inside, total / turned, 0.0).astype(jnp.bfloat16)
        lse_ref[rows, :] += jnp.where(inside, 0.0, top + jnp.log2(total))

    def head_body(head):
        inside, hm, _ = lane_masks(head)
        rest = 1 - hm
        va[...] = vt[...] * hm + rest
        for tile in range(tiles):
            rows = pl.ds(tile * QT, QT)
            q = q_ref[rows, :] * hm
            near = tile * parts * QT
            s_near = dot_nt(q, kt[near : near + parts * QT, :]) + mt_ref[tile]
            top = jnp.max(s_near, axis=1, keepdims=True)
            if tile > 0:
                s_far = dot_nt(q, kt[:near, :])
                top = jnp.maximum(top, jnp.max(s_far, axis=1, keepdims=True))
            p_near = jnp.exp2(s_near - top).astype(jnp.bfloat16)
            total = dot_nn(p_near, va[near : near + parts * QT, :])
            if tile > 0:
                total += dot_nn(jnp.exp2(s_far - top).astype(jnp.bfloat16), va[:near, :])
            finish(rows, top, total, inside)

        for group in range(groups):
            rows = pl.ds(own + group * GROUP, GROUP)
            q = q_ref[rows, :] * hm
            s_near = dot_nt(q, k_ref[rows, :]) + mg_ref[group]
            s_far = dot_nt(q, kt[...])
            top = jnp.maximum(
                jnp.max(s_near, axis=1, keepdims=True), jnp.max(s_far, axis=1, keepdims=True)
            )
            near = v_ref[rows, :] * hm + rest
            total = dot_nn(jnp.exp2(s_near - top).astype(jnp.bfloat16), near)
            total += dot_nn(jnp.exp2(s_far - top).astype(jnp.bfloat16), va[...])
            finish(rows, top, total, inside)

    head_body(0)
    pl.when(2 * pair + 1 < heads)(lambda: head_body(1))


def attention_forward(parts, heads, triple, others, mask_trunk, mask_group, start, stop, before=(), deps=()):
    fixed = 7
    aliases = {fixed + index: index for index in range(len(before))}
    deps = tuple(before) + tuple(deps)
    rows = triple.shape[0]
    pairs = triple.shape[1] // (3 * 128)
    extra = others.shape[0]
    block = lambda count, shift: pl.BlockSpec((count, 128), lambda i: (0, i + shift))
    whole = lambda shape: pl.BlockSpec(shape, lambda i: (0,) * len(shape))
    return pl.pallas_call(
        partial(fwd_kernel, parts, heads, start, len(deps)),
        grid=(stop - start,),
        in_specs=[
            block(rows, start),
            block(rows, start + pairs),
            block(rows, start + 2 * pairs),
            block(extra, start),
            block(extra, start + pairs),
            whole(mask_trunk.shape),
            whole(mask_group.shape),
        ]
        + [pl.BlockSpec(memory_space=pl.ANY)] * len(deps),
        out_specs=[block(rows, start)] * 2,
        input_output_aliases=aliases,
        out_shape=[
            jax.ShapeDtypeStruct((rows, pairs * 128), jnp.bfloat16),
            jax.ShapeDtypeStruct((rows, pairs * 128), jnp.float32),
        ],
        scratch_shapes=[
            pltpu.VMEM((TRUNK, 128), jnp.bfloat16),
            pltpu.VMEM((TRUNK, 128), jnp.bfloat16),
            pltpu.VMEM((TRUNK, 128), jnp.bfloat16),
        ],
        compiler_params=pltpu.CompilerParams(vmem_limit_bytes=48 * 1024 * 1024),
        cost_estimate=pl.CostEstimate(
            flops=(stop - start) * rows * 5_200_000, bytes_accessed=rows * pairs * 2000, transcendentals=0
        ),
        name="attention_forward",
    )(triple, triple, triple, others, others, mask_trunk, mask_group, *deps)


def split_three(value, place, outside):
    high = value.astype(jnp.bfloat16)
    left = value - high.astype(jnp.float32)
    middle = left.astype(jnp.bfloat16)
    low = (left - middle.astype(jnp.float32)).astype(jnp.bfloat16)
    high, middle, low = (v.astype(jnp.float32) for v in (high, middle, low))
    picked = jnp.where(place == 0, high, jnp.where(place == 1, middle, jnp.where(place == 2, low, 0.0)))
    return jnp.where(outside, picked, 0.0).astype(jnp.bfloat16)


def bwd_kernel(
    parts, heads, start, extra, q_ref, k_ref, v_ref, ko_ref, vo_ref, o_ref, do_ref, lse_ref, mt_ref, mg_ref,
    *refs,
):
    dq_ref, dk_ref, dv_ref, dko_ref, dvo_ref = refs[extra : extra + 5]
    kt, vt, ka, va, qa, da, qm, dm, dkt, dvt, dkg, dvg, dqs, kat = refs[extra + 5 :]
    pair = start + pl.program_id(0)
    own = TRUNK // parts
    tiles = own // QT
    groups = (TRUNK // 256) // parts
    rows_all = own + groups * GROUP
    fill_trunk(parts, k_ref, ko_ref, kt)
    fill_trunk(parts, v_ref, vo_ref, vt)
    dkt[...] = jnp.zeros_like(dkt)
    dvt[...] = jnp.zeros_like(dvt)
    dkg[...] = jnp.zeros_like(dkg)
    dvg[...] = jnp.zeros_like(dvg)
    dqs[...] = jnp.zeros_like(dqs)

    def head_body(head):
        inside, hm, place = lane_masks(head)
        rest = 1 - hm
        outside = jnp.logical_not(inside)
        ka[:TRUNK, :] = kt[...] * hm + rest
        va[:TRUNK, :] = vt[...] * hm + rest
        ka[TRUNK:, :] = k_ref[own:, :] * hm + rest
        va[TRUNK:, :] = v_ref[own:, :] * hm + rest

        kat[:, :TRUNK] = (kt[...] * hm).T
        kat[:, TRUNK:] = (k_ref[own:, :] * hm).T

        part = 256 if rows_all % 256 == 0 else 128
        for index in range(rows_all // part):
            rows = pl.ds(index * part, part)
            q = q_ref[rows, :] * hm
            d = do_ref[rows, :] * hm
            qm[rows, :] = q
            dm[rows, :] = d
            qa[rows, :] = q - split_three(lse_ref[rows, :], place, outside)
            delta = jnp.sum(
                d.astype(jnp.float32) * o_ref[rows, :].astype(jnp.float32), axis=1, keepdims=True
            )
            da[rows, :] = d - split_three(jnp.broadcast_to(delta, (part, 128)), place, outside)

        def step(rows, keys, mask, keep, dk, dv):
            st = dot_nt(ka[keys, :], qa[rows, :])
            if mask is not None:
                st = st + mask
            p = jnp.exp2(st)
            dp = dot_nt(va[keys, :], da[rows, :])
            ds = (p * dp).astype(jnp.bfloat16)
            dv[keep, :] += dot_nn(p.astype(jnp.bfloat16), dm[rows, :])
            dk[keep, :] += dot_nn(ds, qm[rows, :])
            dqs[:, rows] += dot_nn(kat[:, keys], ds)

        span = parts * QT
        for tile in range(tiles):
            rows = pl.ds(tile * QT, QT)
            for near in range(tile + 1):
                keys = pl.ds(near * span, span)
                step(rows, keys, mt_ref[tile] if near == tile else None, keys, dkt, dvt)
        step(pl.ds(own, groups * GROUP), pl.ds(0, TRUNK), None, pl.ds(0, TRUNK), dkt, dvt)
        for group in range(groups):
            step(
                pl.ds(own + group * GROUP, GROUP), pl.ds(TRUNK + group * GROUP, GROUP), mg_ref[group],
                pl.ds(group * GROUP, GROUP), dkg, dvg,
            )

    head_body(0)
    pl.when(2 * pair + 1 < heads)(lambda: head_body(1))
    dq_ref[...] = (dqs[...].T * HEAD_DIM**-0.5).astype(jnp.bfloat16)
    dk_ref[own:, :] = (dkg[...] * LN2).astype(jnp.bfloat16)
    dv_ref[own:, :] = dvg[...].astype(jnp.bfloat16)
    for tile in range(tiles):
        for part in range(parts):
            source = pl.ds((tile * parts + part) * QT, QT)
            if part == 0:
                dk_ref[tile * QT : (tile + 1) * QT, :] = (dkt[source, :] * LN2).astype(jnp.bfloat16)
                dv_ref[tile * QT : (tile + 1) * QT, :] = dvt[source, :].astype(jnp.bfloat16)
            else:
                start = (part - 1) * own + tile * QT
                dko_ref[start : start + QT, :] = (dkt[source, :] * LN2).astype(jnp.bfloat16)
                dvo_ref[start : start + QT, :] = dvt[source, :].astype(jnp.bfloat16)


def attention_backward(
    parts, heads, triple, others, mixed, mixed_grad, lse, mask_trunk, mask_group, start, stop, before=(), deps=()
):
    fixed = 10
    aliases = {fixed + index: index for index in range(len(before))}
    deps = tuple(before) + tuple(deps)
    rows = triple.shape[0]
    pairs = triple.shape[1] // (3 * 128)
    extra = others.shape[0]
    block = lambda count, shift: pl.BlockSpec((count, 128), lambda i: (0, i + shift))
    whole = lambda shape: pl.BlockSpec(shape, lambda i: (0,) * len(shape))
    near = rows - TRUNK // parts
    return pl.pallas_call(
        partial(bwd_kernel, parts, heads, start, len(deps)),
        grid=(stop - start,),
        in_specs=[
            block(rows, start),
            block(rows, start + pairs),
            block(rows, start + 2 * pairs),
            block(extra, start),
            block(extra, start + pairs),
            block(rows, start),
            block(rows, start),
            block(rows, start),
            whole(mask_trunk.shape),
            whole(mask_group.shape),
        ]
        + [pl.BlockSpec(memory_space=pl.ANY)] * len(deps),
        out_specs=[block(rows, start)] * 3 + [block(extra, start)] * 2,
        input_output_aliases=aliases,
        out_shape=[
            jax.ShapeDtypeStruct((rows, pairs * 128), jnp.bfloat16),
            jax.ShapeDtypeStruct((rows, pairs * 128), jnp.bfloat16),
            jax.ShapeDtypeStruct((rows, pairs * 128), jnp.bfloat16),
            jax.ShapeDtypeStruct((extra, pairs * 128), jnp.bfloat16),
            jax.ShapeDtypeStruct((extra, pairs * 128), jnp.bfloat16),
        ],
        scratch_shapes=[
            pltpu.VMEM((TRUNK, 128), jnp.bfloat16),
            pltpu.VMEM((TRUNK, 128), jnp.bfloat16),
            pltpu.VMEM((TRUNK + near, 128), jnp.bfloat16),
            pltpu.VMEM((TRUNK + near, 128), jnp.bfloat16),
            pltpu.VMEM((rows, 128), jnp.bfloat16),
            pltpu.VMEM((rows, 128), jnp.bfloat16),
            pltpu.VMEM((rows, 128), jnp.bfloat16),
            pltpu.VMEM((rows, 128), jnp.bfloat16),
            pltpu.VMEM((TRUNK, 128), jnp.float32),
            pltpu.VMEM((TRUNK, 128), jnp.float32),
            pltpu.VMEM((near, 128), jnp.float32),
            pltpu.VMEM((near, 128), jnp.float32),
            pltpu.VMEM((128, rows), jnp.float32),
            pltpu.VMEM((128, TRUNK + near), jnp.bfloat16),
        ],
        compiler_params=pltpu.CompilerParams(vmem_limit_bytes=56 * 1024 * 1024),
        cost_estimate=pl.CostEstimate(
            flops=(stop - start) * rows * 1_000_000, bytes_accessed=rows * pairs * 4000, transcendentals=0
        ),
        name="attention_backward",
    )(triple, triple, triple, others, others, mixed, mixed_grad, lse, mask_trunk, mask_group, *deps)


def normal_share(value):
    size = jnp.abs(value)
    turn = 1.0 / (1.0 + 0.23164189 * size)
    bell = jnp.exp2(value * value * -0.7213475204444817)
    poly = (((0.530702714 * turn - 0.726576013) * turn + 0.710706870) * turn - 0.142248368) * turn
    tail = (poly + 0.127414796) * turn * bell
    return jnp.where(value < 0, tail, 1.0 - tail), bell


FF_BLOCK = 256
ROW_CHUNK = 640


def join_tails(slabs, rows, up, down):
    rest = FF_BLOCK // len(slabs)
    for shift, target in ((0, up), (rest, down)):
        joined = jnp.concatenate([slab[:, shift : shift + rest] for slab in slabs], axis=1)
        target[rows, :] = joined.astype(jnp.bfloat16)


def plain_load(step, is_rest, scalars, refs, up, down):
    main, tails = refs

    @pl.when(jnp.logical_not(is_rest))
    def _():
        up[...] = main[0, 0, :, :FF_BLOCK]
        down[...] = main[0, 0, :, FF_BLOCK:]

    @pl.when(is_rest)
    def _():
        slabs = [tails[0, c].astype(jnp.float32) for c in range(tails.shape[1])]
        join_tails(slabs, slice(None), up, down)


def plain_specs(main):
    last = main.shape[1] - 1
    return [
        pl.BlockSpec((1, 1, main.shape[2], 2 * FF_BLOCK), lambda j, s: (0, jnp.minimum(j, last), 0, 0)),
        pl.BlockSpec(main.shape[:3] + (128,), lambda j, s: (0, 0, 0, 4)),
    ], [main, main]


def quick_load(step, is_rest, scalars, refs, up, down):
    role = scalars[0]
    bodies, tails = (refs[:5], refs[5:10]), (refs[10:15], refs[15:20])
    height = bodies[0][0].shape[1]
    spot = lambda d: pl.ds(pl.multiple_of(scalars[1 + d], 16), height)
    low_quarter = (step % 8) // 2 < 2

    def place(pieces):
        def put(d, piece):
            up[spot(d), :] = piece[0, :, :FF_BLOCK]
            down[spot(d), :] = piece[0, :, FF_BLOCK:]

        for d in range(3):
            put(d, pieces[d])
        pl.when(low_quarter)(lambda: put(3, pieces[3]))
        pl.when(jnp.logical_not(low_quarter))(lambda: put(3, pieces[4]))

    use_mine = jnp.logical_and(step // 8 == role, jnp.logical_not(is_rest))
    use_theirs = jnp.logical_and(step // 8 == 1 - role, jnp.logical_not(is_rest))
    pl.when(use_mine)(lambda: place(bodies[0]))
    pl.when(use_theirs)(lambda: place(bodies[1]))

    def rest(order):
        for d in range(4):
            slabs = []
            for which in order:
                pieces = tails[which]
                for q in range(4):
                    piece = pieces[d][q] if d < 3 else (pieces[3][q] if q < 2 else pieces[4][q - 2])
                    slabs.append(piece.astype(jnp.float32))
            join_tails(slabs, spot(d), up, down)

    pl.when(jnp.logical_and(is_rest, role == 0))(lambda: rest((0, 1)))
    pl.when(jnp.logical_and(is_rest, role != 0))(lambda: rest((1, 0)))


def quick_specs(mine, theirs):
    def body(shape, which, low, high):
        def index(j, s):
            turn = jnp.clip(j - 8 * (s[0] if which == 0 else 1 - s[0]), 0, 7)
            return (jnp.clip(turn // 2, low, high) - low, 0, turn % 2)

        return pl.BlockSpec((1, shape[1], 2 * FF_BLOCK), index)

    spans = ((0, 3), (0, 3), (0, 3), (0, 1), (2, 3))
    bodies = [
        body(piece.shape, which, *span)
        for which, pieces in enumerate((mine, theirs))
        for piece, span in zip(pieces, spans)
    ]
    tails = [
        pl.BlockSpec(piece.shape[:2] + (128,), lambda j, s: (0, 0, 8))
        for pieces in (mine, theirs)
        for piece in pieces
    ]
    arrays = list(mine) + list(theirs)
    return bodies + tails, arrays * 2


def ffn_kernel(load, held, outs, chunk, scalars, *refs):
    weights, refs = refs[:held], refs[held:]
    second, seed, bias = refs[:3]
    lowered, second_grad, bias_grad = refs[3:6]
    mine_grads, theirs_grads = refs[6 : 6 + outs], refs[6 + outs : 6 + 2 * outs]
    up, down, act, wide, up_grad, down_grad, second_t, seed_t = refs[6 + 2 * outs :]
    step = pl.program_id(0)
    role = scalars[0]
    load(step, step == pl.num_programs(0) - 1, scalars, weights, up, down)

    @pl.when(step == 0)
    def _():
        lowered[...] = jnp.zeros_like(lowered)
        second_grad[...] = jnp.zeros_like(second_grad)
        for start in range(0, second.shape[0], 128):
            rows = pl.ds(start, 128)
            second_t[:, rows] = second[rows, :].T
            seed_t[:, rows] = seed[rows, :].T

    total = jnp.zeros((1, FF_BLOCK), jnp.float32)
    for start in range(0, second.shape[0], chunk):
        rows = pl.ds(start, chunk)
        wide_in = dot_nn(second[rows, :], up[...]) + bias[...]
        hidden = dot_nn(seed[rows, :], down[...])
        share, bell = normal_share(wide_in)
        act_now = (wide_in * share).astype(jnp.bfloat16)
        slope = share + wide_in * (bell * 0.3989422804014327)
        wide_now = (hidden * slope).astype(jnp.bfloat16)
        total += jnp.sum(wide_now.astype(jnp.float32), axis=0, keepdims=True)
        act[rows, :] = act_now
        wide[rows, :] = wide_now
        lowered[rows, :] += dot_nt(act_now, down[...])
        second_grad[rows, :] += dot_nt(wide_now, up[...])
    bias_grad[...] = total
    up_grad[...] = dot_nn(second_t[...], wide[...]).astype(jnp.bfloat16)
    down_grad[...] = dot_nn(seed_t[...], act[...]).astype(jnp.bfloat16)

    def deliver(first_grad, second_grad):
        for index in range(outs):
            size = mine_grads[index].shape[0]
            rows = pl.ds(pl.multiple_of(scalars[1 + index], 16), size)
            mine_grads[index][...] = first_grad[rows, :]
            theirs_grads[index][...] = second_grad[rows, :]

    @pl.when(role == 0)
    def _():
        deliver(up_grad, down_grad)

    @pl.when(role != 0)
    def _():
        deliver(down_grad, up_grad)


def feed_forward(scalars, pair, second, seed, bias, outs):
    rows, width = second.shape
    hidden = bias.shape[0]
    quick = len(pair) == 2
    specs, arrays = quick_specs(*pair) if quick else plain_specs(*pair)
    load = quick_load if quick else plain_load
    whole = lambda shape: pl.BlockSpec(shape, lambda j, s: (0, 0))
    grad_spec = pl.BlockSpec((width // outs, FF_BLOCK), lambda j, s: (0, j))
    grad_shape = jax.ShapeDtypeStruct((width // outs, hidden), jnp.bfloat16)
    line = pl.BlockSpec((1, FF_BLOCK), lambda j, s: (0, j))
    chunk = ROW_CHUNK if rows % ROW_CHUNK == 0 else rows // 2
    return pl.pallas_call(
        partial(ffn_kernel, load, len(specs), outs, chunk),
        grid_spec=pltpu.PrefetchScalarGridSpec(
            num_scalar_prefetch=1,
            grid=(hidden // FF_BLOCK,),
            in_specs=specs + [
                whole((rows, width)), whole((rows, width)), line,
            ],
            out_specs=[whole((rows, width)), whole((rows, width)), line] + [grad_spec] * (2 * outs),
            scratch_shapes=[
                pltpu.VMEM((width, FF_BLOCK), jnp.bfloat16),
                pltpu.VMEM((width, FF_BLOCK), jnp.bfloat16),
                pltpu.VMEM((rows, FF_BLOCK), jnp.bfloat16),
                pltpu.VMEM((rows, FF_BLOCK), jnp.bfloat16),
                pltpu.VMEM((width, FF_BLOCK), jnp.bfloat16),
                pltpu.VMEM((width, FF_BLOCK), jnp.bfloat16),
                pltpu.VMEM((width, rows), jnp.bfloat16),
                pltpu.VMEM((width, rows), jnp.bfloat16),
            ],
        ),
        out_shape=[
            jax.ShapeDtypeStruct((rows, width), jnp.float32),
            jax.ShapeDtypeStruct((rows, width), jnp.float32),
            jax.ShapeDtypeStruct((1, hidden), jnp.float32),
        ]
        + [grad_shape] * (2 * outs),
        compiler_params=pltpu.CompilerParams(vmem_limit_bytes=60 * 1024 * 1024),
        cost_estimate=pl.CostEstimate(
            flops=24 * rows * width * hidden, bytes_accessed=8 * width * hidden + 20 * rows * width,
            transcendentals=rows * hidden,
        ),
        name="feed_forward",
    )(scalars, *arrays, second, seed, bias.reshape(1, hidden))


MESH = pl.DeviceIdType.MESH
HOLD = pl.BlockSpec(memory_space=pl.ANY)


def greet(peers):
    barrier = pltpu.get_barrier_semaphore()
    for peer in peers:
        pl.semaphore_signal(barrier, inc=1, device_id=peer, device_id_type=MESH)
    pl.semaphore_wait(barrier, len(peers))


def remote(source, target, send, receive, device):
    return pltpu.make_async_remote_copy(
        src_ref=source, dst_ref=target, send_sem=send, recv_sem=receive,
        device_id=device, device_id_type=MESH,
    )


def chunk_home(chunk):
    block = chunk // 2
    turn = block % 4
    in_trunk = chunk < 16
    owner = jnp.where(in_trunk, ((turn + 1) // 2) % 2, (chunk - 16) // 12)
    spot = jnp.where(
        in_trunk, 2 * (2 * (block // 4) + turn // 2) + chunk % 2, 8 + (chunk - 16) % 12
    )
    return owner, spot


def start_kernel(grain, pack, later_pack, value, full, rows, later_out, z_send, z_recv, r_send, r_recv, c_send, c_recv,
                 x_send, x_recv, own_sem, later_sem):
    row, col = lax.axis_index("row"), lax.axis_index("col")
    z, core = col // 2, col % 2
    at = lambda r, c: (r, c)
    peers = [at(row, (col + shift) % 8) for shift in range(1, 8)] + [at(row ^ 1, col), at(row ^ 2, col)]
    greet(peers)
    later_copy = pltpu.make_async_copy(later_pack, later_out, later_sem)
    later_copy.start()
    here = full.at[core, row, z]
    own = pltpu.make_async_copy(pack, here, own_sem)
    own.start()
    sends = []
    for d in range(1, 4):
        copy = remote(pack, here, z_send.at[d - 1], z_recv.at[d - 1], at(row, (z ^ d) * 2 + core))
        copy.start()
        sends.append(copy)
    own.wait()
    for copy in sends:
        copy.wait_recv()
    later = []

    def pass_on(index, ref, device, send=r_send, receive=r_recv):
        copy = remote(ref, ref, send.at[index], receive.at[index], device)
        copy.start()
        later.append(copy)
        return copy

    beside = pass_on(0, full.at[core, row], at(row ^ 1, col))
    below = pass_on(1, full.at[core, row], at(row ^ 2, col))
    swaps = [pass_on(0, full.at[core, row], at(row, col ^ 1), c_send, c_recv)]

    each = value.shape[1] // grain

    def each_chunk(act_remote, act_own):
        for m in range(4):
            for i in range(each):
                owner, spot = chunk_home(col * each + i)
                source = value.at[m, pl.ds(i * grain, grain), :]
                target = rows.at[pl.ds(pl.multiple_of(spot * grain, grain), grain), :]
                same = jnp.logical_and(z == m, owner == core)
                index = m * each + i

                @pl.when(jnp.logical_not(same))
                def _():
                    act_remote(
                        remote(source, target, x_send.at[index], x_recv, at(row, 2 * m + owner))
                    )

                if act_own:

                    @pl.when(same)
                    def _():
                        pltpu.make_async_copy(source, target, x_recv).start()

    each_chunk(lambda copy: copy.start(), True)
    beside.wait_recv()
    far_a = pass_on(2, full.at[core, row ^ 1, pl.ds(0, 2)], at(row ^ 2, col))
    swaps.append(pass_on(1, full.at[core, row ^ 1], at(row, col ^ 1), c_send, c_recv))
    below.wait_recv()
    far_b = pass_on(3, full.at[core, row ^ 2, pl.ds(2, 2)], at(row ^ 1, col))
    swaps.append(pass_on(2, full.at[core, row ^ 2], at(row, col ^ 1), c_send, c_recv))
    far_a.wait_recv()
    far_b.wait_recv()
    swaps.append(pass_on(3, full.at[core, row ^ 3], at(row, col ^ 1), c_send, c_recv))
    for copy in swaps:
        copy.wait_recv()
    pltpu.make_async_copy(rows, rows, x_recv).wait()
    later_copy.wait()
    for copy in sends + later:
        copy.wait_send()
    each_chunk(lambda copy: copy.wait_send(), False)


def start_exchange(pack, later_pack, value, count):
    grain = 64
    height, lanes = pack.shape
    copies = 4 * (value.shape[1] // grain)
    dma = lambda n: pltpu.SemaphoreType.DMA((n,))
    return pl.pallas_call(
        partial(start_kernel, grain),
        in_specs=[HOLD] * 3,
        out_specs=[HOLD] * 3,
        out_shape=[
            jax.ShapeDtypeStruct((2, 4, 4, height, lanes), pack.dtype),
            jax.ShapeDtypeStruct((count, value.shape[2]), value.dtype),
            jax.ShapeDtypeStruct(later_pack.shape, later_pack.dtype),
        ],
        scratch_shapes=[
            dma(3), dma(3), dma(4), dma(4), dma(4), dma(4), dma(copies),
            pltpu.SemaphoreType.DMA, pltpu.SemaphoreType.DMA, pltpu.SemaphoreType.DMA,
        ],
        compiler_params=pltpu.CompilerParams(collective_id=0, has_side_effects=True),
        cost_estimate=pl.CostEstimate(flops=100_000_000_000, bytes_accessed=0, transcendentals=0),
        name="start_exchange",
    )(pack, later_pack, value)


def end_kernel(
    grain, grads, small, rows, *refs,
):
    final, small_out, tokens, mine, swapped, far, beside, below, tail, small_col, small_row, part = refs[-26:-14]
    own_sem, c_send, c_recv, r_send, r_recv, z_send, z_recv, s_send, s_recv, t_send, t_recv, _, x_send, x_recv = refs[-14:]
    row, col = lax.axis_index("row"), lax.axis_index("col")
    z, core = col // 2, col % 2
    at = lambda r, c: (r, c)
    peers = [at(row, (col + shift) % 8) for shift in range(1, 8)]
    peers += [at(row ^ d, col) for d in range(1, 4)]
    greet(peers)
    own = pltpu.make_async_copy(grads.at[core], mine, own_sem)
    own.start()
    sends = []
    for d in (3, 1, 2, 0):
        copy = remote(
            grads.at[1 - core, row ^ d], swapped.at[row ^ d], c_send.at[d], c_recv.at[d], at(row, col ^ 1)
        )
        copy.start()
        sends.append(copy)
    for shift in range(1, 8):
        copy = remote(
            small, small_col.at[col], s_send.at[shift - 1], s_recv.at[7 - shift], at(row, (col + shift) % 8)
        )
        copy.start()
        sends.append(copy)
    small_col[col] = small[...]
    own.wait()
    f32 = jnp.float32
    each = tokens.shape[1] // grain

    def each_chunk(act_remote, act_own):
        for local in range(rows.shape[0] // grain):
            pair = local // 2
            turn = 4 * (pair // 2) + (core if pair % 2 == 0 else 3 - core)
            chunk = 2 * turn + local % 2 if local < 8 else 16 + 12 * core + local - 8
            shard = chunk // each
            source = rows.at[pl.ds(local * grain, grain), :]
            start = pl.multiple_of((chunk % each) * grain, grain)
            target = tokens.at[z, pl.ds(start, grain), :]

            @pl.when(shard != col)
            def _():
                act_remote(remote(source, target, x_send.at[local], x_recv, at(row, shard)))

            if act_own:

                @pl.when(shard == col)
                def _():
                    pltpu.make_async_copy(source, target, x_recv).start()

    each_chunk(lambda copy: copy.start(), True)

    def add(target, source):
        target[...] = (target[...].astype(f32) + source[...].astype(f32)).astype(target.dtype)

    def add_swapped(position):
        sends[position].wait_recv()
        d = (3, 1, 2, 0)[position]
        for q in range(4):
            add(mine.at[row ^ d, q], swapped.at[row ^ d, q])

    def send(index, source, target, device):
        copy = remote(source, target, r_send.at[index], r_recv.at[index], device)
        copy.start()
        sends.append(copy)
        return copy

    add_swapped(0)
    far_a = send(0, mine.at[row ^ 3, pl.ds(0, 2)], far.at[pl.ds(0, 2)], at(row ^ 2, col))
    far_b = send(1, mine.at[row ^ 3, pl.ds(2, 2)], far.at[pl.ds(2, 2)], at(row ^ 1, col))
    add_swapped(1)
    x_b = send(2, mine.at[row ^ 1, pl.ds(2, 2)], beside.at[pl.ds(2, 2)], at(row ^ 1, col))
    add_swapped(2)
    y_a = send(3, mine.at[row ^ 2, pl.ds(0, 2)], below.at[pl.ds(0, 2)], at(row ^ 2, col))
    add_swapped(3)
    for shift in range(1, 8):
        sends[3 + shift].wait_recv()
    part[...] = small_col[0]
    for c in range(1, 8):
        part[...] += small_col[c]
    rounds = []
    for d in range(1, 4):
        copy = remote(part, small_row.at[row], t_send.at[d - 1], t_recv.at[d - 1], at(row ^ d, col))
        copy.start()
        rounds.append(copy)
    small_row[row] = part[...]
    far_a.wait_recv()
    for q in (0, 1):
        add(mine.at[row ^ 1, q], far.at[q])
    x_a = send(4, mine.at[row ^ 1, pl.ds(0, 2)], beside.at[pl.ds(0, 2)], at(row ^ 1, col))
    far_b.wait_recv()
    for q in (2, 3):
        add(mine.at[row ^ 2, q], far.at[q])
    y_b = send(5, mine.at[row ^ 2, pl.ds(2, 2)], below.at[pl.ds(2, 2)], at(row ^ 2, col))
    for copy in (x_b, y_a, x_a, y_b):
        copy.wait_recv()

    def total(q):
        return (
            mine[row, q].astype(f32) + beside[q].astype(f32) + below[q].astype(f32)
        )

    lasts = []
    for d in range(1, 4):
        q = z ^ d
        mine[row, q] = total(q).astype(mine.dtype)
        copy = remote(
            mine.at[row, q], tail.at[d - 1], z_send.at[d - 1], z_recv.at[d - 1], at(row, q * 2 + core)
        )
        copy.start()
        lasts.append(copy)
    result = total(z)
    for d in range(1, 4):
        lasts[d - 1].wait_recv()
        result = result + tail[d - 1].astype(f32)
    final[...] = result
    for copy in rounds:
        copy.wait_recv()
    pltpu.make_async_copy(tokens, tokens, x_recv).wait()
    each_chunk(lambda copy: copy.wait_send(), False)
    small_out[...] = small_row[0] + small_row[1] + small_row[2] + small_row[3]
    for copy in sends + lasts + rounds:
        copy.wait_send()


def end_exchange(grads, small, rows, shape, deps):
    grain = 64
    height, lanes = grads.shape[3:]
    slab = lambda *n: pltpu.VMEM(n + (height, lanes), grads.dtype)
    dma = lambda n: pltpu.SemaphoreType.DMA((n,))
    return pl.pallas_call(
        partial(end_kernel, grain),
        in_specs=[HOLD, pl.BlockSpec(memory_space=pltpu.VMEM), HOLD] + [HOLD] * len(deps),
        out_specs=[pl.BlockSpec(memory_space=pltpu.VMEM)] * 2 + [HOLD],
        out_shape=[
            jax.ShapeDtypeStruct((height, lanes), jnp.float32),
            jax.ShapeDtypeStruct(small.shape, jnp.float32),
            jax.ShapeDtypeStruct(shape, rows.dtype),
        ],
        scratch_shapes=[
            slab(4, 4), slab(4, 4), slab(4), slab(4), slab(4), slab(3),
            pltpu.VMEM((8,) + small.shape, jnp.float32), pltpu.VMEM((4,) + small.shape, jnp.float32),
            pltpu.VMEM(small.shape, jnp.float32),
            pltpu.SemaphoreType.DMA, dma(4), dma(4), dma(6), dma(6), dma(3), dma(3),
            dma(7), dma(7), dma(3), dma(3), dma(1), dma(rows.shape[0] // grain), pltpu.SemaphoreType.DMA,
        ],
        compiler_params=pltpu.CompilerParams(
            collective_id=1, has_side_effects=True, vmem_limit_bytes=40 * 1024 * 1024
        ),
        cost_estimate=pl.CostEstimate(flops=100_000_000_000, bytes_accessed=0, transcendentals=0),
        name="end_exchange",
    )(grads, small, rows, *deps)


def lane_runs(width, padded, columns, qkv_cols, out_cols):
    runs = []
    for c in range(columns):
        start = c * qkv_cols
        while start < (c + 1) * qkv_cols:
            third = start // width
            stop = min((c + 1) * qkv_cols, (third + 1) * width)
            runs.append((0, third * padded + start - third * width, c, start - c * qkv_cols, stop - start))
            start = stop
        runs.append((1, c * out_cols, c, qkv_cols, out_cols))
    return runs


def assemble_kernel(runs, width, padded, full, triple, out):
    step = pl.program_id(0)
    height = full.shape[3]
    columns = 2 * full.shape[2]
    slabs = [full[c % 2, 0, c // 2].astype(jnp.float32) for c in range(columns)]
    piece = lambda run: slabs[run[2]][:, run[3] : run[3] + run[4]]
    gap = jnp.zeros((height, padded - width), jnp.float32)

    def line(which, third):
        low, high = third * padded, third * padded + padded
        chosen = [r for r in runs if r[0] == which and low <= r[1] < high]
        return jnp.concatenate([piece(r) for r in chosen] + [gap], axis=1).astype(triple.dtype)

    for third in range(3):
        triple[:, third * padded : (third + 1) * padded] = line(0, third)

    @pl.when(step == 0)
    def _():
        out[width:, :] = jnp.zeros((padded - width, padded), out.dtype)

    out[pl.ds(pl.multiple_of(step * height, 16), height), :] = line(1, 0)


def assemble(full, width, padded, qkv_cols):
    height, lanes = full.shape[3:]
    runs = lane_runs(width, padded, 2 * full.shape[2], qkv_cols, lanes - qkv_cols)
    return pl.pallas_call(
        partial(assemble_kernel, runs, width, padded),
        grid=(full.shape[1],),
        in_specs=[pl.BlockSpec((2, 1, full.shape[2], height, lanes), lambda r: (0, r, 0, 0, 0))],
        out_specs=[
            pl.BlockSpec((height, 3 * padded), lambda r: (r, 0)),
            pl.BlockSpec((padded, padded), lambda r: (0, 0)),
        ],
        out_shape=[
            jax.ShapeDtypeStruct((width, 3 * padded), full.dtype),
            jax.ShapeDtypeStruct((padded, padded), full.dtype),
        ],
        compiler_params=pltpu.CompilerParams(vmem_limit_bytes=48 * 1024 * 1024),
        cost_estimate=pl.CostEstimate(flops=12_000_000_000, bytes_accessed=0, transcendentals=0),
        name="assemble_weights",
    )(full)


def divide_kernel(runs, triple, out, full):
    wide = triple[...].astype(jnp.float32)
    last = out[...].astype(jnp.float32)
    for c in range(2 * full.shape[2]):
        parts = [
            (wide, last)[r[0]][:, r[1] : r[1] + r[4]] for r in runs if r[2] == c
        ]
        full[c % 2, 0, c // 2] = jnp.concatenate(parts, axis=1).astype(full.dtype)


def divide(triple, out, width, padded, qkv_cols, out_cols, columns, rows):
    height, lanes = width // rows, qkv_cols + out_cols
    runs = lane_runs(width, padded, columns, qkv_cols, out_cols)
    return pl.pallas_call(
        partial(divide_kernel, runs),
        grid=(rows,),
        in_specs=[
            pl.BlockSpec((height, 3 * padded), lambda r: (r, 0)),
            pl.BlockSpec((height, out.shape[1]), lambda r: (r, 0)),
        ],
        out_specs=pl.BlockSpec((2, 1, columns // 2, height, lanes), lambda r: (0, r, 0, 0, 0)),
        out_shape=jax.ShapeDtypeStruct((2, rows, columns // 2, height, lanes), jnp.bfloat16),
        compiler_params=pltpu.CompilerParams(vmem_limit_bytes=48 * 1024 * 1024),
        cost_estimate=pl.CostEstimate(flops=1_000_000_000, bytes_accessed=0, transcendentals=0),
        name="divide_gradients",
    )(triple, out)


def finish_kernel(own_trunk, dq, dk, dv, other_k, other_v, *refs):
    total, sums = refs[-2:]
    step = pl.program_id(0)
    each = pl.num_programs(0) // 3

    def deliver(value):
        total[...] = value
        sums[...] = jnp.sum(value.astype(jnp.float32), axis=0, keepdims=True)

    @pl.when(step < each)
    def _():
        deliver(dq[...])

    for index, (near, far) in enumerate(((dk, other_k), (dv, other_v))):

        @pl.when(step // each == index + 1)
        def _():
            value = near[:own_trunk, :].astype(jnp.float32)
            for start in range(0, far.shape[0], own_trunk):
                value = value + far[start : start + own_trunk, :].astype(jnp.float32)
            deliver(jnp.concatenate([value.astype(total.dtype), near[own_trunk:, :]], axis=0))


def finish_gradients(own_trunk, dq, dk, dv, other_k, other_v, deps):
    rows, padded = dq.shape
    block = 384
    each = padded // block

    def spec(count, third):
        return pl.BlockSpec((count, block), lambda j: (0, jnp.clip(j - third * each, 0, each - 1)))

    return pl.pallas_call(
        partial(finish_kernel, own_trunk),
        grid=(3 * each,),
        in_specs=[
            spec(rows, 0), spec(rows, 1), spec(rows, 2), spec(other_k.shape[0], 1), spec(other_v.shape[0], 2),
        ]
        + [HOLD] * len(deps),
        out_specs=[
            pl.BlockSpec((rows, block), lambda j: (0, j)), pl.BlockSpec((1, block), lambda j: (0, j)),
        ],
        out_shape=[
            jax.ShapeDtypeStruct((rows, 3 * padded), jnp.bfloat16),
            jax.ShapeDtypeStruct((1, 3 * padded), jnp.float32),
        ],
        compiler_params=pltpu.CompilerParams(vmem_limit_bytes=48 * 1024 * 1024),
        cost_estimate=pl.CostEstimate(flops=1_000_000_000, bytes_accessed=0, transcendentals=0),
        name="finish_gradients",
    )(dq, dk, dv, other_k, other_v, *deps)


def norm_parts(value):
    center = value - jnp.mean(value, axis=-1, keepdims=True)
    scale = lax.rsqrt(jnp.mean(center * center, axis=-1, keepdims=True) + 1e-05)
    return center * scale, scale


def norm_back(grad, value, gain):
    unit, scale = norm_parts(value)
    scaled = grad * gain
    back = scaled - jnp.mean(scaled, axis=-1, keepdims=True)
    back = scale * (back - unit * jnp.mean(scaled * unit, axis=-1, keepdims=True))
    return back, jnp.sum(grad * unit, axis=0, keepdims=True), jnp.sum(grad, axis=0, keepdims=True)


def out_kernel(mixed, weight, bias, rows, gain, shift, middle, second):
    width = rows.shape[1]
    attended = dot_nn(mixed[...], weight[...])[:, :width] + bias[...]
    total = rows[...].astype(jnp.float32) + attended.astype(jnp.bfloat16).astype(jnp.float32)
    middle[...] = total
    unit, _ = norm_parts(total)
    second[...] = (unit * gain[...] + shift[...]).astype(jnp.bfloat16)


def by_rows(kernel, name, count, chunked, fixed, outs, sums=(), scratch=(), flops=0, deps=()):
    chunk = count // 5
    block = lambda width: pl.BlockSpec((chunk, width), lambda i: (i, 0))
    whole = lambda shape: pl.BlockSpec(shape, lambda i: (0,) * len(shape))
    return pl.pallas_call(
        kernel,
        grid=(5,),
        in_specs=[block(v.shape[1]) for v in chunked] + [whole(v.shape) for v in fixed]
        + [HOLD] * len(deps),
        out_specs=[block(width) for width, _ in outs] + [whole(shape) for shape, _ in sums],
        out_shape=[jax.ShapeDtypeStruct((count, width), dtype) for width, dtype in outs]
        + [jax.ShapeDtypeStruct(shape, dtype) for shape, dtype in sums],
        scratch_shapes=list(scratch),
        compiler_params=pltpu.CompilerParams(vmem_limit_bytes=56 * 1024 * 1024),
        cost_estimate=pl.CostEstimate(flops=flops, bytes_accessed=0, transcendentals=0),
        name=name,
    )(*chunked, *fixed, *deps)


def project_out(mixed, rows, weight, bias, gain, shift):
    width = rows.shape[1]

    def kernel(mixed, rows, weight, bias, gain, shift, middle, second):
        out_kernel(mixed, weight, bias, rows, gain, shift, middle, second)

    line = lambda v: v.reshape(1, width)
    return by_rows(
        kernel, "project_out", rows.shape[0], (mixed, rows), (weight, line(bias), line(gain), line(shift)),
        ((width, jnp.float32), (width, jnp.bfloat16)), flops=12_000_000_000,
    )


def middle_kernel(held, second_grad, lowered, middle, seed, mixed, weight, gain, down_bias, *refs):
    result, middle_grad, mixed_grad, sums, out_grad, total = refs[held:]
    step = pl.program_id(0)
    width = middle.shape[1]
    value, up = middle[...], seed[...].astype(jnp.float32)
    result[...] = (value + lowered[...] + down_bias[...]).astype(jnp.bfloat16)
    back, gain_sum, shift_sum = norm_back(second_grad[...], value, gain[...])
    grad = up + back
    middle_grad[...] = grad
    low = grad.astype(jnp.bfloat16)
    mixed_grad[...] = dot_nt(low, weight[:, :width]).astype(jnp.bfloat16)
    part = dot_tn(mixed[...], low)
    low_sum = jnp.sum(low.astype(jnp.float32), axis=0, keepdims=True)
    up_sum = jnp.sum(up, axis=0, keepdims=True)
    lines = jnp.concatenate([low_sum, gain_sum, shift_sum, up_sum], axis=0)

    @pl.when(step == 0)
    def _():
        sums[...] = lines
        total[...] = part

    @pl.when(step > 0)
    def _():
        sums[...] += lines
        total[...] += part

    @pl.when(step == pl.num_programs(0) - 1)
    def _():
        out_grad[:, :width] = total[:width, :].astype(jnp.bfloat16)
        out_grad[:, width:] = jnp.zeros((width, out_grad.shape[1] - width), jnp.bfloat16)


def middle_back(second_grad, lowered, middle, seed, mixed, weight, gain, down_bias, deps):
    rows, width = middle.shape
    padded = weight.shape[0]
    line = lambda v: v.reshape(1, width)
    return by_rows(
        partial(middle_kernel, len(deps)), "middle_back", rows, (second_grad, lowered, middle, seed, mixed),
        (weight, line(gain), line(down_bias)),
        ((width, jnp.bfloat16), (width, jnp.float32), (padded, jnp.bfloat16)),
        (((4, width), jnp.float32), ((width, padded), jnp.bfloat16)),
        (pltpu.VMEM((padded, width), jnp.float32),), flops=25_000_000_000, deps=deps,
    )


def first_kernel(held, triple_grad, rows, middle_grad, weight, gain, *refs):
    input_grad, sums = refs[held:]
    step = pl.program_id(0)
    grad = dot_nt(triple_grad[...], weight[...])
    back, gain_sum, shift_sum = norm_back(grad, rows[...].astype(jnp.float32), gain[...])
    input_grad[...] = (middle_grad[...] + back).astype(jnp.bfloat16)
    lines = jnp.concatenate([gain_sum, shift_sum], axis=0)

    @pl.when(step == 0)
    def _():
        sums[...] = lines

    @pl.when(step > 0)
    def _():
        sums[...] += lines


def first_back(triple_grad, rows, middle_grad, weight, gain, deps):
    count, width = rows.shape
    return by_rows(
        partial(first_kernel, len(deps)), "first_back", count, (triple_grad, rows, middle_grad), (weight, gain.reshape(1, width)),
        ((width, jnp.bfloat16),), (((2, width), jnp.float32),), flops=4_000_000_000, deps=deps,
    )


def blocks_kernel(rest, core, total, other, total_tail, other_tail, out):
    quarter = pl.program_id(0)
    main = total.shape[1]
    out[0, :, :main] = total[...]
    out[0, :, main : 2 * main] = other[...]
    for shard in range(8):

        @pl.when(quarter + 4 * core[0] == shard)
        def _():
            cut = slice(shard * rest, (shard + 1) * rest)
            out[0, :, 2 * main : 2 * main + rest] = total_tail[:, cut]
            out[0, :, 2 * main + rest :] = other_tail[:, cut]


def pair_blocks(core, total, other, main, rest):
    rows = total.shape[0]
    spec = pl.BlockSpec((rows, main), lambda q, s: (0, q + 4 * s[0]))
    tail = pl.BlockSpec((rows, 8 * rest), lambda q, s: (0, main // rest))
    return pl.pallas_call(
        partial(blocks_kernel, rest),
        grid_spec=pltpu.PrefetchScalarGridSpec(
            num_scalar_prefetch=1,
            grid=(4,),
            in_specs=[spec, spec, tail, tail],
            out_specs=pl.BlockSpec((1, rows, 2 * (main + rest)), lambda q, s: (q, 0, 0)),
        ),
        out_shape=jax.ShapeDtypeStruct((4, rows, 2 * (main + rest)), total.dtype),
        cost_estimate=pl.CostEstimate(flops=1_000_000_000, bytes_accessed=0, transcendentals=0),
        name="pair_blocks",
    )(core, total, other, total, other)


def after(value, *deps):
    def kernel(*refs):
        pass

    return pl.pallas_call(
        kernel,
        in_specs=[HOLD] * (1 + len(deps)),
        out_specs=HOLD,
        out_shape=jax.ShapeDtypeStruct(value.shape, value.dtype),
        input_output_aliases={0: 0},
        name="after",
    )(value, *deps)


def order_kernel(table, *refs):
    pieces, out = refs[:-1], refs[-1]
    for index, piece in enumerate(pieces):
        out[table[index]] = piece[...]


def in_order(table, pieces):
    rows, width = pieces[0].shape
    whole = pl.BlockSpec((rows, width), lambda i, s: (0, 0))
    return pl.pallas_call(
        order_kernel,
        grid_spec=pltpu.PrefetchScalarGridSpec(
            num_scalar_prefetch=1,
            grid=(1,),
            in_specs=[whole] * len(pieces),
            out_specs=pl.BlockSpec((len(pieces), rows, width), lambda i, s: (0, 0, 0)),
        ),
        out_shape=jax.ShapeDtypeStruct((len(pieces), rows, width), pieces[0].dtype),
        compiler_params=pltpu.CompilerParams(vmem_limit_bytes=48 * 1024 * 1024),
        cost_estimate=pl.CostEstimate(flops=0, bytes_accessed=4 * len(pieces) * rows * width, transcendentals=0),
        name="in_order",
    )(table, *pieces)


def layer_norm(value, gain, bias):
    center = value - jnp.mean(value, axis=-1, keepdims=True)
    spread = jnp.mean(center * center, axis=-1, keepdims=True)
    return center * lax.rsqrt(spread + 1e-05) * gain + bias


def own_rows(parts, part):
    blocks = TRUNK // (128 * parts)
    starts = []
    for k in range(blocks):
        base = (k // 2) * 2 * parts
        starts.append(128 * (base + (part if k % 2 == 0 else 2 * parts - 1 - part)))
    rows = [np.arange(128) + s for s in starts]
    groups = (TRUNK // 256) // parts
    rows.append(TRUNK + part * groups * GROUP + np.arange(groups * GROUP))
    return np.concatenate(rows)


def spread_kernel(grain, table, *refs):
    pieces, out = refs[:-1], refs[-1]
    each = pieces[0].shape[0] // grain
    for index, piece in enumerate(pieces):
        for i in range(each):
            target = table[index * each + i]

            @pl.when(target >= 0)
            def _():
                rows = pl.ds(pl.multiple_of(target * grain, grain), grain)
                out[rows, :] = piece[i * grain : (i + 1) * grain, :]


def spread(table, pieces, grain, count):
    width = pieces[0].shape[1]
    whole = lambda rows: pl.BlockSpec((rows, width), lambda i, s: (0, 0))
    return pl.pallas_call(
        partial(spread_kernel, grain),
        grid_spec=pltpu.PrefetchScalarGridSpec(
            num_scalar_prefetch=1,
            grid=(1,),
            in_specs=[whole(p.shape[0]) for p in pieces],
            out_specs=whole(count),
        ),
        out_shape=jax.ShapeDtypeStruct((count, width), pieces[0].dtype),
        compiler_params=pltpu.CompilerParams(vmem_limit_bytes=48 * 1024 * 1024),
        cost_estimate=pl.CostEstimate(flops=0, bytes_accessed=6 * count * width, transcendentals=0),
        name="spread_rows",
    )(table, *pieces)


def collect_kernel(grain, count, table, *refs):
    sources, outs = refs[:-count], refs[-count:]
    each = outs[0].shape[0] // grain
    for index, out in enumerate(outs):
        for i in range(each):
            owner = table[2 * (index * each + i)]
            start = table[2 * (index * each + i) + 1]
            for which, source in enumerate(sources):

                @pl.when(owner == which)
                def _():
                    rows = pl.ds(pl.multiple_of(start * grain, grain), grain)
                    out[i * grain : (i + 1) * grain, :] = source[rows, :]


def collect(table, sources, grain, count, length):
    width = sources[0].shape[1]
    whole = lambda rows: pl.BlockSpec((rows, width), lambda i, s: (0, 0))
    return pl.pallas_call(
        partial(collect_kernel, grain, count),
        grid_spec=pltpu.PrefetchScalarGridSpec(
            num_scalar_prefetch=1,
            grid=(1,),
            in_specs=[whole(s.shape[0]) for s in sources],
            out_specs=[whole(length)] * count,
        ),
        out_shape=[jax.ShapeDtypeStruct((length, width), sources[0].dtype)] * count,
        compiler_params=pltpu.CompilerParams(vmem_limit_bytes=48 * 1024 * 1024),
        cost_estimate=pl.CostEstimate(flops=0, bytes_accessed=6 * count * length * width, transcendentals=0),
        name="collect_rows",
    )(table, *sources)


class Place:
    def __init__(self, micro, tree):
        self.columns = lax.axis_size("col")
        self.micro = micro
        self.parts = self.columns // micro
        self.tree = tree
        self.length = tree // self.columns
        self.grain = math.gcd(self.length, 128)
        me = lax.axis_index("col")
        self.quarter, self.part = me // self.parts, me % self.parts
        self.own = np.stack([own_rows(self.parts, part) for part in range(self.parts)])
        self.count = self.own.shape[1]

    def quarter_perm(self, shift):
        p = self.parts
        return [(c, ((c // p) ^ shift) * p + c % p) for c in range(self.columns)]

    def part_perm(self, shift):
        return [(c, c ^ shift) for c in range(self.columns)]

    def swap_quarters(self, value):
        groups = [
            [q * self.parts + part for q in range(self.micro)] for part in range(self.parts)
        ]
        return lax.all_to_all(value, "col", 0, 0, axis_index_groups=groups, tiled=True)

    def tree_sources(self, value):
        flat = (self.micro * self.length, value.shape[2])
        moved = [lax.ppermute(value, "col", self.part_perm(e)) for e in range(1, self.parts)]
        return [v.reshape(flat) for v in [value] + moved]

    def to_tree(self, sources):
        grain, each = self.grain, self.length // self.grain
        table = np.full((self.parts, self.tree // grain), -1, np.int32)
        for part in range(self.parts):
            table[part, self.own[part, ::grain] // grain] = np.arange(self.count // grain)
        mine = lax.dynamic_index_in_dim(jnp.asarray(table), self.part, 0, keepdims=False)
        e, rest = np.divmod(np.arange(self.tree // grain, dtype=np.int32), self.micro * each)
        quarter, inside = np.divmod(rest, each)
        chunk = (quarter * self.parts + (self.part ^ e)) * each + inside
        return spread(mine[chunk], sources, grain, self.count)

    def from_tree_sources(self, value):
        split = value.reshape(-1, self.grain, value.shape[1])
        moved = [lax.ppermute(split, "col", self.part_perm(e)) for e in range(1, self.parts)]
        return [value] + [v.reshape(value.shape) for v in moved]

    def from_tree_parts(self, sources):
        grain, each, parts = self.grain, self.length // self.grain, self.parts
        owner = np.zeros(self.tree // grain, np.int32)
        local = np.zeros(self.tree // grain, np.int32)
        for part in range(parts):
            owner[self.own[part, ::grain] // grain] = part
            local[self.own[part, ::grain] // grain] = np.arange(self.count // grain)
        quarter, inside = np.divmod(np.arange(self.micro * each, dtype=np.int32), each)
        chunk = (quarter * parts + self.part) * each + inside
        table = jnp.stack([jnp.asarray(owner)[chunk] ^ self.part, jnp.asarray(local)[chunk]], axis=1)
        (out,) = collect(table.reshape(-1), sources, grain, 1, self.micro * self.length)
        return out.reshape(self.micro, self.length, sources[0].shape[1])

    def masks(self, own_ids, parent_ids):
        parts = self.parts
        own = jnp.asarray(self.own, jnp.int32)
        mine = lax.dynamic_index_in_dim(own, self.part, 0, keepdims=False)
        trunk_rows = TRUNK // parts
        tiles = trunk_rows // QT
        trunk = []
        for tile in range(tiles):
            span = slice(tile * QT, (tile + 1) * QT)
            keys = jnp.concatenate(
                [
                    lax.dynamic_index_in_dim(own, self.part ^ e, 0, keepdims=False)[span]
                    for e in range(parts)
                ]
            )
            trunk.append(jnp.where(keys[None, :] <= mine[span][:, None], 0.0, -1e30))
        group = []
        groups = (TRUNK // 256) // parts
        places = jnp.arange(GROUP)
        for g in range(groups):
            start = TRUNK + (self.part * groups + g) * GROUP
            ids = lax.dynamic_slice_in_dim(own_ids, start, GROUP)
            parent = lax.dynamic_slice_in_dim(parent_ids, start, GROUP)
            seen = (places[None, :] <= places[:, None]) & (
                (ids[None, :] == 0) | (ids[None, :] == ids[:, None]) | (ids[None, :] == parent[:, None])
            )
            group.append(jnp.where(seen, 0.0, -1e30))
        return jnp.stack(trunk).astype(jnp.float32), jnp.stack(group).astype(jnp.float32)


BOTH = ("row", "col")
ROW_CUT = 144


def plain_gather(block):
    full = lax.all_gather(block, BOTH, axis=0, tiled=False)
    full = full.reshape(lax.axis_size("row"), lax.axis_size("col"), *block.shape)
    return full.transpose(0, 2, 1, 3).reshape(full.shape[0] * full.shape[2], full.shape[1] * full.shape[3])


def plain_scatter(grad):
    rows, cols = lax.axis_size("row"), lax.axis_size("col")
    blocks = grad.astype(jnp.bfloat16).reshape(rows, grad.shape[0] // rows, cols, grad.shape[1] // cols)
    blocks = blocks.transpose(0, 2, 1, 3).reshape(rows * cols, grad.shape[0] // rows, grad.shape[1] // cols)
    return lax.psum_scatter(blocks, BOTH, scatter_dimension=0, tiled=False).astype(jnp.float32)


def across(value, shift):
    return lax.ppermute(value, "row", [(r, r ^ shift) for r in range(lax.axis_size("row"))])


def row_gather(block):
    beside = across(block, 1)
    below = across(block, 2)
    return [block, beside, below, across(beside[:ROW_CUT], 2), across(below[ROW_CUT:], 1)]


def row_starts(rows):
    me = lax.axis_index("row")
    far = (me ^ 3) * rows
    return [me * rows, (me ^ 1) * rows, (me ^ 2) * rows, far, far + ROW_CUT]


def core_swap(place, value):
    return lax.ppermute(value, "col", place.part_perm(1))


def far_sums(own, swapped):
    f32, bf16 = jnp.float32, jnp.bfloat16
    add = lambda d, part: (own[d][part].astype(f32) + swapped[d][part].astype(f32)).astype(bf16)
    top, bottom = slice(0, ROW_CUT), slice(ROW_CUT, None)
    return add(3, top), add(3, bottom), add(1, bottom), add(2, top)


def far_sends(sums):
    return across(sums[0], 2), across(sums[1], 1), across(sums[2], 1), across(sums[3], 2)


def near_sums(own, swapped, received):
    f32 = jnp.float32
    beside = own[1][:ROW_CUT].astype(f32) + swapped[1][:ROW_CUT].astype(f32) + received[0].astype(f32)
    below = own[2][ROW_CUT:].astype(f32) + swapped[2][ROW_CUT:].astype(f32) + received[1].astype(f32)
    return beside.astype(jnp.bfloat16), below.astype(jnp.bfloat16)


def near_sends(sums):
    return across(sums[0], 1), across(sums[1], 2)


def row_total(own, swapped, received, last):
    f32 = jnp.float32
    base = own[0].astype(f32) + swapped[0].astype(f32)
    beside = jnp.concatenate([last[0], received[2]], axis=0).astype(f32)
    below = jnp.concatenate([received[3], last[1]], axis=0).astype(f32)
    return (base + beside + below).astype(jnp.bfloat16)


def pack_pair(w_up, w_down):
    main = w_up.shape[1] // 256 * 256
    down = w_down.T
    parts = []
    for start in range(0, main, FF_BLOCK):
        parts += [w_up[:, start : start + FF_BLOCK], down[:, start : start + FF_BLOCK]]
    return jnp.concatenate(parts + [w_up[:, main:], down[:, main:]], axis=1)


class QuickWeights:
    def __init__(self, place, w_qkv, w_out, w_up, w_down, padded):
        self.place, self.padded = place, padded
        self.rows = w_qkv.shape[0]
        self.cols = place.columns
        self.width = w_out.shape[1] * self.cols
        self.qkv_cols, self.out_cols, self.up_cols = w_qkv.shape[1], w_out.shape[1], w_up.shape[1]
        self.main = main = self.up_cols // 256 * 256
        self.rest = rest = self.up_cols - main
        self.role = place.part
        self.scalars = jnp.stack([self.role] + row_starts(self.rows)).astype(jnp.int32)
        self.pack = pack_pair(w_up, w_down)

    def start(self, w_qkv, w_out, value):
        full, rows, pack = start_exchange(
            jnp.concatenate([w_qkv, w_out], axis=1), self.pack, value, self.place.count
        )
        place = self.place
        pieces = [pack] + [
            lax.ppermute(pack, "col", place.quarter_perm(d)) for d in range(1, place.micro)
        ]
        self.own = in_order(place.quarter ^ jnp.arange(place.micro, dtype=jnp.int32), pieces)
        self.beside, self.below = across(self.own, 1), across(self.own, 2)
        self.far = (self.beside[:2], self.below[2:])
        mine = [self.own, self.beside, self.below, across(self.far[0], 2), across(self.far[1], 1)]
        self.pair = (mine, [core_swap(place, piece) for piece in mine])
        self.triple, self.out = assemble(full, self.width, self.padded, self.qkv_cols)
        return rows

    def end(self, triple_grad, out_grad, small, rows, shape, deps):
        blocks = divide(
            triple_grad, out_grad, self.width, self.padded, self.qkv_cols, self.out_cols, self.cols, 4
        )
        final, summed, tokens = end_exchange(blocks, small, rows, shape, deps)
        return final[:, : self.qkv_cols], final[:, self.qkv_cols :], summed, tokens

    def bias_order(self, bias):
        blocks = bias.reshape(self.place.micro, self.place.parts, self.up_cols).transpose(1, 0, 2)
        blocks = blocks.reshape(self.cols, self.up_cols)
        return jnp.concatenate([blocks[:, : self.main].reshape(-1), blocks[:, self.main :].reshape(-1)])

    def bias_back(self, grad):
        edge = self.cols * self.main
        blocks = jnp.concatenate(
            [grad[:edge].reshape(self.cols, self.main), grad[edge:].reshape(self.cols, self.rest)], axis=1
        )
        blocks = blocks.reshape(self.place.parts, self.place.micro, self.up_cols)
        return blocks.transpose(1, 0, 2).reshape(-1)

    def pair_final(self, parts):
        final = jnp.sum(parts.astype(jnp.float32), axis=0)
        main, rest = self.main, self.rest
        own = jnp.concatenate([final[:, :main], final[:, 2 * main : 2 * main + rest]], axis=1)
        far = jnp.concatenate([final[:, main : 2 * main], final[:, 2 * main + rest :]], axis=1)
        up = jnp.where(self.role == 0, own, far)
        down = jnp.where(self.role == 0, far, own)
        return up, down.T


class PlainWeights:
    def __init__(self, place, w_qkv, w_out, w_up, w_down, padded):
        self.place, self.padded = place, padded
        qkv, out = plain_gather(w_qkv), plain_gather(w_out)
        self.width = width = out.shape[1]
        pad = padded - width
        self.triple = jnp.pad(qkv.reshape(width, 3, width), ((0, 0), (0, 0), (0, pad))).reshape(
            width, 3 * padded
        )
        self.out = jnp.pad(out, ((0, pad), (0, pad)))
        self.rows, self.cols, self.up_cols = w_qkv.shape[0], place.columns, w_up.shape[1]
        self.main = self.up_cols // 256 * 256
        self.rest = self.up_cols - self.main
        full = lax.all_gather(pack_pair(w_up, w_down), BOTH, axis=0, tiled=False)
        full = full.reshape(lax.axis_size("row"), self.cols, self.rows, 2 * self.up_cols)
        self.pair = (full.transpose(1, 0, 2, 3).reshape(1, self.cols, width, 2 * self.up_cols),)
        self.scalars = jnp.zeros((2,), jnp.int32)

    def bias_order(self, bias):
        blocks = bias.reshape(self.cols, self.up_cols)
        return jnp.concatenate([blocks[:, : self.main].reshape(-1), blocks[:, self.main :].reshape(-1)])

    def bias_back(self, grad):
        edge = self.cols * self.main
        return jnp.concatenate(
            [grad[:edge].reshape(self.cols, self.main), grad[edge:].reshape(self.cols, self.rest)], axis=1
        ).reshape(-1)

    def natural(self, grad):
        edge = self.cols * self.main
        cut = lambda value: value.reshape(grad.shape[0], self.cols, -1)
        return jnp.concatenate([cut(grad[:, :edge]), cut(grad[:, edge:])], axis=2).reshape(grad.shape)

    def scatter_pair(self, mine, theirs):
        return plain_scatter(self.natural(mine)), plain_scatter(self.natural(theirs)).T

    def scatter_first(self, triple_grad, out_grad):
        width, padded = self.width, self.padded
        qkv = triple_grad.reshape(width, 3, padded)[:, :, :width].reshape(width, 3 * width)
        return plain_scatter(qkv), plain_scatter(out_grad[:, :width])


def cuts_of(pairs, count):
    edges = [round(i * pairs / count) for i in range(count + 1)]
    return list(zip(edges[:-1], edges[1:]))


def local(
    block_input, paths, ln1_gain, ln1_bias, w_qkv, q_bias, v_bias, w_out, out_bias,
    ln2_gain, ln2_bias, w_up, up_bias, w_down, down_bias, cotangent,
):
    micro, _, width = block_input.shape
    place = Place(micro, paths.shape[2])
    parts = place.parts
    heads = width // HEAD_DIM
    padded = (heads + 1) // 2 * 128
    pairs = padded // 128
    pad = padded - width
    own_trunk = TRUNK // parts
    f32, bf16 = jnp.float32, jnp.bfloat16

    quick = lax.axis_size("row") == 4 and parts == 2 and w_qkv.shape[0] == 272
    if quick:
        weights = QuickWeights(place, w_qkv, w_out, w_up, w_down, padded)
        rows_low = weights.start(w_qkv, w_out, block_input)
    else:
        weights = PlainWeights(place, w_qkv, w_out, w_up, w_down, padded)
        rows_low = place.to_tree(place.tree_sources(place.swap_quarters(block_input)))
    rows_in = rows_low.astype(f32)

    own_ids = lax.dynamic_index_in_dim(paths[0], place.quarter, 0, keepdims=False)
    parent_ids = lax.dynamic_index_in_dim(paths[1], place.quarter, 0, keepdims=False)
    mask_trunk, mask_group = place.masks(own_ids, parent_ids)

    seed_moved = place.swap_quarters(after(cotangent, weights.own) if quick else cotangent)

    q_scale = HEAD_DIM**-0.5 * LOG2E
    triple_bias = jnp.concatenate(
        [jnp.pad(q_bias * q_scale, (0, pad)), jnp.zeros((padded,), f32), jnp.pad(v_bias, (0, pad))]
    )
    triple_scale = jnp.concatenate([jnp.full((padded,), q_scale, f32), jnp.ones((2 * padded,), f32)])
    first = layer_norm(rows_in, ln1_gain, ln1_bias).astype(bf16)
    triple = (dot_nn(first, weights.triple) * triple_scale + triple_bias).astype(bf16)
    shared = triple[:own_trunk, padded:]
    others = jnp.concatenate(
        [lax.ppermute(shared, "col", place.part_perm(e)) for e in range(1, parts)], axis=0
    )
    cuts = [round(pairs * part / 9) for part in (0, 6, 8, 9)]
    before, gates = (), ((), (), ())
    if quick:
        gates = ((weights.own,), weights.far, tuple(weights.pair[0][3:]))
    for start, stop, deps in zip(cuts[:-1], cuts[1:], gates):
        before = attention_forward(
            parts, heads, triple, others, mask_trunk, mask_group, start, stop, before, deps
        )
    mixed, lse = before
    seed_rows = place.to_tree(place.tree_sources(after(seed_moved, mixed)))
    middle, second = project_out(mixed, rows_low, weights.out, out_bias, ln2_gain, ln2_bias)
    outs = 4 if quick else 1
    lowered, second_grad, up_bias_grad, *pair_grads = feed_forward(
        weights.scalars, weights.pair, second, seed_rows, weights.bias_order(up_bias), outs
    )
    pair_mine, pair_theirs = pair_grads[:outs], pair_grads[outs:]
    up_bias_grad = weights.bias_back(up_bias_grad.reshape(-1))
    far = ()
    if quick:
        pair_swapped = {d: core_swap(place, pair_theirs[d]) for d in (3, 1, 2, 0)}
        far = far_sums(pair_mine, pair_swapped)
        received = far_sends(far)
    result, middle_grad, mixed_grad, sums, out_padded = middle_back(
        second_grad, lowered, middle, seed_rows, mixed, weights.out, ln2_gain, down_bias, far
    )
    out_bias_grad, gain_two, shift_two, down_bias_grad = sums[0], sums[1], sums[2], sums[3]

    turned = jnp.swapaxes(mask_trunk, 1, 2), jnp.swapaxes(mask_group, 1, 2)
    result_sources = place.from_tree_sources(result)
    result_parts = place.from_tree_parts(result_sources)
    result_out = place.swap_quarters(result_parts)
    cut = 5 * pairs // 9
    deps = (result_parts,)
    if quick:
        near = near_sums(pair_mine, pair_swapped, received)
        last = near_sends(near)
        deps += near
    inputs = parts, heads, triple, others, mixed, mixed_grad, lse, *turned
    grads = attention_backward(*inputs, 0, cut, (), deps)
    deps = ()
    if quick:
        last = after(last[0], grads[0]), last[1]
        total = row_total(pair_mine, pair_swapped, received, last)
        deps = (total,)
    grads = attention_backward(*inputs, cut, pairs, grads, deps)
    finish_deps, first_deps = (), ()
    if quick:
        blocks = pair_blocks(
            place.part.reshape(1).astype(jnp.int32), total, core_swap(place, total), weights.main, weights.rest
        )
        pair_parts = place.swap_quarters(blocks)
        finish_deps = (blocks,)
    else:
        up_grad, down_grad = weights.scatter_pair(pair_mine[0], pair_theirs[0])
    dq, dk, dv, dko, dvo = grads
    other_k, other_v = (
        jnp.concatenate(
            [
                lax.ppermute(part[(e - 1) * own_trunk : e * own_trunk], "col", place.part_perm(e))
                for e in range(1, parts)
            ],
            axis=0,
        )
        for part in (dko, dvo)
    )
    triple_grad, triple_sums = finish_gradients(own_trunk, dq, dk, dv, other_k, other_v, finish_deps)
    q_bias_grad = triple_sums[0, :width]
    v_bias_grad = triple_sums[0, 2 * padded : 2 * padded + width]
    input_grad, sums = first_back(
        triple_grad, rows_low, middle_grad, weights.triple, ln1_gain, first_deps
    )
    gain_one, shift_one = sums[0], sums[1]
    triple_weight_grad = dot_tn(first, triple_grad).astype(bf16)
    small = [
        gain_one, shift_one, q_bias_grad, v_bias_grad, out_bias_grad, gain_two, shift_two, up_bias_grad,
        down_bias_grad,
    ]
    if quick:
        up_grad, down_grad = weights.pair_final(pair_parts)
        flat = jnp.concatenate(small)
        flat = jnp.pad(flat, (0, -flat.shape[0] % 1024)).reshape(-1, 128)
        qkv_grad, out_grad, flat, input_grad_out = weights.end(
            triple_weight_grad, out_padded, flat, input_grad, block_input.shape, (up_grad, down_grad)
        )
        edges = np.cumsum([0] + [v.shape[0] for v in small])
        flat = flat.reshape(-1)
        small = [flat[low:high] for low, high in zip(edges[:-1], edges[1:])]
    else:
        qkv_grad, out_grad = weights.scatter_first(triple_weight_grad, out_padded)
        small = lax.psum(small, BOTH)
        input_grad_out = place.swap_quarters(
            place.from_tree_parts(place.from_tree_sources(input_grad))
        )
    return (
        result_out, input_grad_out, small[0], small[1], qkv_grad, small[2], small[3],
        out_grad, small[4], small[5], small[6], up_grad, small[7], down_grad, small[8],
    )


def solution(mesh):
    rows = P(None, BOTH, None)
    placed = (
        rows, P(None, None, "row"), P(), P(), P("row", "col"), P(), P(), P("row", "col"), P(),
        P(), P(), P("row", "col"), P(), P("col", "row"), P(), rows,
    )
    out = (
        rows, rows, P(), P(), P("row", "col"), P(), P(), P("row", "col"), P(),
        P(), P(), P("row", "col"), P(), P("col", "row"), P(),
    )
    return jax.shard_map(local, mesh=mesh, in_specs=placed, out_specs=out, check_vma=False)
```

```python
import math
from functools import partial

import jax
import jax.numpy as jnp
import numpy as np
from jax import lax
from jax.experimental import pallas as pl
from jax.experimental.pallas import tpu as pltpu
from jax.sharding import PartitionSpec as P

HEAD_DIM = 64
TRUNK = 1024
GROUP = 384
QT = 256
LOG2E = 1.4426950408889634
LN2 = 0.6931471805599453


def dot_nn(a, b):
    return jnp.dot(a, b, preferred_element_type=jnp.float32)


def dot_nt(a, b):
    return lax.dot_general(a, b, (((1,), (1,)), ((), ())), preferred_element_type=jnp.float32)


def dot_tn(a, b):
    return lax.dot_general(a, b, (((0,), (0,)), ((), ())), preferred_element_type=jnp.float32)


def lane_masks(head):
    lane = lax.broadcasted_iota(jnp.int32, (1, 128), 1)
    inside = (lane // HEAD_DIM) == head
    return inside, inside.astype(jnp.float32).astype(jnp.bfloat16), lane % HEAD_DIM


def fill_trunk(parts, own_ref, other_ref, out_ref):
    own = TRUNK // parts
    for tile in range(own // QT):
        for part in range(parts):
            rows = (
                own_ref[tile * QT : (tile + 1) * QT, :]
                if part == 0
                else other_ref[(part - 1) * own + tile * QT : (part - 1) * own + (tile + 1) * QT, :]
            )
            start = (tile * parts + part) * QT
            out_ref[start : start + QT, :] = rows


def fwd_kernel(parts, heads, start, extra, q_ref, k_ref, v_ref, ko_ref, vo_ref, mt_ref, mg_ref, *refs):
    o_ref, lse_ref, kt, vt, va = refs[extra:]
    pair = start + pl.program_id(0)
    own = TRUNK // parts
    tiles = own // QT
    groups = (TRUNK // 256) // parts
    fill_trunk(parts, k_ref, ko_ref, kt)
    fill_trunk(parts, v_ref, vo_ref, vt)
    o_ref[...] = jnp.zeros_like(o_ref)
    lse_ref[...] = jnp.zeros_like(lse_ref)

    def finish(rows, top, total, inside):
        turned = pltpu.roll(total, HEAD_DIM, 1)
        o_ref[rows, :] += jnp.where(inside, total / turned, 0.0).astype(jnp.bfloat16)
        lse_ref[rows, :] += jnp.where(inside, 0.0, top + jnp.log2(total))

    def head_body(head):
        inside, hm, _ = lane_masks(head)
        rest = 1 - hm
        va[...] = vt[...] * hm + rest
        for tile in range(tiles):
            rows = pl.ds(tile * QT, QT)
            q = q_ref[rows, :] * hm
            near = tile * parts * QT
            s_near = dot_nt(q, kt[near : near + parts * QT, :]) + mt_ref[tile]
            top = jnp.max(s_near, axis=1, keepdims=True)
            if tile > 0:
                s_far = dot_nt(q, kt[:near, :])
                top = jnp.maximum(top, jnp.max(s_far, axis=1, keepdims=True))
            p_near = jnp.exp2(s_near - top).astype(jnp.bfloat16)
            total = dot_nn(p_near, va[near : near + parts * QT, :])
            if tile > 0:
                total += dot_nn(jnp.exp2(s_far - top).astype(jnp.bfloat16), va[:near, :])
            finish(rows, top, total, inside)

        for group in range(groups):
            rows = pl.ds(own + group * GROUP, GROUP)
            q = q_ref[rows, :] * hm
            s_near = dot_nt(q, k_ref[rows, :]) + mg_ref[group]
            s_far = dot_nt(q, kt[...])
            top = jnp.maximum(
                jnp.max(s_near, axis=1, keepdims=True), jnp.max(s_far, axis=1, keepdims=True)
            )
            near = v_ref[rows, :] * hm + rest
            total = dot_nn(jnp.exp2(s_near - top).astype(jnp.bfloat16), near)
            total += dot_nn(jnp.exp2(s_far - top).astype(jnp.bfloat16), va[...])
            finish(rows, top, total, inside)

    head_body(0)
    pl.when(2 * pair + 1 < heads)(lambda: head_body(1))


def attention_forward(parts, heads, triple, others, mask_trunk, mask_group, start, stop, before=(), deps=()):
    fixed = 7
    aliases = {fixed + index: index for index in range(len(before))}
    deps = tuple(before) + tuple(deps)
    rows = triple.shape[0]
    pairs = triple.shape[1] // (3 * 128)
    extra = others.shape[0]
    block = lambda count, shift: pl.BlockSpec((count, 128), lambda i: (0, i + shift))
    whole = lambda shape: pl.BlockSpec(shape, lambda i: (0,) * len(shape))
    return pl.pallas_call(
        partial(fwd_kernel, parts, heads, start, len(deps)),
        grid=(stop - start,),
        in_specs=[
            block(rows, start),
            block(rows, start + pairs),
            block(rows, start + 2 * pairs),
            block(extra, start),
            block(extra, start + pairs),
            whole(mask_trunk.shape),
            whole(mask_group.shape),
        ]
        + [pl.BlockSpec(memory_space=pl.ANY)] * len(deps),
        out_specs=[block(rows, start)] * 2,
        input_output_aliases=aliases,
        out_shape=[
            jax.ShapeDtypeStruct((rows, pairs * 128), jnp.bfloat16),
            jax.ShapeDtypeStruct((rows, pairs * 128), jnp.float32),
        ],
        scratch_shapes=[
            pltpu.VMEM((TRUNK, 128), jnp.bfloat16),
            pltpu.VMEM((TRUNK, 128), jnp.bfloat16),
            pltpu.VMEM((TRUNK, 128), jnp.bfloat16),
        ],
        compiler_params=pltpu.CompilerParams(vmem_limit_bytes=48 * 1024 * 1024),
        cost_estimate=pl.CostEstimate(
            flops=(stop - start) * rows * 5_200_000, bytes_accessed=rows * pairs * 2000, transcendentals=0
        ),
        name="attention_forward",
    )(triple, triple, triple, others, others, mask_trunk, mask_group, *deps)


def split_three(value, place, outside):
    high = value.astype(jnp.bfloat16)
    left = value - high.astype(jnp.float32)
    middle = left.astype(jnp.bfloat16)
    low = (left - middle.astype(jnp.float32)).astype(jnp.bfloat16)
    high, middle, low = (v.astype(jnp.float32) for v in (high, middle, low))
    picked = jnp.where(place == 0, high, jnp.where(place == 1, middle, jnp.where(place == 2, low, 0.0)))
    return jnp.where(outside, picked, 0.0).astype(jnp.bfloat16)


def bwd_kernel(
    parts, heads, start, extra, q_ref, k_ref, v_ref, ko_ref, vo_ref, o_ref, do_ref, lse_ref, mt_ref, mg_ref,
    *refs,
):
    dq_ref, dk_ref, dv_ref, dko_ref, dvo_ref = refs[extra : extra + 5]
    kt, vt, ka, va, qa, da, qm, dm, dkt, dvt, dkg, dvg, dqs, kat = refs[extra + 5 :]
    pair = start + pl.program_id(0)
    own = TRUNK // parts
    tiles = own // QT
    groups = (TRUNK // 256) // parts
    rows_all = own + groups * GROUP
    fill_trunk(parts, k_ref, ko_ref, kt)
    fill_trunk(parts, v_ref, vo_ref, vt)
    dkt[...] = jnp.zeros_like(dkt)
    dvt[...] = jnp.zeros_like(dvt)
    dkg[...] = jnp.zeros_like(dkg)
    dvg[...] = jnp.zeros_like(dvg)
    dqs[...] = jnp.zeros_like(dqs)

    def head_body(head):
        inside, hm, place = lane_masks(head)
        rest = 1 - hm
        outside = jnp.logical_not(inside)
        ka[:TRUNK, :] = kt[...] * hm + rest
        va[:TRUNK, :] = vt[...] * hm + rest
        ka[TRUNK:, :] = k_ref[own:, :] * hm + rest
        va[TRUNK:, :] = v_ref[own:, :] * hm + rest

        kat[:, :TRUNK] = (kt[...] * hm).T
        kat[:, TRUNK:] = (k_ref[own:, :] * hm).T

        part = 256 if rows_all % 256 == 0 else 128
        for index in range(rows_all // part):
            rows = pl.ds(index * part, part)
            q = q_ref[rows, :] * hm
            d = do_ref[rows, :] * hm
            qm[rows, :] = q
            dm[rows, :] = d
            qa[rows, :] = q - split_three(lse_ref[rows, :], place, outside)
            delta = jnp.sum(
                d.astype(jnp.float32) * o_ref[rows, :].astype(jnp.float32), axis=1, keepdims=True
            )
            da[rows, :] = d - split_three(jnp.broadcast_to(delta, (part, 128)), place, outside)

        def step(rows, keys, mask, keep, dk, dv):
            st = dot_nt(ka[keys, :], qa[rows, :])
            if mask is not None:
                st = st + mask
            p = jnp.exp2(st)
            dp = dot_nt(va[keys, :], da[rows, :])
            ds = (p * dp).astype(jnp.bfloat16)
            dv[keep, :] += dot_nn(p.astype(jnp.bfloat16), dm[rows, :])
            dk[keep, :] += dot_nn(ds, qm[rows, :])
            dqs[:, rows] += dot_nn(kat[:, keys], ds)

        span = parts * QT
        for tile in range(tiles):
            rows = pl.ds(tile * QT, QT)
            for near in range(tile + 1):
                keys = pl.ds(near * span, span)
                step(rows, keys, mt_ref[tile] if near == tile else None, keys, dkt, dvt)
        step(pl.ds(own, groups * GROUP), pl.ds(0, TRUNK), None, pl.ds(0, TRUNK), dkt, dvt)
        for group in range(groups):
            step(
                pl.ds(own + group * GROUP, GROUP), pl.ds(TRUNK + group * GROUP, GROUP), mg_ref[group],
                pl.ds(group * GROUP, GROUP), dkg, dvg,
            )

    head_body(0)
    pl.when(2 * pair + 1 < heads)(lambda: head_body(1))
    dq_ref[...] = (dqs[...].T * HEAD_DIM**-0.5).astype(jnp.bfloat16)
    dk_ref[own:, :] = (dkg[...] * LN2).astype(jnp.bfloat16)
    dv_ref[own:, :] = dvg[...].astype(jnp.bfloat16)
    for tile in range(tiles):
        for part in range(parts):
            source = pl.ds((tile * parts + part) * QT, QT)
            if part == 0:
                dk_ref[tile * QT : (tile + 1) * QT, :] = (dkt[source, :] * LN2).astype(jnp.bfloat16)
                dv_ref[tile * QT : (tile + 1) * QT, :] = dvt[source, :].astype(jnp.bfloat16)
            else:
                start = (part - 1) * own + tile * QT
                dko_ref[start : start + QT, :] = (dkt[source, :] * LN2).astype(jnp.bfloat16)
                dvo_ref[start : start + QT, :] = dvt[source, :].astype(jnp.bfloat16)


def attention_backward(
    parts, heads, triple, others, mixed, mixed_grad, lse, mask_trunk, mask_group, start, stop, before=(), deps=()
):
    fixed = 10
    aliases = {fixed + index: index for index in range(len(before))}
    deps = tuple(before) + tuple(deps)
    rows = triple.shape[0]
    pairs = triple.shape[1] // (3 * 128)
    extra = others.shape[0]
    block = lambda count, shift: pl.BlockSpec((count, 128), lambda i: (0, i + shift))
    whole = lambda shape: pl.BlockSpec(shape, lambda i: (0,) * len(shape))
    near = rows - TRUNK // parts
    return pl.pallas_call(
        partial(bwd_kernel, parts, heads, start, len(deps)),
        grid=(stop - start,),
        in_specs=[
            block(rows, start),
            block(rows, start + pairs),
            block(rows, start + 2 * pairs),
            block(extra, start),
            block(extra, start + pairs),
            block(rows, start),
            block(rows, start),
            block(rows, start),
            whole(mask_trunk.shape),
            whole(mask_group.shape),
        ]
        + [pl.BlockSpec(memory_space=pl.ANY)] * len(deps),
        out_specs=[block(rows, start)] * 3 + [block(extra, start)] * 2,
        input_output_aliases=aliases,
        out_shape=[
            jax.ShapeDtypeStruct((rows, pairs * 128), jnp.bfloat16),
            jax.ShapeDtypeStruct((rows, pairs * 128), jnp.bfloat16),
            jax.ShapeDtypeStruct((rows, pairs * 128), jnp.bfloat16),
            jax.ShapeDtypeStruct((extra, pairs * 128), jnp.bfloat16),
            jax.ShapeDtypeStruct((extra, pairs * 128), jnp.bfloat16),
        ],
        scratch_shapes=[
            pltpu.VMEM((TRUNK, 128), jnp.bfloat16),
            pltpu.VMEM((TRUNK, 128), jnp.bfloat16),
            pltpu.VMEM((TRUNK + near, 128), jnp.bfloat16),
            pltpu.VMEM((TRUNK + near, 128), jnp.bfloat16),
            pltpu.VMEM((rows, 128), jnp.bfloat16),
            pltpu.VMEM((rows, 128), jnp.bfloat16),
            pltpu.VMEM((rows, 128), jnp.bfloat16),
            pltpu.VMEM((rows, 128), jnp.bfloat16),
            pltpu.VMEM((TRUNK, 128), jnp.float32),
            pltpu.VMEM((TRUNK, 128), jnp.float32),
            pltpu.VMEM((near, 128), jnp.float32),
            pltpu.VMEM((near, 128), jnp.float32),
            pltpu.VMEM((128, rows), jnp.float32),
            pltpu.VMEM((128, TRUNK + near), jnp.bfloat16),
        ],
        compiler_params=pltpu.CompilerParams(vmem_limit_bytes=56 * 1024 * 1024),
        cost_estimate=pl.CostEstimate(
            flops=(stop - start) * rows * 1_000_000, bytes_accessed=rows * pairs * 4000, transcendentals=0
        ),
        name="attention_backward",
    )(triple, triple, triple, others, others, mixed, mixed_grad, lse, mask_trunk, mask_group, *deps)


def normal_share(value):
    size = jnp.abs(value)
    turn = 1.0 / (1.0 + 0.23164189 * size)
    bell = jnp.exp2(value * value * -0.7213475204444817)
    poly = (((0.530702714 * turn - 0.726576013) * turn + 0.710706870) * turn - 0.142248368) * turn
    tail = (poly + 0.127414796) * turn * bell
    return jnp.where(value < 0, tail, 1.0 - tail), bell


FF_BLOCK = 256
ROW_CHUNK = 640


def join_tails(slabs, rows, up, down):
    rest = FF_BLOCK // len(slabs)
    for shift, target in ((0, up), (rest, down)):
        joined = jnp.concatenate([slab[:, shift : shift + rest] for slab in slabs], axis=1)
        target[rows, :] = joined.astype(jnp.bfloat16)


def plain_load(step, is_rest, scalars, refs, up, down):
    main, tails = refs

    @pl.when(jnp.logical_not(is_rest))
    def _():
        up[...] = main[0, 0, :, :FF_BLOCK]
        down[...] = main[0, 0, :, FF_BLOCK:]

    @pl.when(is_rest)
    def _():
        slabs = [tails[0, c].astype(jnp.float32) for c in range(tails.shape[1])]
        join_tails(slabs, slice(None), up, down)


def plain_specs(main):
    last = main.shape[1] - 1
    return [
        pl.BlockSpec((1, 1, main.shape[2], 2 * FF_BLOCK), lambda j, s: (0, jnp.minimum(j, last), 0, 0)),
        pl.BlockSpec(main.shape[:3] + (128,), lambda j, s: (0, 0, 0, 4)),
    ], [main, main]


def quick_load(step, is_rest, scalars, refs, up, down):
    role = scalars[0]
    bodies, tails = (refs[:5], refs[5:10]), (refs[10:15], refs[15:20])
    height = bodies[0][0].shape[1]
    spot = lambda d: pl.ds(pl.multiple_of(scalars[1 + d], 16), height)
    low_quarter = (step % 8) // 2 < 2

    def place(pieces):
        def put(d, piece):
            up[spot(d), :] = piece[0, :, :FF_BLOCK]
            down[spot(d), :] = piece[0, :, FF_BLOCK:]

        for d in range(3):
            put(d, pieces[d])
        pl.when(low_quarter)(lambda: put(3, pieces[3]))
        pl.when(jnp.logical_not(low_quarter))(lambda: put(3, pieces[4]))

    use_mine = jnp.logical_and(step // 8 == role, jnp.logical_not(is_rest))
    use_theirs = jnp.logical_and(step // 8 == 1 - role, jnp.logical_not(is_rest))
    pl.when(use_mine)(lambda: place(bodies[0]))
    pl.when(use_theirs)(lambda: place(bodies[1]))

    def rest(order):
        for d in range(4):
            slabs = []
            for which in order:
                pieces = tails[which]
                for q in range(4):
                    piece = pieces[d][q] if d < 3 else (pieces[3][q] if q < 2 else pieces[4][q - 2])
                    slabs.append(piece.astype(jnp.float32))
            join_tails(slabs, spot(d), up, down)

    pl.when(jnp.logical_and(is_rest, role == 0))(lambda: rest((0, 1)))
    pl.when(jnp.logical_and(is_rest, role != 0))(lambda: rest((1, 0)))


def quick_specs(mine, theirs):
    def body(shape, which, low, high):
        def index(j, s):
            turn = jnp.clip(j - 8 * (s[0] if which == 0 else 1 - s[0]), 0, 7)
            return (jnp.clip(turn // 2, low, high) - low, 0, turn % 2)

        return pl.BlockSpec((1, shape[1], 2 * FF_BLOCK), index)

    spans = ((0, 3), (0, 3), (0, 3), (0, 1), (2, 3))
    bodies = [
        body(piece.shape, which, *span)
        for which, pieces in enumerate((mine, theirs))
        for piece, span in zip(pieces, spans)
    ]
    tails = [
        pl.BlockSpec(piece.shape[:2] + (128,), lambda j, s: (0, 0, 8))
        for pieces in (mine, theirs)
        for piece in pieces
    ]
    arrays = list(mine) + list(theirs)
    return bodies + tails, arrays * 2


def ffn_kernel(load, held, outs, chunk, scalars, *refs):
    weights, refs = refs[:held], refs[held:]
    second, seed, bias = refs[:3]
    lowered, second_grad, bias_grad = refs[3:6]
    mine_grads, theirs_grads = refs[6 : 6 + outs], refs[6 + outs : 6 + 2 * outs]
    up, down, act, wide, up_grad, down_grad, second_t, seed_t = refs[6 + 2 * outs :]
    step = pl.program_id(0)
    role = scalars[0]
    load(step, step == pl.num_programs(0) - 1, scalars, weights, up, down)

    @pl.when(step == 0)
    def _():
        lowered[...] = jnp.zeros_like(lowered)
        second_grad[...] = jnp.zeros_like(second_grad)
        for start in range(0, second.shape[0], 128):
            rows = pl.ds(start, 128)
            second_t[:, rows] = second[rows, :].T
            seed_t[:, rows] = seed[rows, :].T

    total = jnp.zeros((1, FF_BLOCK), jnp.float32)
    for start in range(0, second.shape[0], chunk):
        rows = pl.ds(start, chunk)
        wide_in = dot_nn(second[rows, :], up[...]) + bias[...]
        hidden = dot_nn(seed[rows, :], down[...])
        share, bell = normal_share(wide_in)
        act_now = (wide_in * share).astype(jnp.bfloat16)
        slope = share + wide_in * (bell * 0.3989422804014327)
        wide_now = (hidden * slope).astype(jnp.bfloat16)
        total += jnp.sum(wide_now.astype(jnp.float32), axis=0, keepdims=True)
        act[rows, :] = act_now
        wide[rows, :] = wide_now
        lowered[rows, :] += dot_nt(act_now, down[...])
        second_grad[rows, :] += dot_nt(wide_now, up[...])
    bias_grad[...] = total
    up_grad[...] = dot_nn(second_t[...], wide[...]).astype(jnp.bfloat16)
    down_grad[...] = dot_nn(seed_t[...], act[...]).astype(jnp.bfloat16)

    def deliver(first_grad, second_grad):
        for index in range(outs):
            size = mine_grads[index].shape[0]
            rows = pl.ds(pl.multiple_of(scalars[1 + index], 16), size)
            mine_grads[index][...] = first_grad[rows, :]
            theirs_grads[index][...] = second_grad[rows, :]

    @pl.when(role == 0)
    def _():
        deliver(up_grad, down_grad)

    @pl.when(role != 0)
    def _():
        deliver(down_grad, up_grad)


def feed_forward(scalars, pair, second, seed, bias, outs):
    rows, width = second.shape
    hidden = bias.shape[0]
    quick = len(pair) == 2
    specs, arrays = quick_specs(*pair) if quick else plain_specs(*pair)
    load = quick_load if quick else plain_load
    whole = lambda shape: pl.BlockSpec(shape, lambda j, s: (0, 0))
    grad_spec = pl.BlockSpec((width // outs, FF_BLOCK), lambda j, s: (0, j))
    grad_shape = jax.ShapeDtypeStruct((width // outs, hidden), jnp.bfloat16)
    line = pl.BlockSpec((1, FF_BLOCK), lambda j, s: (0, j))
    chunk = ROW_CHUNK if rows % ROW_CHUNK == 0 else rows // 2
    return pl.pallas_call(
        partial(ffn_kernel, load, len(specs), outs, chunk),
        grid_spec=pltpu.PrefetchScalarGridSpec(
            num_scalar_prefetch=1,
            grid=(hidden // FF_BLOCK,),
            in_specs=specs + [
                whole((rows, width)), whole((rows, width)), line,
            ],
            out_specs=[whole((rows, width)), whole((rows, width)), line] + [grad_spec] * (2 * outs),
            scratch_shapes=[
                pltpu.VMEM((width, FF_BLOCK), jnp.bfloat16),
                pltpu.VMEM((width, FF_BLOCK), jnp.bfloat16),
                pltpu.VMEM((rows, FF_BLOCK), jnp.bfloat16),
                pltpu.VMEM((rows, FF_BLOCK), jnp.bfloat16),
                pltpu.VMEM((width, FF_BLOCK), jnp.bfloat16),
                pltpu.VMEM((width, FF_BLOCK), jnp.bfloat16),
                pltpu.VMEM((width, rows), jnp.bfloat16),
                pltpu.VMEM((width, rows), jnp.bfloat16),
            ],
        ),
        out_shape=[
            jax.ShapeDtypeStruct((rows, width), jnp.float32),
            jax.ShapeDtypeStruct((rows, width), jnp.float32),
            jax.ShapeDtypeStruct((1, hidden), jnp.float32),
        ]
        + [grad_shape] * (2 * outs),
        compiler_params=pltpu.CompilerParams(vmem_limit_bytes=60 * 1024 * 1024),
        cost_estimate=pl.CostEstimate(
            flops=24 * rows * width * hidden, bytes_accessed=8 * width * hidden + 20 * rows * width,
            transcendentals=rows * hidden,
        ),
        name="feed_forward",
    )(scalars, *arrays, second, seed, bias.reshape(1, hidden))


MESH = pl.DeviceIdType.MESH
HOLD = pl.BlockSpec(memory_space=pl.ANY)


def greet(peers):
    barrier = pltpu.get_barrier_semaphore()
    for peer in peers:
        pl.semaphore_signal(barrier, inc=1, device_id=peer, device_id_type=MESH)
    pl.semaphore_wait(barrier, len(peers))


def remote(source, target, send, receive, device):
    return pltpu.make_async_remote_copy(
        src_ref=source, dst_ref=target, send_sem=send, recv_sem=receive,
        device_id=device, device_id_type=MESH,
    )


def chunk_home(chunk):
    block = chunk // 2
    turn = block % 4
    in_trunk = chunk < 16
    owner = jnp.where(in_trunk, ((turn + 1) // 2) % 2, (chunk - 16) // 12)
    spot = jnp.where(
        in_trunk, 2 * (2 * (block // 4) + turn // 2) + chunk % 2, 8 + (chunk - 16) % 12
    )
    return owner, spot


def start_kernel(grain, pack, later_pack, value, full, rows, later_out, z_send, z_recv, r_send, r_recv, c_send, c_recv,
                 x_send, x_recv, own_sem, later_sem):
    row, col = lax.axis_index("row"), lax.axis_index("col")
    z, core = col // 2, col % 2
    at = lambda r, c: (r, c)
    peers = [at(row, (col + shift) % 8) for shift in range(1, 8)] + [at(row ^ 1, col), at(row ^ 2, col)]
    greet(peers)
    later_copy = pltpu.make_async_copy(later_pack, later_out, later_sem)
    later_copy.start()
    here = full.at[core, row, z]
    own = pltpu.make_async_copy(pack, here, own_sem)
    own.start()
    sends = []
    for d in range(1, 4):
        copy = remote(pack, here, z_send.at[d - 1], z_recv.at[d - 1], at(row, (z ^ d) * 2 + core))
        copy.start()
        sends.append(copy)
    own.wait()
    for copy in sends:
        copy.wait_recv()
    later = []

    def pass_on(index, ref, device, send=r_send, receive=r_recv):
        copy = remote(ref, ref, send.at[index], receive.at[index], device)
        copy.start()
        later.append(copy)
        return copy

    beside = pass_on(0, full.at[core, row], at(row ^ 1, col))
    below = pass_on(1, full.at[core, row], at(row ^ 2, col))
    swaps = [pass_on(0, full.at[core, row], at(row, col ^ 1), c_send, c_recv)]

    each = value.shape[1] // grain

    def each_chunk(act_remote, act_own):
        for m in range(4):
            for i in range(each):
                owner, spot = chunk_home(col * each + i)
                source = value.at[m, pl.ds(i * grain, grain), :]
                target = rows.at[pl.ds(pl.multiple_of(spot * grain, grain), grain), :]
                same = jnp.logical_and(z == m, owner == core)
                index = m * each + i

                @pl.when(jnp.logical_not(same))
                def _():
                    act_remote(
                        remote(source, target, x_send.at[index], x_recv, at(row, 2 * m + owner))
                    )

                if act_own:

                    @pl.when(same)
                    def _():
                        pltpu.make_async_copy(source, target, x_recv).start()

    each_chunk(lambda copy: copy.start(), True)
    beside.wait_recv()
    far_a = pass_on(2, full.at[core, row ^ 1, pl.ds(0, 2)], at(row ^ 2, col))
    swaps.append(pass_on(1, full.at[core, row ^ 1], at(row, col ^ 1), c_send, c_recv))
    below.wait_recv()
    far_b = pass_on(3, full.at[core, row ^ 2, pl.ds(2, 2)], at(row ^ 1, col))
    swaps.append(pass_on(2, full.at[core, row ^ 2], at(row, col ^ 1), c_send, c_recv))
    far_a.wait_recv()
    far_b.wait_recv()
    swaps.append(pass_on(3, full.at[core, row ^ 3], at(row, col ^ 1), c_send, c_recv))
    for copy in swaps:
        copy.wait_recv()
    pltpu.make_async_copy(rows, rows, x_recv).wait()
    later_copy.wait()
    for copy in sends + later:
        copy.wait_send()
    each_chunk(lambda copy: copy.wait_send(), False)


def start_exchange(pack, later_pack, value, count):
    grain = 64
    height, lanes = pack.shape
    copies = 4 * (value.shape[1] // grain)
    dma = lambda n: pltpu.SemaphoreType.DMA((n,))
    return pl.pallas_call(
        partial(start_kernel, grain),
        in_specs=[HOLD] * 3,
        out_specs=[HOLD] * 3,
        out_shape=[
            jax.ShapeDtypeStruct((2, 4, 4, height, lanes), pack.dtype),
            jax.ShapeDtypeStruct((count, value.shape[2]), value.dtype),
            jax.ShapeDtypeStruct(later_pack.shape, later_pack.dtype),
        ],
        scratch_shapes=[
            dma(3), dma(3), dma(4), dma(4), dma(4), dma(4), dma(copies),
            pltpu.SemaphoreType.DMA, pltpu.SemaphoreType.DMA, pltpu.SemaphoreType.DMA,
        ],
        compiler_params=pltpu.CompilerParams(collective_id=0, has_side_effects=True),
        cost_estimate=pl.CostEstimate(flops=100_000_000_000, bytes_accessed=0, transcendentals=0),
        name="start_exchange",
    )(pack, later_pack, value)


def end_kernel(
    grain, grads, small, rows, *refs,
):
    final, small_out, tokens, mine, swapped, far, beside, below, tail, small_col, small_row, part = refs[-26:-14]
    own_sem, c_send, c_recv, r_send, r_recv, z_send, z_recv, s_send, s_recv, t_send, t_recv, _, x_send, x_recv = refs[-14:]
    row, col = lax.axis_index("row"), lax.axis_index("col")
    z, core = col // 2, col % 2
    at = lambda r, c: (r, c)
    peers = [at(row, (col + shift) % 8) for shift in range(1, 8)]
    peers += [at(row ^ d, col) for d in range(1, 4)]
    greet(peers)
    own = pltpu.make_async_copy(grads.at[core], mine, own_sem)
    own.start()
    sends = []
    for d in (3, 1, 2, 0):
        copy = remote(
            grads.at[1 - core, row ^ d], swapped.at[row ^ d], c_send.at[d], c_recv.at[d], at(row, col ^ 1)
        )
        copy.start()
        sends.append(copy)
    for shift in range(1, 8):
        copy = remote(
            small, small_col.at[col], s_send.at[shift - 1], s_recv.at[7 - shift], at(row, (col + shift) % 8)
        )
        copy.start()
        sends.append(copy)
    small_col[col] = small[...]
    own.wait()
    f32 = jnp.float32
    each = tokens.shape[1] // grain

    def each_chunk(act_remote, act_own):
        for local in range(rows.shape[0] // grain):
            pair = local // 2
            turn = 4 * (pair // 2) + (core if pair % 2 == 0 else 3 - core)
            chunk = 2 * turn + local % 2 if local < 8 else 16 + 12 * core + local - 8
            shard = chunk // each
            source = rows.at[pl.ds(local * grain, grain), :]
            start = pl.multiple_of((chunk % each) * grain, grain)
            target = tokens.at[z, pl.ds(start, grain), :]

            @pl.when(shard != col)
            def _():
                act_remote(remote(source, target, x_send.at[local], x_recv, at(row, shard)))

            if act_own:

                @pl.when(shard == col)
                def _():
                    pltpu.make_async_copy(source, target, x_recv).start()

    each_chunk(lambda copy: copy.start(), True)

    def add(target, source):
        target[...] = (target[...].astype(f32) + source[...].astype(f32)).astype(target.dtype)

    def add_swapped(position):
        sends[position].wait_recv()
        d = (3, 1, 2, 0)[position]
        for q in range(4):
            add(mine.at[row ^ d, q], swapped.at[row ^ d, q])

    def send(index, source, target, device):
        copy = remote(source, target, r_send.at[index], r_recv.at[index], device)
        copy.start()
        sends.append(copy)
        return copy

    add_swapped(0)
    far_a = send(0, mine.at[row ^ 3, pl.ds(0, 2)], far.at[pl.ds(0, 2)], at(row ^ 2, col))
    far_b = send(1, mine.at[row ^ 3, pl.ds(2, 2)], far.at[pl.ds(2, 2)], at(row ^ 1, col))
    add_swapped(1)
    x_b = send(2, mine.at[row ^ 1, pl.ds(2, 2)], beside.at[pl.ds(2, 2)], at(row ^ 1, col))
    add_swapped(2)
    y_a = send(3, mine.at[row ^ 2, pl.ds(0, 2)], below.at[pl.ds(0, 2)], at(row ^ 2, col))
    add_swapped(3)
    for shift in range(1, 8):
        sends[3 + shift].wait_recv()
    part[...] = small_col[0]
    for c in range(1, 8):
        part[...] += small_col[c]
    rounds = []
    for d in range(1, 4):
        copy = remote(part, small_row.at[row], t_send.at[d - 1], t_recv.at[d - 1], at(row ^ d, col))
        copy.start()
        rounds.append(copy)
    small_row[row] = part[...]
    far_a.wait_recv()
    for q in (0, 1):
        add(mine.at[row ^ 1, q], far.at[q])
    x_a = send(4, mine.at[row ^ 1, pl.ds(0, 2)], beside.at[pl.ds(0, 2)], at(row ^ 1, col))
    far_b.wait_recv()
    for q in (2, 3):
        add(mine.at[row ^ 2, q], far.at[q])
    y_b = send(5, mine.at[row ^ 2, pl.ds(2, 2)], below.at[pl.ds(2, 2)], at(row ^ 2, col))
    for copy in (x_b, y_a, x_a, y_b):
        copy.wait_recv()

    def total(q):
        return (
            mine[row, q].astype(f32) + beside[q].astype(f32) + below[q].astype(f32)
        )

    lasts = []
    for d in range(1, 4):
        q = z ^ d
        mine[row, q] = total(q).astype(mine.dtype)
        copy = remote(
            mine.at[row, q], tail.at[d - 1], z_send.at[d - 1], z_recv.at[d - 1], at(row, q * 2 + core)
        )
        copy.start()
        lasts.append(copy)
    result = total(z)
    for d in range(1, 4):
        lasts[d - 1].wait_recv()
        result = result + tail[d - 1].astype(f32)
    final[...] = result
    for copy in rounds:
        copy.wait_recv()
    pltpu.make_async_copy(tokens, tokens, x_recv).wait()
    each_chunk(lambda copy: copy.wait_send(), False)
    small_out[...] = small_row[0] + small_row[1] + small_row[2] + small_row[3]
    for copy in sends + lasts + rounds:
        copy.wait_send()


def end_exchange(grads, small, rows, shape, deps):
    grain = 64
    height, lanes = grads.shape[3:]
    slab = lambda *n: pltpu.VMEM(n + (height, lanes), grads.dtype)
    dma = lambda n: pltpu.SemaphoreType.DMA((n,))
    return pl.pallas_call(
        partial(end_kernel, grain),
        in_specs=[HOLD, pl.BlockSpec(memory_space=pltpu.VMEM), HOLD] + [HOLD] * len(deps),
        out_specs=[pl.BlockSpec(memory_space=pltpu.VMEM)] * 2 + [HOLD],
        out_shape=[
            jax.ShapeDtypeStruct((height, lanes), jnp.float32),
            jax.ShapeDtypeStruct(small.shape, jnp.float32),
            jax.ShapeDtypeStruct(shape, rows.dtype),
        ],
        scratch_shapes=[
            slab(4, 4), slab(4, 4), slab(4), slab(4), slab(4), slab(3),
            pltpu.VMEM((8,) + small.shape, jnp.float32), pltpu.VMEM((4,) + small.shape, jnp.float32),
            pltpu.VMEM(small.shape, jnp.float32),
            pltpu.SemaphoreType.DMA, dma(4), dma(4), dma(6), dma(6), dma(3), dma(3),
            dma(7), dma(7), dma(3), dma(3), dma(1), dma(rows.shape[0] // grain), pltpu.SemaphoreType.DMA,
        ],
        compiler_params=pltpu.CompilerParams(
            collective_id=1, has_side_effects=True, vmem_limit_bytes=40 * 1024 * 1024
        ),
        cost_estimate=pl.CostEstimate(flops=100_000_000_000, bytes_accessed=0, transcendentals=0),
        name="end_exchange",
    )(grads, small, rows, *deps)


def lane_runs(width, padded, columns, qkv_cols, out_cols):
    runs = []
    for c in range(columns):
        start = c * qkv_cols
        while start < (c + 1) * qkv_cols:
            third = start // width
            stop = min((c + 1) * qkv_cols, (third + 1) * width)
            runs.append((0, third * padded + start - third * width, c, start - c * qkv_cols, stop - start))
            start = stop
        runs.append((1, c * out_cols, c, qkv_cols, out_cols))
    return runs


def assemble_kernel(runs, width, padded, full, triple, out):
    step = pl.program_id(0)
    height = full.shape[3]
    columns = 2 * full.shape[2]
    slabs = [full[c % 2, 0, c // 2].astype(jnp.float32) for c in range(columns)]
    piece = lambda run: slabs[run[2]][:, run[3] : run[3] + run[4]]
    gap = jnp.zeros((height, padded - width), jnp.float32)

    def line(which, third):
        low, high = third * padded, third * padded + padded
        chosen = [r for r in runs if r[0] == which and low <= r[1] < high]
        return jnp.concatenate([piece(r) for r in chosen] + [gap], axis=1).astype(triple.dtype)

    for third in range(3):
        triple[:, third * padded : (third + 1) * padded] = line(0, third)

    @pl.when(step == 0)
    def _():
        out[width:, :] = jnp.zeros((padded - width, padded), out.dtype)

    out[pl.ds(pl.multiple_of(step * height, 16), height), :] = line(1, 0)


def assemble(full, width, padded, qkv_cols):
    height, lanes = full.shape[3:]
    runs = lane_runs(width, padded, 2 * full.shape[2], qkv_cols, lanes - qkv_cols)
    return pl.pallas_call(
        partial(assemble_kernel, runs, width, padded),
        grid=(full.shape[1],),
        in_specs=[pl.BlockSpec((2, 1, full.shape[2], height, lanes), lambda r: (0, r, 0, 0, 0))],
        out_specs=[
            pl.BlockSpec((height, 3 * padded), lambda r: (r, 0)),
            pl.BlockSpec((padded, padded), lambda r: (0, 0)),
        ],
        out_shape=[
            jax.ShapeDtypeStruct((width, 3 * padded), full.dtype),
            jax.ShapeDtypeStruct((padded, padded), full.dtype),
        ],
        compiler_params=pltpu.CompilerParams(vmem_limit_bytes=48 * 1024 * 1024),
        cost_estimate=pl.CostEstimate(flops=12_000_000_000, bytes_accessed=0, transcendentals=0),
        name="assemble_weights",
    )(full)


def divide_kernel(runs, triple, out, full):
    wide = triple[...].astype(jnp.float32)
    last = out[...].astype(jnp.float32)
    for c in range(2 * full.shape[2]):
        parts = [
            (wide, last)[r[0]][:, r[1] : r[1] + r[4]] for r in runs if r[2] == c
        ]
        full[c % 2, 0, c // 2] = jnp.concatenate(parts, axis=1).astype(full.dtype)


def divide(triple, out, width, padded, qkv_cols, out_cols, columns, rows):
    height, lanes = width // rows, qkv_cols + out_cols
    runs = lane_runs(width, padded, columns, qkv_cols, out_cols)
    return pl.pallas_call(
        partial(divide_kernel, runs),
        grid=(rows,),
        in_specs=[
            pl.BlockSpec((height, 3 * padded), lambda r: (r, 0)),
            pl.BlockSpec((height, out.shape[1]), lambda r: (r, 0)),
        ],
        out_specs=pl.BlockSpec((2, 1, columns // 2, height, lanes), lambda r: (0, r, 0, 0, 0)),
        out_shape=jax.ShapeDtypeStruct((2, rows, columns // 2, height, lanes), jnp.bfloat16),
        compiler_params=pltpu.CompilerParams(vmem_limit_bytes=48 * 1024 * 1024),
        cost_estimate=pl.CostEstimate(flops=1_000_000_000, bytes_accessed=0, transcendentals=0),
        name="divide_gradients",
    )(triple, out)


def finish_kernel(own_trunk, dq, dk, dv, other_k, other_v, *refs):
    total, sums = refs[-2:]
    step = pl.program_id(0)
    each = pl.num_programs(0) // 3

    def deliver(value):
        total[...] = value
        sums[...] = jnp.sum(value.astype(jnp.float32), axis=0, keepdims=True)

    @pl.when(step < each)
    def _():
        deliver(dq[...])

    for index, (near, far) in enumerate(((dk, other_k), (dv, other_v))):

        @pl.when(step // each == index + 1)
        def _():
            value = near[:own_trunk, :].astype(jnp.float32)
            for start in range(0, far.shape[0], own_trunk):
                value = value + far[start : start + own_trunk, :].astype(jnp.float32)
            deliver(jnp.concatenate([value.astype(total.dtype), near[own_trunk:, :]], axis=0))


def finish_gradients(own_trunk, dq, dk, dv, other_k, other_v, deps):
    rows, padded = dq.shape
    block = 384
    each = padded // block

    def spec(count, third):
        return pl.BlockSpec((count, block), lambda j: (0, jnp.clip(j - third * each, 0, each - 1)))

    return pl.pallas_call(
        partial(finish_kernel, own_trunk),
        grid=(3 * each,),
        in_specs=[
            spec(rows, 0), spec(rows, 1), spec(rows, 2), spec(other_k.shape[0], 1), spec(other_v.shape[0], 2),
        ]
        + [HOLD] * len(deps),
        out_specs=[
            pl.BlockSpec((rows, block), lambda j: (0, j)), pl.BlockSpec((1, block), lambda j: (0, j)),
        ],
        out_shape=[
            jax.ShapeDtypeStruct((rows, 3 * padded), jnp.bfloat16),
            jax.ShapeDtypeStruct((1, 3 * padded), jnp.float32),
        ],
        compiler_params=pltpu.CompilerParams(vmem_limit_bytes=48 * 1024 * 1024),
        cost_estimate=pl.CostEstimate(flops=1_000_000_000, bytes_accessed=0, transcendentals=0),
        name="finish_gradients",
    )(dq, dk, dv, other_k, other_v, *deps)


def norm_parts(value):
    center = value - jnp.mean(value, axis=-1, keepdims=True)
    scale = lax.rsqrt(jnp.mean(center * center, axis=-1, keepdims=True) + 1e-05)
    return center * scale, scale


def norm_back(grad, value, gain):
    unit, scale = norm_parts(value)
    scaled = grad * gain
    back = scaled - jnp.mean(scaled, axis=-1, keepdims=True)
    back = scale * (back - unit * jnp.mean(scaled * unit, axis=-1, keepdims=True))
    return back, jnp.sum(grad * unit, axis=0, keepdims=True), jnp.sum(grad, axis=0, keepdims=True)


def out_kernel(mixed, weight, bias, rows, gain, shift, middle, second):
    width = rows.shape[1]
    attended = dot_nn(mixed[...], weight[...])[:, :width] + bias[...]
    total = rows[...].astype(jnp.float32) + attended.astype(jnp.bfloat16).astype(jnp.float32)
    middle[...] = total
    unit, _ = norm_parts(total)
    second[...] = (unit * gain[...] + shift[...]).astype(jnp.bfloat16)


def by_rows(kernel, name, count, chunked, fixed, outs, sums=(), scratch=(), flops=0, deps=()):
    chunk = count // 5
    block = lambda width: pl.BlockSpec((chunk, width), lambda i: (i, 0))
    whole = lambda shape: pl.BlockSpec(shape, lambda i: (0,) * len(shape))
    return pl.pallas_call(
        kernel,
        grid=(5,),
        in_specs=[block(v.shape[1]) for v in chunked] + [whole(v.shape) for v in fixed]
        + [HOLD] * len(deps),
        out_specs=[block(width) for width, _ in outs] + [whole(shape) for shape, _ in sums],
        out_shape=[jax.ShapeDtypeStruct((count, width), dtype) for width, dtype in outs]
        + [jax.ShapeDtypeStruct(shape, dtype) for shape, dtype in sums],
        scratch_shapes=list(scratch),
        compiler_params=pltpu.CompilerParams(vmem_limit_bytes=56 * 1024 * 1024),
        cost_estimate=pl.CostEstimate(flops=flops, bytes_accessed=0, transcendentals=0),
        name=name,
    )(*chunked, *fixed, *deps)


def project_out(mixed, rows, weight, bias, gain, shift):
    width = rows.shape[1]

    def kernel(mixed, rows, weight, bias, gain, shift, middle, second):
        out_kernel(mixed, weight, bias, rows, gain, shift, middle, second)

    line = lambda v: v.reshape(1, width)
    return by_rows(
        kernel, "project_out", rows.shape[0], (mixed, rows), (weight, line(bias), line(gain), line(shift)),
        ((width, jnp.float32), (width, jnp.bfloat16)), flops=12_000_000_000,
    )


def middle_kernel(held, second_grad, lowered, middle, seed, mixed, weight, gain, down_bias, *refs):
    result, middle_grad, mixed_grad, sums, out_grad, total = refs[held:]
    step = pl.program_id(0)
    width = middle.shape[1]
    value, up = middle[...], seed[...].astype(jnp.float32)
    result[...] = (value + lowered[...] + down_bias[...]).astype(jnp.bfloat16)
    back, gain_sum, shift_sum = norm_back(second_grad[...], value, gain[...])
    grad = up + back
    middle_grad[...] = grad
    low = grad.astype(jnp.bfloat16)
    mixed_grad[...] = dot_nt(low, weight[:, :width]).astype(jnp.bfloat16)
    part = dot_tn(mixed[...], low)
    low_sum = jnp.sum(low.astype(jnp.float32), axis=0, keepdims=True)
    up_sum = jnp.sum(up, axis=0, keepdims=True)
    lines = jnp.concatenate([low_sum, gain_sum, shift_sum, up_sum], axis=0)

    @pl.when(step == 0)
    def _():
        sums[...] = lines
        total[...] = part

    @pl.when(step > 0)
    def _():
        sums[...] += lines
        total[...] += part

    @pl.when(step == pl.num_programs(0) - 1)
    def _():
        out_grad[:, :width] = total[:width, :].astype(jnp.bfloat16)
        out_grad[:, width:] = jnp.zeros((width, out_grad.shape[1] - width), jnp.bfloat16)


def middle_back(second_grad, lowered, middle, seed, mixed, weight, gain, down_bias, deps):
    rows, width = middle.shape
    padded = weight.shape[0]
    line = lambda v: v.reshape(1, width)
    return by_rows(
        partial(middle_kernel, len(deps)), "middle_back", rows, (second_grad, lowered, middle, seed, mixed),
        (weight, line(gain), line(down_bias)),
        ((width, jnp.bfloat16), (width, jnp.float32), (padded, jnp.bfloat16)),
        (((4, width), jnp.float32), ((width, padded), jnp.bfloat16)),
        (pltpu.VMEM((padded, width), jnp.float32),), flops=25_000_000_000, deps=deps,
    )


def first_kernel(held, triple_grad, rows, middle_grad, weight, gain, *refs):
    input_grad, sums = refs[held:]
    step = pl.program_id(0)
    grad = dot_nt(triple_grad[...], weight[...])
    back, gain_sum, shift_sum = norm_back(grad, rows[...].astype(jnp.float32), gain[...])
    input_grad[...] = (middle_grad[...] + back).astype(jnp.bfloat16)
    lines = jnp.concatenate([gain_sum, shift_sum], axis=0)

    @pl.when(step == 0)
    def _():
        sums[...] = lines

    @pl.when(step > 0)
    def _():
        sums[...] += lines


def first_back(triple_grad, rows, middle_grad, weight, gain, deps):
    count, width = rows.shape
    return by_rows(
        partial(first_kernel, len(deps)), "first_back", count, (triple_grad, rows, middle_grad), (weight, gain.reshape(1, width)),
        ((width, jnp.bfloat16),), (((2, width), jnp.float32),), flops=4_000_000_000, deps=deps,
    )


def blocks_kernel(rest, core, total, other, total_tail, other_tail, out):
    quarter = pl.program_id(0)
    main = total.shape[1]
    out[0, :, :main] = total[...]
    out[0, :, main : 2 * main] = other[...]
    for shard in range(8):

        @pl.when(quarter + 4 * core[0] == shard)
        def _():
            cut = slice(shard * rest, (shard + 1) * rest)
            out[0, :, 2 * main : 2 * main + rest] = total_tail[:, cut]
            out[0, :, 2 * main + rest :] = other_tail[:, cut]


def pair_blocks(core, total, other, main, rest):
    rows = total.shape[0]
    spec = pl.BlockSpec((rows, main), lambda q, s: (0, q + 4 * s[0]))
    tail = pl.BlockSpec((rows, 8 * rest), lambda q, s: (0, main // rest))
    return pl.pallas_call(
        partial(blocks_kernel, rest),
        grid_spec=pltpu.PrefetchScalarGridSpec(
            num_scalar_prefetch=1,
            grid=(4,),
            in_specs=[spec, spec, tail, tail],
            out_specs=pl.BlockSpec((1, rows, 2 * (main + rest)), lambda q, s: (q, 0, 0)),
        ),
        out_shape=jax.ShapeDtypeStruct((4, rows, 2 * (main + rest)), total.dtype),
        cost_estimate=pl.CostEstimate(flops=1_000_000_000, bytes_accessed=0, transcendentals=0),
        name="pair_blocks",
    )(core, total, other, total, other)


def after(value, *deps):
    def kernel(*refs):
        pass

    return pl.pallas_call(
        kernel,
        in_specs=[HOLD] * (1 + len(deps)),
        out_specs=HOLD,
        out_shape=jax.ShapeDtypeStruct(value.shape, value.dtype),
        input_output_aliases={0: 0},
        name="after",
    )(value, *deps)


def order_kernel(table, *refs):
    pieces, out = refs[:-1], refs[-1]
    for index, piece in enumerate(pieces):
        out[table[index]] = piece[...]


def in_order(table, pieces):
    rows, width = pieces[0].shape
    whole = pl.BlockSpec((rows, width), lambda i, s: (0, 0))
    return pl.pallas_call(
        order_kernel,
        grid_spec=pltpu.PrefetchScalarGridSpec(
            num_scalar_prefetch=1,
            grid=(1,),
            in_specs=[whole] * len(pieces),
            out_specs=pl.BlockSpec((len(pieces), rows, width), lambda i, s: (0, 0, 0)),
        ),
        out_shape=jax.ShapeDtypeStruct((len(pieces), rows, width), pieces[0].dtype),
        compiler_params=pltpu.CompilerParams(vmem_limit_bytes=48 * 1024 * 1024),
        cost_estimate=pl.CostEstimate(flops=0, bytes_accessed=4 * len(pieces) * rows * width, transcendentals=0),
        name="in_order",
    )(table, *pieces)


def layer_norm(value, gain, bias):
    center = value - jnp.mean(value, axis=-1, keepdims=True)
    spread = jnp.mean(center * center, axis=-1, keepdims=True)
    return center * lax.rsqrt(spread + 1e-05) * gain + bias


def own_rows(parts, part):
    blocks = TRUNK // (128 * parts)
    starts = []
    for k in range(blocks):
        base = (k // 2) * 2 * parts
        starts.append(128 * (base + (part if k % 2 == 0 else 2 * parts - 1 - part)))
    rows = [np.arange(128) + s for s in starts]
    groups = (TRUNK // 256) // parts
    rows.append(TRUNK + part * groups * GROUP + np.arange(groups * GROUP))
    return np.concatenate(rows)


def spread_kernel(grain, table, *refs):
    pieces, out = refs[:-1], refs[-1]
    each = pieces[0].shape[0] // grain
    for index, piece in enumerate(pieces):
        for i in range(each):
            target = table[index * each + i]

            @pl.when(target >= 0)
            def _():
                rows = pl.ds(pl.multiple_of(target * grain, grain), grain)
                out[rows, :] = piece[i * grain : (i + 1) * grain, :]


def spread(table, pieces, grain, count):
    width = pieces[0].shape[1]
    whole = lambda rows: pl.BlockSpec((rows, width), lambda i, s: (0, 0))
    return pl.pallas_call(
        partial(spread_kernel, grain),
        grid_spec=pltpu.PrefetchScalarGridSpec(
            num_scalar_prefetch=1,
            grid=(1,),
            in_specs=[whole(p.shape[0]) for p in pieces],
            out_specs=whole(count),
        ),
        out_shape=jax.ShapeDtypeStruct((count, width), pieces[0].dtype),
        compiler_params=pltpu.CompilerParams(vmem_limit_bytes=48 * 1024 * 1024),
        cost_estimate=pl.CostEstimate(flops=0, bytes_accessed=6 * count * width, transcendentals=0),
        name="spread_rows",
    )(table, *pieces)


def collect_kernel(grain, count, table, *refs):
    sources, outs = refs[:-count], refs[-count:]
    each = outs[0].shape[0] // grain
    for index, out in enumerate(outs):
        for i in range(each):
            owner = table[2 * (index * each + i)]
            start = table[2 * (index * each + i) + 1]
            for which, source in enumerate(sources):

                @pl.when(owner == which)
                def _():
                    rows = pl.ds(pl.multiple_of(start * grain, grain), grain)
                    out[i * grain : (i + 1) * grain, :] = source[rows, :]


def collect(table, sources, grain, count, length):
    width = sources[0].shape[1]
    whole = lambda rows: pl.BlockSpec((rows, width), lambda i, s: (0, 0))
    return pl.pallas_call(
        partial(collect_kernel, grain, count),
        grid_spec=pltpu.PrefetchScalarGridSpec(
            num_scalar_prefetch=1,
            grid=(1,),
            in_specs=[whole(s.shape[0]) for s in sources],
            out_specs=[whole(length)] * count,
        ),
        out_shape=[jax.ShapeDtypeStruct((length, width), sources[0].dtype)] * count,
        compiler_params=pltpu.CompilerParams(vmem_limit_bytes=48 * 1024 * 1024),
        cost_estimate=pl.CostEstimate(flops=0, bytes_accessed=6 * count * length * width, transcendentals=0),
        name="collect_rows",
    )(table, *sources)


class Place:
    def __init__(self, micro, tree):
        self.columns = lax.axis_size("col")
        self.micro = micro
        self.parts = self.columns // micro
        self.tree = tree
        self.length = tree // self.columns
        self.grain = math.gcd(self.length, 128)
        me = lax.axis_index("col")
        self.quarter, self.part = me // self.parts, me % self.parts
        self.own = np.stack([own_rows(self.parts, part) for part in range(self.parts)])
        self.count = self.own.shape[1]

    def quarter_perm(self, shift):
        p = self.parts
        return [(c, ((c // p) ^ shift) * p + c % p) for c in range(self.columns)]

    def part_perm(self, shift):
        return [(c, c ^ shift) for c in range(self.columns)]

    def swap_quarters(self, value):
        groups = [
            [q * self.parts + part for q in range(self.micro)] for part in range(self.parts)
        ]
        return lax.all_to_all(value, "col", 0, 0, axis_index_groups=groups, tiled=True)

    def tree_sources(self, value):
        flat = (self.micro * self.length, value.shape[2])
        moved = [lax.ppermute(value, "col", self.part_perm(e)) for e in range(1, self.parts)]
        return [v.reshape(flat) for v in [value] + moved]

    def to_tree(self, sources):
        grain, each = self.grain, self.length // self.grain
        table = np.full((self.parts, self.tree // grain), -1, np.int32)
        for part in range(self.parts):
            table[part, self.own[part, ::grain] // grain] = np.arange(self.count // grain)
        mine = lax.dynamic_index_in_dim(jnp.asarray(table), self.part, 0, keepdims=False)
        e, rest = np.divmod(np.arange(self.tree // grain, dtype=np.int32), self.micro * each)
        quarter, inside = np.divmod(rest, each)
        chunk = (quarter * self.parts + (self.part ^ e)) * each + inside
        return spread(mine[chunk], sources, grain, self.count)

    def from_tree_sources(self, value):
        split = value.reshape(-1, self.grain, value.shape[1])
        moved = [lax.ppermute(split, "col", self.part_perm(e)) for e in range(1, self.parts)]
        return [value] + [v.reshape(value.shape) for v in moved]

    def from_tree_parts(self, sources):
        grain, each, parts = self.grain, self.length // self.grain, self.parts
        owner = np.zeros(self.tree // grain, np.int32)
        local = np.zeros(self.tree // grain, np.int32)
        for part in range(parts):
            owner[self.own[part, ::grain] // grain] = part
            local[self.own[part, ::grain] // grain] = np.arange(self.count // grain)
        quarter, inside = np.divmod(np.arange(self.micro * each, dtype=np.int32), each)
        chunk = (quarter * parts + self.part) * each + inside
        table = jnp.stack([jnp.asarray(owner)[chunk] ^ self.part, jnp.asarray(local)[chunk]], axis=1)
        (out,) = collect(table.reshape(-1), sources, grain, 1, self.micro * self.length)
        return out.reshape(self.micro, self.length, sources[0].shape[1])

    def masks(self, own_ids, parent_ids):
        parts = self.parts
        own = jnp.asarray(self.own, jnp.int32)
        mine = lax.dynamic_index_in_dim(own, self.part, 0, keepdims=False)
        trunk_rows = TRUNK // parts
        tiles = trunk_rows // QT
        trunk = []
        for tile in range(tiles):
            span = slice(tile * QT, (tile + 1) * QT)
            keys = jnp.concatenate(
                [
                    lax.dynamic_index_in_dim(own, self.part ^ e, 0, keepdims=False)[span]
                    for e in range(parts)
                ]
            )
            trunk.append(jnp.where(keys[None, :] <= mine[span][:, None], 0.0, -1e30))
        group = []
        groups = (TRUNK // 256) // parts
        places = jnp.arange(GROUP)
        for g in range(groups):
            start = TRUNK + (self.part * groups + g) * GROUP
            ids = lax.dynamic_slice_in_dim(own_ids, start, GROUP)
            parent = lax.dynamic_slice_in_dim(parent_ids, start, GROUP)
            seen = (places[None, :] <= places[:, None]) & (
                (ids[None, :] == 0) | (ids[None, :] == ids[:, None]) | (ids[None, :] == parent[:, None])
            )
            group.append(jnp.where(seen, 0.0, -1e30))
        return jnp.stack(trunk).astype(jnp.float32), jnp.stack(group).astype(jnp.float32)


BOTH = ("row", "col")
ROW_CUT = 144


def plain_gather(block):
    full = lax.all_gather(block, BOTH, axis=0, tiled=False)
    full = full.reshape(lax.axis_size("row"), lax.axis_size("col"), *block.shape)
    return full.transpose(0, 2, 1, 3).reshape(full.shape[0] * full.shape[2], full.shape[1] * full.shape[3])


def plain_scatter(grad):
    rows, cols = lax.axis_size("row"), lax.axis_size("col")
    blocks = grad.astype(jnp.bfloat16).reshape(rows, grad.shape[0] // rows, cols, grad.shape[1] // cols)
    blocks = blocks.transpose(0, 2, 1, 3).reshape(rows * cols, grad.shape[0] // rows, grad.shape[1] // cols)
    return lax.psum_scatter(blocks, BOTH, scatter_dimension=0, tiled=False).astype(jnp.float32)


def across(value, shift):
    return lax.ppermute(value, "row", [(r, r ^ shift) for r in range(lax.axis_size("row"))])


def row_gather(block):
    beside = across(block, 1)
    below = across(block, 2)
    return [block, beside, below, across(beside[:ROW_CUT], 2), across(below[ROW_CUT:], 1)]


def row_starts(rows):
    me = lax.axis_index("row")
    far = (me ^ 3) * rows
    return [me * rows, (me ^ 1) * rows, (me ^ 2) * rows, far, far + ROW_CUT]


def core_swap(place, value):
    return lax.ppermute(value, "col", place.part_perm(1))


def far_sums(own, swapped):
    f32, bf16 = jnp.float32, jnp.bfloat16
    total = (own[3].astype(f32) + swapped[3].astype(f32)).astype(bf16)
    return total[:ROW_CUT], total[ROW_CUT:]


def far_sends(sums):
    return across(sums[0], 2), across(sums[1], 1)


def near_sums(own, swapped, received):
    f32 = jnp.float32
    beside = own[1].astype(f32) + swapped[1].astype(f32)
    below = own[2].astype(f32) + swapped[2].astype(f32)
    beside = jnp.concatenate([beside[:ROW_CUT] + received[0].astype(f32), beside[ROW_CUT:]], axis=0)
    below = jnp.concatenate([below[:ROW_CUT], below[ROW_CUT:] + received[1].astype(f32)], axis=0)
    return beside.astype(jnp.bfloat16), below.astype(jnp.bfloat16)


def near_sends(sums):
    return across(sums[0], 1), across(sums[1], 2)


def row_total(own, swapped, last):
    f32 = jnp.float32
    base = own[0].astype(f32) + swapped[0].astype(f32)
    return (base + last[0].astype(f32) + last[1].astype(f32)).astype(jnp.bfloat16)


def pack_pair(w_up, w_down):
    main = w_up.shape[1] // 256 * 256
    down = w_down.T
    parts = []
    for start in range(0, main, FF_BLOCK):
        parts += [w_up[:, start : start + FF_BLOCK], down[:, start : start + FF_BLOCK]]
    return jnp.concatenate(parts + [w_up[:, main:], down[:, main:]], axis=1)


class QuickWeights:
    def __init__(self, place, w_qkv, w_out, w_up, w_down, padded):
        self.place, self.padded = place, padded
        self.rows = w_qkv.shape[0]
        self.cols = place.columns
        self.width = w_out.shape[1] * self.cols
        self.qkv_cols, self.out_cols, self.up_cols = w_qkv.shape[1], w_out.shape[1], w_up.shape[1]
        self.main = main = self.up_cols // 256 * 256
        self.rest = rest = self.up_cols - main
        self.role = place.part
        self.scalars = jnp.stack([self.role] + row_starts(self.rows)).astype(jnp.int32)
        self.pack = pack_pair(w_up, w_down)

    def start(self, w_qkv, w_out, value):
        full, rows, pack = start_exchange(
            jnp.concatenate([w_qkv, w_out], axis=1), self.pack, value, self.place.count
        )
        place = self.place
        pieces = [pack] + [
            lax.ppermute(pack, "col", place.quarter_perm(d)) for d in range(1, place.micro)
        ]
        self.own = in_order(place.quarter ^ jnp.arange(place.micro, dtype=jnp.int32), pieces)
        self.beside, self.below = across(self.own, 1), across(self.own, 2)
        self.far = (self.beside[:2], self.below[2:])
        mine = [self.own, self.beside, self.below, across(self.far[0], 2), across(self.far[1], 1)]
        self.pair = (mine, [core_swap(place, piece) for piece in mine])
        self.triple, self.out = assemble(full, self.width, self.padded, self.qkv_cols)
        return rows

    def end(self, triple_grad, out_grad, small, rows, shape, deps):
        blocks = divide(
            triple_grad, out_grad, self.width, self.padded, self.qkv_cols, self.out_cols, self.cols, 4
        )
        final, summed, tokens = end_exchange(blocks, small, rows, shape, deps)
        return final[:, : self.qkv_cols], final[:, self.qkv_cols :], summed, tokens

    def bias_order(self, bias):
        blocks = bias.reshape(self.place.micro, self.place.parts, self.up_cols).transpose(1, 0, 2)
        blocks = blocks.reshape(self.cols, self.up_cols)
        return jnp.concatenate([blocks[:, : self.main].reshape(-1), blocks[:, self.main :].reshape(-1)])

    def bias_back(self, grad):
        edge = self.cols * self.main
        blocks = jnp.concatenate(
            [grad[:edge].reshape(self.cols, self.main), grad[edge:].reshape(self.cols, self.rest)], axis=1
        )
        blocks = blocks.reshape(self.place.parts, self.place.micro, self.up_cols)
        return blocks.transpose(1, 0, 2).reshape(-1)

    def pair_final(self, parts):
        final = jnp.sum(parts.astype(jnp.float32), axis=0)
        main, rest = self.main, self.rest
        own = jnp.concatenate([final[:, :main], final[:, 2 * main : 2 * main + rest]], axis=1)
        far = jnp.concatenate([final[:, main : 2 * main], final[:, 2 * main + rest :]], axis=1)
        up = jnp.where(self.role == 0, own, far)
        down = jnp.where(self.role == 0, far, own)
        return up, down.T


class PlainWeights:
    def __init__(self, place, w_qkv, w_out, w_up, w_down, padded):
        self.place, self.padded = place, padded
        qkv, out = plain_gather(w_qkv), plain_gather(w_out)
        self.width = width = out.shape[1]
        pad = padded - width
        self.triple = jnp.pad(qkv.reshape(width, 3, width), ((0, 0), (0, 0), (0, pad))).reshape(
            width, 3 * padded
        )
        self.out = jnp.pad(out, ((0, pad), (0, pad)))
        self.rows, self.cols, self.up_cols = w_qkv.shape[0], place.columns, w_up.shape[1]
        self.main = self.up_cols // 256 * 256
        self.rest = self.up_cols - self.main
        full = lax.all_gather(pack_pair(w_up, w_down), BOTH, axis=0, tiled=False)
        full = full.reshape(lax.axis_size("row"), self.cols, self.rows, 2 * self.up_cols)
        self.pair = (full.transpose(1, 0, 2, 3).reshape(1, self.cols, width, 2 * self.up_cols),)
        self.scalars = jnp.zeros((2,), jnp.int32)

    def bias_order(self, bias):
        blocks = bias.reshape(self.cols, self.up_cols)
        return jnp.concatenate([blocks[:, : self.main].reshape(-1), blocks[:, self.main :].reshape(-1)])

    def bias_back(self, grad):
        edge = self.cols * self.main
        return jnp.concatenate(
            [grad[:edge].reshape(self.cols, self.main), grad[edge:].reshape(self.cols, self.rest)], axis=1
        ).reshape(-1)

    def natural(self, grad):
        edge = self.cols * self.main
        cut = lambda value: value.reshape(grad.shape[0], self.cols, -1)
        return jnp.concatenate([cut(grad[:, :edge]), cut(grad[:, edge:])], axis=2).reshape(grad.shape)

    def scatter_pair(self, mine, theirs):
        return plain_scatter(self.natural(mine)), plain_scatter(self.natural(theirs)).T

    def scatter_first(self, triple_grad, out_grad):
        width, padded = self.width, self.padded
        qkv = triple_grad.reshape(width, 3, padded)[:, :, :width].reshape(width, 3 * width)
        return plain_scatter(qkv), plain_scatter(out_grad[:, :width])


def cuts_of(pairs, count):
    edges = [round(i * pairs / count) for i in range(count + 1)]
    return list(zip(edges[:-1], edges[1:]))


def local(
    block_input, paths, ln1_gain, ln1_bias, w_qkv, q_bias, v_bias, w_out, out_bias,
    ln2_gain, ln2_bias, w_up, up_bias, w_down, down_bias, cotangent,
):
    micro, _, width = block_input.shape
    place = Place(micro, paths.shape[2])
    parts = place.parts
    heads = width // HEAD_DIM
    padded = (heads + 1) // 2 * 128
    pairs = padded // 128
    pad = padded - width
    own_trunk = TRUNK // parts
    f32, bf16 = jnp.float32, jnp.bfloat16

    quick = lax.axis_size("row") == 4 and parts == 2 and w_qkv.shape[0] == 272
    if quick:
        weights = QuickWeights(place, w_qkv, w_out, w_up, w_down, padded)
        rows_low = weights.start(w_qkv, w_out, block_input)
    else:
        weights = PlainWeights(place, w_qkv, w_out, w_up, w_down, padded)
        rows_low = place.to_tree(place.tree_sources(place.swap_quarters(block_input)))
    rows_in = rows_low.astype(f32)

    own_ids = lax.dynamic_index_in_dim(paths[0], place.quarter, 0, keepdims=False)
    parent_ids = lax.dynamic_index_in_dim(paths[1], place.quarter, 0, keepdims=False)
    mask_trunk, mask_group = place.masks(own_ids, parent_ids)

    seed_moved = place.swap_quarters(after(cotangent, weights.own) if quick else cotangent)

    q_scale = HEAD_DIM**-0.5 * LOG2E
    triple_bias = jnp.concatenate(
        [jnp.pad(q_bias * q_scale, (0, pad)), jnp.zeros((padded,), f32), jnp.pad(v_bias, (0, pad))]
    )
    triple_scale = jnp.concatenate([jnp.full((padded,), q_scale, f32), jnp.ones((2 * padded,), f32)])
    first = layer_norm(rows_in, ln1_gain, ln1_bias).astype(bf16)
    triple = (dot_nn(first, weights.triple) * triple_scale + triple_bias).astype(bf16)
    shared = triple[:own_trunk, padded:]
    others = jnp.concatenate(
        [lax.ppermute(shared, "col", place.part_perm(e)) for e in range(1, parts)], axis=0
    )
    cuts = [round(pairs * part / 9) for part in (0, 6, 8, 9)]
    before, gates = (), ((), (), ())
    if quick:
        gates = ((weights.own,), weights.far, tuple(weights.pair[0][3:]))
    for start, stop, deps in zip(cuts[:-1], cuts[1:], gates):
        before = attention_forward(
            parts, heads, triple, others, mask_trunk, mask_group, start, stop, before, deps
        )
    mixed, lse = before
    seed_rows = place.to_tree(place.tree_sources(after(seed_moved, mixed)))
    middle, second = project_out(mixed, rows_low, weights.out, out_bias, ln2_gain, ln2_bias)
    outs = 4 if quick else 1
    lowered, second_grad, up_bias_grad, *pair_grads = feed_forward(
        weights.scalars, weights.pair, second, seed_rows, weights.bias_order(up_bias), outs
    )
    pair_mine, pair_theirs = pair_grads[:outs], pair_grads[outs:]
    up_bias_grad = weights.bias_back(up_bias_grad.reshape(-1))
    far = ()
    if quick:
        pair_swapped = {d: core_swap(place, pair_theirs[d]) for d in (3, 1, 2, 0)}
        far = far_sums(pair_mine, pair_swapped)
        received = far_sends(far)
    result, middle_grad, mixed_grad, sums, out_padded = middle_back(
        second_grad, lowered, middle, seed_rows, mixed, weights.out, ln2_gain, down_bias, far
    )
    out_bias_grad, gain_two, shift_two, down_bias_grad = sums[0], sums[1], sums[2], sums[3]

    turned = jnp.swapaxes(mask_trunk, 1, 2), jnp.swapaxes(mask_group, 1, 2)
    result_sources = place.from_tree_sources(result)
    result_parts = place.from_tree_parts(result_sources)
    result_out = place.swap_quarters(result_parts)
    cut = 5 * pairs // 9
    deps = (result_parts,)
    if quick:
        near = near_sums(pair_mine, pair_swapped, received)
        last = near_sends(near)
        deps += near
    inputs = parts, heads, triple, others, mixed, mixed_grad, lse, *turned
    grads = attention_backward(*inputs, 0, cut, (), deps)
    deps = ()
    if quick:
        last = after(last[0], grads[0]), last[1]
        total = row_total(pair_mine, pair_swapped, last)
        deps = (total,)
    grads = attention_backward(*inputs, cut, pairs, grads, deps)
    finish_deps, first_deps = (), ()
    if quick:
        blocks = pair_blocks(
            place.part.reshape(1).astype(jnp.int32), total, core_swap(place, total), weights.main, weights.rest
        )
        pair_parts = place.swap_quarters(blocks)
        finish_deps = (blocks,)
    else:
        up_grad, down_grad = weights.scatter_pair(pair_mine[0], pair_theirs[0])
    dq, dk, dv, dko, dvo = grads
    other_k, other_v = (
        jnp.concatenate(
            [
                lax.ppermute(part[(e - 1) * own_trunk : e * own_trunk], "col", place.part_perm(e))
                for e in range(1, parts)
            ],
            axis=0,
        )
        for part in (dko, dvo)
    )
    triple_grad, triple_sums = finish_gradients(own_trunk, dq, dk, dv, other_k, other_v, finish_deps)
    q_bias_grad = triple_sums[0, :width]
    v_bias_grad = triple_sums[0, 2 * padded : 2 * padded + width]
    input_grad, sums = first_back(
        triple_grad, rows_low, middle_grad, weights.triple, ln1_gain, first_deps
    )
    gain_one, shift_one = sums[0], sums[1]
    triple_weight_grad = dot_tn(first, triple_grad).astype(bf16)
    small = [
        gain_one, shift_one, q_bias_grad, v_bias_grad, out_bias_grad, gain_two, shift_two, up_bias_grad,
        down_bias_grad,
    ]
    if quick:
        up_grad, down_grad = weights.pair_final(pair_parts)
        flat = jnp.concatenate(small)
        flat = jnp.pad(flat, (0, -flat.shape[0] % 1024)).reshape(-1, 128)
        qkv_grad, out_grad, flat, input_grad_out = weights.end(
            triple_weight_grad, out_padded, flat, input_grad, block_input.shape, (up_grad, down_grad)
        )
        edges = np.cumsum([0] + [v.shape[0] for v in small])
        flat = flat.reshape(-1)
        small = [flat[low:high] for low, high in zip(edges[:-1], edges[1:])]
    else:
        qkv_grad, out_grad = weights.scatter_first(triple_weight_grad, out_padded)
        small = lax.psum(small, BOTH)
        input_grad_out = place.swap_quarters(
            place.from_tree_parts(place.from_tree_sources(input_grad))
        )
    return (
        result_out, input_grad_out, small[0], small[1], qkv_grad, small[2], small[3],
        out_grad, small[4], small[5], small[6], up_grad, small[7], down_grad, small[8],
    )


def solution(mesh):
    rows = P(None, BOTH, None)
    placed = (
        rows, P(None, None, "row"), P(), P(), P("row", "col"), P(), P(), P("row", "col"), P(),
        P(), P(), P("row", "col"), P(), P("col", "row"), P(), rows,
    )
    out = (
        rows, rows, P(), P(), P("row", "col"), P(), P(), P("row", "col"), P(),
        P(), P(), P("row", "col"), P(), P("col", "row"), P(),
    )
    return jax.shard_map(local, mesh=mesh, in_specs=placed, out_specs=out, check_vma=False)
```

```python
import math
from functools import partial

import jax
import jax.numpy as jnp
import numpy as np
from jax import lax
from jax.experimental import pallas as pl
from jax.experimental.pallas import tpu as pltpu
from jax.sharding import PartitionSpec as P

HEAD_DIM = 64
TRUNK = 1024
GROUP = 384
QT = 256
LOG2E = 1.4426950408889634
LN2 = 0.6931471805599453


def dot_nn(a, b):
    return jnp.dot(a, b, preferred_element_type=jnp.float32)


def dot_nt(a, b):
    return lax.dot_general(a, b, (((1,), (1,)), ((), ())), preferred_element_type=jnp.float32)


def dot_tn(a, b):
    return lax.dot_general(a, b, (((0,), (0,)), ((), ())), preferred_element_type=jnp.float32)


def lane_masks(head):
    lane = lax.broadcasted_iota(jnp.int32, (1, 128), 1)
    inside = (lane // HEAD_DIM) == head
    return inside, inside.astype(jnp.float32).astype(jnp.bfloat16), lane % HEAD_DIM


def fill_trunk(parts, own_ref, other_ref, out_ref):
    own = TRUNK // parts
    for tile in range(own // QT):
        for part in range(parts):
            rows = (
                own_ref[tile * QT : (tile + 1) * QT, :]
                if part == 0
                else other_ref[(part - 1) * own + tile * QT : (part - 1) * own + (tile + 1) * QT, :]
            )
            start = (tile * parts + part) * QT
            out_ref[start : start + QT, :] = rows


def fwd_kernel(parts, heads, start, extra, q_ref, k_ref, v_ref, ko_ref, vo_ref, mt_ref, mg_ref, *refs):
    o_ref, lse_ref, kt, vt, va = refs[extra:]
    pair = start + pl.program_id(0)
    own = TRUNK // parts
    tiles = own // QT
    groups = (TRUNK // 256) // parts
    fill_trunk(parts, k_ref, ko_ref, kt)
    fill_trunk(parts, v_ref, vo_ref, vt)
    o_ref[...] = jnp.zeros_like(o_ref)
    lse_ref[...] = jnp.zeros_like(lse_ref)

    def finish(rows, top, total, inside):
        turned = pltpu.roll(total, HEAD_DIM, 1)
        o_ref[rows, :] += jnp.where(inside, total / turned, 0.0).astype(jnp.bfloat16)
        lse_ref[rows, :] += jnp.where(inside, 0.0, top + jnp.log2(total))

    def head_body(head):
        inside, hm, _ = lane_masks(head)
        rest = 1 - hm
        va[...] = vt[...] * hm + rest
        for tile in range(tiles):
            rows = pl.ds(tile * QT, QT)
            q = q_ref[rows, :] * hm
            near = tile * parts * QT
            s_near = dot_nt(q, kt[near : near + parts * QT, :]) + mt_ref[tile]
            top = jnp.max(s_near, axis=1, keepdims=True)
            if tile > 0:
                s_far = dot_nt(q, kt[:near, :])
                top = jnp.maximum(top, jnp.max(s_far, axis=1, keepdims=True))
            p_near = jnp.exp2(s_near - top).astype(jnp.bfloat16)
            total = dot_nn(p_near, va[near : near + parts * QT, :])
            if tile > 0:
                total += dot_nn(jnp.exp2(s_far - top).astype(jnp.bfloat16), va[:near, :])
            finish(rows, top, total, inside)

        for group in range(groups):
            rows = pl.ds(own + group * GROUP, GROUP)
            q = q_ref[rows, :] * hm
            s_near = dot_nt(q, k_ref[rows, :]) + mg_ref[group]
            s_far = dot_nt(q, kt[...])
            top = jnp.maximum(
                jnp.max(s_near, axis=1, keepdims=True), jnp.max(s_far, axis=1, keepdims=True)
            )
            near = v_ref[rows, :] * hm + rest
            total = dot_nn(jnp.exp2(s_near - top).astype(jnp.bfloat16), near)
            total += dot_nn(jnp.exp2(s_far - top).astype(jnp.bfloat16), va[...])
            finish(rows, top, total, inside)

    head_body(0)
    pl.when(2 * pair + 1 < heads)(lambda: head_body(1))


def attention_forward(parts, heads, triple, others, mask_trunk, mask_group, start, stop, before=(), deps=()):
    fixed = 7
    aliases = {fixed + index: index for index in range(len(before))}
    deps = tuple(before) + tuple(deps)
    rows = triple.shape[0]
    pairs = triple.shape[1] // (3 * 128)
    extra = others.shape[0]
    block = lambda count, shift: pl.BlockSpec((count, 128), lambda i: (0, i + shift))
    whole = lambda shape: pl.BlockSpec(shape, lambda i: (0,) * len(shape))
    return pl.pallas_call(
        partial(fwd_kernel, parts, heads, start, len(deps)),
        grid=(stop - start,),
        in_specs=[
            block(rows, start),
            block(rows, start + pairs),
            block(rows, start + 2 * pairs),
            block(extra, start),
            block(extra, start + pairs),
            whole(mask_trunk.shape),
            whole(mask_group.shape),
        ]
        + [pl.BlockSpec(memory_space=pl.ANY)] * len(deps),
        out_specs=[block(rows, start)] * 2,
        input_output_aliases=aliases,
        out_shape=[
            jax.ShapeDtypeStruct((rows, pairs * 128), jnp.bfloat16),
            jax.ShapeDtypeStruct((rows, pairs * 128), jnp.float32),
        ],
        scratch_shapes=[
            pltpu.VMEM((TRUNK, 128), jnp.bfloat16),
            pltpu.VMEM((TRUNK, 128), jnp.bfloat16),
            pltpu.VMEM((TRUNK, 128), jnp.bfloat16),
        ],
        compiler_params=pltpu.CompilerParams(vmem_limit_bytes=48 * 1024 * 1024),
        cost_estimate=pl.CostEstimate(
            flops=(stop - start) * rows * 5_200_000, bytes_accessed=rows * pairs * 2000, transcendentals=0
        ),
        name="attention_forward",
    )(triple, triple, triple, others, others, mask_trunk, mask_group, *deps)


def split_three(value, place, outside):
    high = value.astype(jnp.bfloat16)
    left = value - high.astype(jnp.float32)
    middle = left.astype(jnp.bfloat16)
    low = (left - middle.astype(jnp.float32)).astype(jnp.bfloat16)
    high, middle, low = (v.astype(jnp.float32) for v in (high, middle, low))
    picked = jnp.where(place == 0, high, jnp.where(place == 1, middle, jnp.where(place == 2, low, 0.0)))
    return jnp.where(outside, picked, 0.0).astype(jnp.bfloat16)


def bwd_kernel(
    parts, heads, start, extra, q_ref, k_ref, v_ref, ko_ref, vo_ref, o_ref, do_ref, lse_ref, mt_ref, mg_ref,
    *refs,
):
    dq_ref, dk_ref, dv_ref, dko_ref, dvo_ref = refs[extra : extra + 5]
    kt, vt, ka, va, qa, da, qm, dm, dkt, dvt, dkg, dvg, dqs, kat = refs[extra + 5 :]
    pair = start + pl.program_id(0)
    own = TRUNK // parts
    tiles = own // QT
    groups = (TRUNK // 256) // parts
    rows_all = own + groups * GROUP
    fill_trunk(parts, k_ref, ko_ref, kt)
    fill_trunk(parts, v_ref, vo_ref, vt)
    dkt[...] = jnp.zeros_like(dkt)
    dvt[...] = jnp.zeros_like(dvt)
    dkg[...] = jnp.zeros_like(dkg)
    dvg[...] = jnp.zeros_like(dvg)
    dqs[...] = jnp.zeros_like(dqs)

    def head_body(head):
        inside, hm, place = lane_masks(head)
        rest = 1 - hm
        outside = jnp.logical_not(inside)
        ka[:TRUNK, :] = kt[...] * hm + rest
        va[:TRUNK, :] = vt[...] * hm + rest
        ka[TRUNK:, :] = k_ref[own:, :] * hm + rest
        va[TRUNK:, :] = v_ref[own:, :] * hm + rest

        kat[:, :TRUNK] = (kt[...] * hm).T
        kat[:, TRUNK:] = (k_ref[own:, :] * hm).T

        part = 256 if rows_all % 256 == 0 else 128
        for index in range(rows_all // part):
            rows = pl.ds(index * part, part)
            q = q_ref[rows, :] * hm
            d = do_ref[rows, :] * hm
            qm[rows, :] = q
            dm[rows, :] = d
            qa[rows, :] = q - split_three(lse_ref[rows, :], place, outside)
            delta = jnp.sum(
                d.astype(jnp.float32) * o_ref[rows, :].astype(jnp.float32), axis=1, keepdims=True
            )
            da[rows, :] = d - split_three(jnp.broadcast_to(delta, (part, 128)), place, outside)

        def step(rows, keys, mask, keep, dk, dv):
            st = dot_nt(ka[keys, :], qa[rows, :])
            if mask is not None:
                st = st + mask
            p = jnp.exp2(st)
            dp = dot_nt(va[keys, :], da[rows, :])
            ds = (p * dp).astype(jnp.bfloat16)
            dv[keep, :] += dot_nn(p.astype(jnp.bfloat16), dm[rows, :])
            dk[keep, :] += dot_nn(ds, qm[rows, :])
            dqs[:, rows] += dot_nn(kat[:, keys], ds)

        span = parts * QT
        for tile in range(tiles):
            rows = pl.ds(tile * QT, QT)
            for near in range(tile + 1):
                keys = pl.ds(near * span, span)
                step(rows, keys, mt_ref[tile] if near == tile else None, keys, dkt, dvt)
        step(pl.ds(own, groups * GROUP), pl.ds(0, TRUNK), None, pl.ds(0, TRUNK), dkt, dvt)
        for group in range(groups):
            step(
                pl.ds(own + group * GROUP, GROUP), pl.ds(TRUNK + group * GROUP, GROUP), mg_ref[group],
                pl.ds(group * GROUP, GROUP), dkg, dvg,
            )

    head_body(0)
    pl.when(2 * pair + 1 < heads)(lambda: head_body(1))
    dq_ref[...] = (dqs[...].T * HEAD_DIM**-0.5).astype(jnp.bfloat16)
    dk_ref[own:, :] = (dkg[...] * LN2).astype(jnp.bfloat16)
    dv_ref[own:, :] = dvg[...].astype(jnp.bfloat16)
    for tile in range(tiles):
        for part in range(parts):
            source = pl.ds((tile * parts + part) * QT, QT)
            if part == 0:
                dk_ref[tile * QT : (tile + 1) * QT, :] = (dkt[source, :] * LN2).astype(jnp.bfloat16)
                dv_ref[tile * QT : (tile + 1) * QT, :] = dvt[source, :].astype(jnp.bfloat16)
            else:
                start = (part - 1) * own + tile * QT
                dko_ref[start : start + QT, :] = (dkt[source, :] * LN2).astype(jnp.bfloat16)
                dvo_ref[start : start + QT, :] = dvt[source, :].astype(jnp.bfloat16)


def attention_backward(
    parts, heads, triple, others, mixed, mixed_grad, lse, mask_trunk, mask_group, start, stop, before=(), deps=()
):
    fixed = 10
    aliases = {fixed + index: index for index in range(len(before))}
    deps = tuple(before) + tuple(deps)
    rows = triple.shape[0]
    pairs = triple.shape[1] // (3 * 128)
    extra = others.shape[0]
    block = lambda count, shift: pl.BlockSpec((count, 128), lambda i: (0, i + shift))
    whole = lambda shape: pl.BlockSpec(shape, lambda i: (0,) * len(shape))
    near = rows - TRUNK // parts
    return pl.pallas_call(
        partial(bwd_kernel, parts, heads, start, len(deps)),
        grid=(stop - start,),
        in_specs=[
            block(rows, start),
            block(rows, start + pairs),
            block(rows, start + 2 * pairs),
            block(extra, start),
            block(extra, start + pairs),
            block(rows, start),
            block(rows, start),
            block(rows, start),
            whole(mask_trunk.shape),
            whole(mask_group.shape),
        ]
        + [pl.BlockSpec(memory_space=pl.ANY)] * len(deps),
        out_specs=[block(rows, start)] * 3 + [block(extra, start)] * 2,
        input_output_aliases=aliases,
        out_shape=[
            jax.ShapeDtypeStruct((rows, pairs * 128), jnp.bfloat16),
            jax.ShapeDtypeStruct((rows, pairs * 128), jnp.bfloat16),
            jax.ShapeDtypeStruct((rows, pairs * 128), jnp.bfloat16),
            jax.ShapeDtypeStruct((extra, pairs * 128), jnp.bfloat16),
            jax.ShapeDtypeStruct((extra, pairs * 128), jnp.bfloat16),
        ],
        scratch_shapes=[
            pltpu.VMEM((TRUNK, 128), jnp.bfloat16),
            pltpu.VMEM((TRUNK, 128), jnp.bfloat16),
            pltpu.VMEM((TRUNK + near, 128), jnp.bfloat16),
            pltpu.VMEM((TRUNK + near, 128), jnp.bfloat16),
            pltpu.VMEM((rows, 128), jnp.bfloat16),
            pltpu.VMEM((rows, 128), jnp.bfloat16),
            pltpu.VMEM((rows, 128), jnp.bfloat16),
            pltpu.VMEM((rows, 128), jnp.bfloat16),
            pltpu.VMEM((TRUNK, 128), jnp.float32),
            pltpu.VMEM((TRUNK, 128), jnp.float32),
            pltpu.VMEM((near, 128), jnp.float32),
            pltpu.VMEM((near, 128), jnp.float32),
            pltpu.VMEM((128, rows), jnp.float32),
            pltpu.VMEM((128, TRUNK + near), jnp.bfloat16),
        ],
        compiler_params=pltpu.CompilerParams(vmem_limit_bytes=56 * 1024 * 1024),
        cost_estimate=pl.CostEstimate(
            flops=(stop - start) * rows * 1_000_000, bytes_accessed=rows * pairs * 4000, transcendentals=0
        ),
        name="attention_backward",
    )(triple, triple, triple, others, others, mixed, mixed_grad, lse, mask_trunk, mask_group, *deps)


def normal_share(value):
    size = jnp.abs(value)
    turn = 1.0 / (1.0 + 0.23164189 * size)
    bell = jnp.exp2(value * value * -0.7213475204444817)
    poly = (((0.530702714 * turn - 0.726576013) * turn + 0.710706870) * turn - 0.142248368) * turn
    tail = (poly + 0.127414796) * turn * bell
    return jnp.where(value < 0, tail, 1.0 - tail), bell


FF_BLOCK = 256
ROW_CHUNK = 640


def join_tails(slabs, rows, up, down):
    rest = FF_BLOCK // len(slabs)
    for shift, target in ((0, up), (rest, down)):
        joined = jnp.concatenate([slab[:, shift : shift + rest] for slab in slabs], axis=1)
        target[rows, :] = joined.astype(jnp.bfloat16)


def plain_load(step, is_rest, scalars, refs, up, down):
    main, tails = refs

    @pl.when(jnp.logical_not(is_rest))
    def _():
        up[...] = main[0, 0, :, :FF_BLOCK]
        down[...] = main[0, 0, :, FF_BLOCK:]

    @pl.when(is_rest)
    def _():
        slabs = [tails[0, c].astype(jnp.float32) for c in range(tails.shape[1])]
        join_tails(slabs, slice(None), up, down)


def plain_specs(main):
    last = main.shape[1] - 1
    return [
        pl.BlockSpec((1, 1, main.shape[2], 2 * FF_BLOCK), lambda j, s: (0, jnp.minimum(j, last), 0, 0)),
        pl.BlockSpec(main.shape[:3] + (128,), lambda j, s: (0, 0, 0, 4)),
    ], [main, main]


def quick_load(step, is_rest, scalars, refs, up, down):
    role = scalars[0]
    bodies, tails = (refs[:5], refs[5:10]), (refs[10:15], refs[15:20])
    height = bodies[0][0].shape[1]
    spot = lambda d: pl.ds(pl.multiple_of(scalars[1 + d], 16), height)
    low_quarter = (step % 8) // 2 < 2

    def place(pieces):
        def put(d, piece):
            up[spot(d), :] = piece[0, :, :FF_BLOCK]
            down[spot(d), :] = piece[0, :, FF_BLOCK:]

        for d in range(3):
            put(d, pieces[d])
        pl.when(low_quarter)(lambda: put(3, pieces[3]))
        pl.when(jnp.logical_not(low_quarter))(lambda: put(3, pieces[4]))

    use_mine = jnp.logical_and(step // 8 == role, jnp.logical_not(is_rest))
    use_theirs = jnp.logical_and(step // 8 == 1 - role, jnp.logical_not(is_rest))
    pl.when(use_mine)(lambda: place(bodies[0]))
    pl.when(use_theirs)(lambda: place(bodies[1]))

    def rest(order):
        for d in range(4):
            slabs = []
            for which in order:
                pieces = tails[which]
                for q in range(4):
                    piece = pieces[d][q] if d < 3 else (pieces[3][q] if q < 2 else pieces[4][q - 2])
                    slabs.append(piece.astype(jnp.float32))
            join_tails(slabs, spot(d), up, down)

    pl.when(jnp.logical_and(is_rest, role == 0))(lambda: rest((0, 1)))
    pl.when(jnp.logical_and(is_rest, role != 0))(lambda: rest((1, 0)))


def quick_specs(mine, theirs):
    def body(shape, which, low, high):
        def index(j, s):
            turn = jnp.clip(j - 8 * (s[0] if which == 0 else 1 - s[0]), 0, 7)
            return (jnp.clip(turn // 2, low, high) - low, 0, turn % 2)

        return pl.BlockSpec((1, shape[1], 2 * FF_BLOCK), index)

    spans = ((0, 3), (0, 3), (0, 3), (0, 1), (2, 3))
    bodies = [
        body(piece.shape, which, *span)
        for which, pieces in enumerate((mine, theirs))
        for piece, span in zip(pieces, spans)
    ]
    tails = [
        pl.BlockSpec(piece.shape[:2] + (128,), lambda j, s: (0, 0, 8))
        for pieces in (mine, theirs)
        for piece in pieces
    ]
    arrays = list(mine) + list(theirs)
    return bodies + tails, arrays * 2


def ffn_kernel(load, held, outs, chunk, scalars, *refs):
    weights, refs = refs[:held], refs[held:]
    second, seed, bias = refs[:3]
    lowered, second_grad, bias_grad = refs[3:6]
    mine_grads, theirs_grads = refs[6 : 6 + outs], refs[6 + outs : 6 + 2 * outs]
    up, down, act, wide, up_grad, down_grad, second_t, seed_t = refs[6 + 2 * outs :]
    step = pl.program_id(0)
    role = scalars[0]
    load(step, step == pl.num_programs(0) - 1, scalars, weights, up, down)

    @pl.when(step == 0)
    def _():
        lowered[...] = jnp.zeros_like(lowered)
        second_grad[...] = jnp.zeros_like(second_grad)
        for start in range(0, second.shape[0], 128):
            rows = pl.ds(start, 128)
            second_t[:, rows] = second[rows, :].T
            seed_t[:, rows] = seed[rows, :].T

    total = jnp.zeros((1, FF_BLOCK), jnp.float32)
    for start in range(0, second.shape[0], chunk):
        rows = pl.ds(start, chunk)
        wide_in = dot_nn(second[rows, :], up[...]) + bias[...]
        hidden = dot_nn(seed[rows, :], down[...])
        share, bell = normal_share(wide_in)
        act_now = (wide_in * share).astype(jnp.bfloat16)
        slope = share + wide_in * (bell * 0.3989422804014327)
        wide_now = (hidden * slope).astype(jnp.bfloat16)
        total += jnp.sum(wide_now.astype(jnp.float32), axis=0, keepdims=True)
        act[rows, :] = act_now
        wide[rows, :] = wide_now
        lowered[rows, :] += dot_nt(act_now, down[...])
        second_grad[rows, :] += dot_nt(wide_now, up[...])
    bias_grad[...] = total
    up_grad[...] = dot_nn(second_t[...], wide[...]).astype(jnp.bfloat16)
    down_grad[...] = dot_nn(seed_t[...], act[...]).astype(jnp.bfloat16)

    def deliver(first_grad, second_grad):
        for index in range(outs):
            size = mine_grads[index].shape[0]
            rows = pl.ds(pl.multiple_of(scalars[1 + index], 16), size)
            mine_grads[index][...] = first_grad[rows, :]
            theirs_grads[index][...] = second_grad[rows, :]

    @pl.when(role == 0)
    def _():
        deliver(up_grad, down_grad)

    @pl.when(role != 0)
    def _():
        deliver(down_grad, up_grad)


def feed_forward(scalars, pair, second, seed, bias, outs):
    rows, width = second.shape
    hidden = bias.shape[0]
    quick = len(pair) == 2
    specs, arrays = quick_specs(*pair) if quick else plain_specs(*pair)
    load = quick_load if quick else plain_load
    whole = lambda shape: pl.BlockSpec(shape, lambda j, s: (0, 0))
    grad_spec = pl.BlockSpec((width // outs, FF_BLOCK), lambda j, s: (0, j))
    grad_shape = jax.ShapeDtypeStruct((width // outs, hidden), jnp.bfloat16)
    line = pl.BlockSpec((1, FF_BLOCK), lambda j, s: (0, j))
    chunk = ROW_CHUNK if rows % ROW_CHUNK == 0 else rows // 2
    return pl.pallas_call(
        partial(ffn_kernel, load, len(specs), outs, chunk),
        grid_spec=pltpu.PrefetchScalarGridSpec(
            num_scalar_prefetch=1,
            grid=(hidden // FF_BLOCK,),
            in_specs=specs + [
                whole((rows, width)), whole((rows, width)), line,
            ],
            out_specs=[whole((rows, width)), whole((rows, width)), line] + [grad_spec] * (2 * outs),
            scratch_shapes=[
                pltpu.VMEM((width, FF_BLOCK), jnp.bfloat16),
                pltpu.VMEM((width, FF_BLOCK), jnp.bfloat16),
                pltpu.VMEM((rows, FF_BLOCK), jnp.bfloat16),
                pltpu.VMEM((rows, FF_BLOCK), jnp.bfloat16),
                pltpu.VMEM((width, FF_BLOCK), jnp.bfloat16),
                pltpu.VMEM((width, FF_BLOCK), jnp.bfloat16),
                pltpu.VMEM((width, rows), jnp.bfloat16),
                pltpu.VMEM((width, rows), jnp.bfloat16),
            ],
        ),
        out_shape=[
            jax.ShapeDtypeStruct((rows, width), jnp.float32),
            jax.ShapeDtypeStruct((rows, width), jnp.float32),
            jax.ShapeDtypeStruct((1, hidden), jnp.float32),
        ]
        + [grad_shape] * (2 * outs),
        compiler_params=pltpu.CompilerParams(vmem_limit_bytes=60 * 1024 * 1024),
        cost_estimate=pl.CostEstimate(
            flops=24 * rows * width * hidden, bytes_accessed=8 * width * hidden + 20 * rows * width,
            transcendentals=rows * hidden,
        ),
        name="feed_forward",
    )(scalars, *arrays, second, seed, bias.reshape(1, hidden))


MESH = pl.DeviceIdType.MESH
HOLD = pl.BlockSpec(memory_space=pl.ANY)


def greet(peers):
    barrier = pltpu.get_barrier_semaphore()
    for peer in peers:
        pl.semaphore_signal(barrier, inc=1, device_id=peer, device_id_type=MESH)
    pl.semaphore_wait(barrier, len(peers))


def remote(source, target, send, receive, device):
    return pltpu.make_async_remote_copy(
        src_ref=source, dst_ref=target, send_sem=send, recv_sem=receive,
        device_id=device, device_id_type=MESH,
    )


def chunk_home(chunk):
    block = chunk // 2
    turn = block % 4
    in_trunk = chunk < 16
    owner = jnp.where(in_trunk, ((turn + 1) // 2) % 2, (chunk - 16) // 12)
    spot = jnp.where(
        in_trunk, 2 * (2 * (block // 4) + turn // 2) + chunk % 2, 8 + (chunk - 16) % 12
    )
    return owner, spot


def start_kernel(grain, pack, later_pack, value, full, rows, later_out, z_send, z_recv, r_send, r_recv, c_send, c_recv,
                 x_send, x_recv, own_sem, later_sem):
    row, col = lax.axis_index("row"), lax.axis_index("col")
    z, core = col // 2, col % 2
    at = lambda r, c: (r, c)
    peers = [at(row, (col + shift) % 8) for shift in range(1, 8)] + [at(row ^ 1, col), at(row ^ 2, col)]
    greet(peers)
    later_copy = pltpu.make_async_copy(later_pack, later_out, later_sem)
    later_copy.start()
    here = full.at[core, row, z]
    own = pltpu.make_async_copy(pack, here, own_sem)
    own.start()
    sends = []
    for d in range(1, 4):
        copy = remote(pack, here, z_send.at[d - 1], z_recv.at[d - 1], at(row, (z ^ d) * 2 + core))
        copy.start()
        sends.append(copy)
    own.wait()
    for copy in sends:
        copy.wait_recv()
    later = []

    def pass_on(index, ref, device, send=r_send, receive=r_recv):
        copy = remote(ref, ref, send.at[index], receive.at[index], device)
        copy.start()
        later.append(copy)
        return copy

    beside = pass_on(0, full.at[core, row], at(row ^ 1, col))
    below = pass_on(1, full.at[core, row], at(row ^ 2, col))
    swaps = [pass_on(0, full.at[core, row], at(row, col ^ 1), c_send, c_recv)]

    each = value.shape[1] // grain

    def each_chunk(act_remote, act_own):
        for m in range(4):
            for i in range(each):
                owner, spot = chunk_home(col * each + i)
                source = value.at[m, pl.ds(i * grain, grain), :]
                target = rows.at[pl.ds(pl.multiple_of(spot * grain, grain), grain), :]
                same = jnp.logical_and(z == m, owner == core)
                index = m * each + i

                @pl.when(jnp.logical_not(same))
                def _():
                    act_remote(
                        remote(source, target, x_send.at[index], x_recv, at(row, 2 * m + owner))
                    )

                if act_own:

                    @pl.when(same)
                    def _():
                        pltpu.make_async_copy(source, target, x_recv).start()

    each_chunk(lambda copy: copy.start(), True)
    beside.wait_recv()
    far_a = pass_on(2, full.at[core, row ^ 1, pl.ds(0, 2)], at(row ^ 2, col))
    swaps.append(pass_on(1, full.at[core, row ^ 1], at(row, col ^ 1), c_send, c_recv))
    below.wait_recv()
    far_b = pass_on(3, full.at[core, row ^ 2, pl.ds(2, 2)], at(row ^ 1, col))
    swaps.append(pass_on(2, full.at[core, row ^ 2], at(row, col ^ 1), c_send, c_recv))
    far_a.wait_recv()
    far_b.wait_recv()
    swaps.append(pass_on(3, full.at[core, row ^ 3], at(row, col ^ 1), c_send, c_recv))
    for copy in swaps:
        copy.wait_recv()
    pltpu.make_async_copy(rows, rows, x_recv).wait()
    later_copy.wait()
    for copy in sends + later:
        copy.wait_send()
    each_chunk(lambda copy: copy.wait_send(), False)


def start_exchange(pack, later_pack, value, count):
    grain = 64
    height, lanes = pack.shape
    copies = 4 * (value.shape[1] // grain)
    dma = lambda n: pltpu.SemaphoreType.DMA((n,))
    return pl.pallas_call(
        partial(start_kernel, grain),
        in_specs=[HOLD] * 3,
        out_specs=[HOLD] * 3,
        out_shape=[
            jax.ShapeDtypeStruct((2, 4, 4, height, lanes), pack.dtype),
            jax.ShapeDtypeStruct((count, value.shape[2]), value.dtype),
            jax.ShapeDtypeStruct(later_pack.shape, later_pack.dtype),
        ],
        scratch_shapes=[
            dma(3), dma(3), dma(4), dma(4), dma(4), dma(4), dma(copies),
            pltpu.SemaphoreType.DMA, pltpu.SemaphoreType.DMA, pltpu.SemaphoreType.DMA,
        ],
        compiler_params=pltpu.CompilerParams(collective_id=0, has_side_effects=True),
        cost_estimate=pl.CostEstimate(flops=100_000_000_000, bytes_accessed=0, transcendentals=0),
        name="start_exchange",
    )(pack, later_pack, value)


def end_kernel(
    grain, grads, small, rows, *refs,
):
    final, small_out, tokens, mine, swapped, far, beside, below, tail, small_col, small_row, part = refs[-26:-14]
    own_sem, c_send, c_recv, r_send, r_recv, z_send, z_recv, s_send, s_recv, t_send, t_recv, _, x_send, x_recv = refs[-14:]
    row, col = lax.axis_index("row"), lax.axis_index("col")
    z, core = col // 2, col % 2
    at = lambda r, c: (r, c)
    peers = [at(row, (col + shift) % 8) for shift in range(1, 8)]
    peers += [at(row ^ d, col) for d in range(1, 4)]
    greet(peers)
    own = pltpu.make_async_copy(grads.at[core], mine, own_sem)
    own.start()
    sends = []
    for d in (3, 1, 2, 0):
        copy = remote(
            grads.at[1 - core, row ^ d], swapped.at[row ^ d], c_send.at[d], c_recv.at[d], at(row, col ^ 1)
        )
        copy.start()
        sends.append(copy)
    for shift in range(1, 8):
        copy = remote(
            small, small_col.at[col], s_send.at[shift - 1], s_recv.at[7 - shift], at(row, (col + shift) % 8)
        )
        copy.start()
        sends.append(copy)
    small_col[col] = small[...]
    f32 = jnp.float32
    each = tokens.shape[1] // grain

    def each_chunk(act_remote, act_own):
        for local in range(rows.shape[0] // grain):
            pair = local // 2
            turn = 4 * (pair // 2) + (core if pair % 2 == 0 else 3 - core)
            chunk = 2 * turn + local % 2 if local < 8 else 16 + 12 * core + local - 8
            shard = chunk // each
            source = rows.at[pl.ds(local * grain, grain), :]
            start = pl.multiple_of((chunk % each) * grain, grain)
            target = tokens.at[z, pl.ds(start, grain), :]

            @pl.when(shard != col)
            def _():
                act_remote(remote(source, target, x_send.at[local], x_recv, at(row, shard)))

            if act_own:

                @pl.when(shard == col)
                def _():
                    pltpu.make_async_copy(source, target, x_recv).start()

    each_chunk(lambda copy: copy.start(), True)
    own.wait()

    def add(target, source):
        target[...] = (target[...].astype(f32) + source[...].astype(f32)).astype(target.dtype)

    def add_swapped(position):
        sends[position].wait_recv()
        d = (3, 1, 2, 0)[position]
        for q in range(4):
            add(mine.at[row ^ d, q], swapped.at[row ^ d, q])

    def send(index, source, target, device):
        copy = remote(source, target, r_send.at[index], r_recv.at[index], device)
        copy.start()
        sends.append(copy)
        return copy

    add_swapped(0)
    far_a = send(0, mine.at[row ^ 3, pl.ds(0, 2)], far.at[pl.ds(0, 2)], at(row ^ 2, col))
    far_b = send(1, mine.at[row ^ 3, pl.ds(2, 2)], far.at[pl.ds(2, 2)], at(row ^ 1, col))
    add_swapped(1)
    x_b = send(2, mine.at[row ^ 1, pl.ds(2, 2)], beside.at[pl.ds(2, 2)], at(row ^ 1, col))
    add_swapped(2)
    y_a = send(3, mine.at[row ^ 2, pl.ds(0, 2)], below.at[pl.ds(0, 2)], at(row ^ 2, col))
    add_swapped(3)
    for shift in range(1, 8):
        sends[3 + shift].wait_recv()
    part[...] = small_col[0]
    for c in range(1, 8):
        part[...] += small_col[c]
    rounds = []
    for d in range(1, 4):
        copy = remote(part, small_row.at[row], t_send.at[d - 1], t_recv.at[d - 1], at(row ^ d, col))
        copy.start()
        rounds.append(copy)
    small_row[row] = part[...]
    far_a.wait_recv()
    for q in (0, 1):
        add(mine.at[row ^ 1, q], far.at[q])
    x_a = send(4, mine.at[row ^ 1, pl.ds(0, 2)], beside.at[pl.ds(0, 2)], at(row ^ 1, col))
    far_b.wait_recv()
    for q in (2, 3):
        add(mine.at[row ^ 2, q], far.at[q])
    y_b = send(5, mine.at[row ^ 2, pl.ds(2, 2)], below.at[pl.ds(2, 2)], at(row ^ 2, col))
    for copy in (x_b, y_a, x_a, y_b):
        copy.wait_recv()

    def total(q):
        return (
            mine[row, q].astype(f32) + beside[q].astype(f32) + below[q].astype(f32)
        )

    lasts = []
    for d in range(1, 4):
        q = z ^ d
        mine[row, q] = total(q).astype(mine.dtype)
        copy = remote(
            mine.at[row, q], tail.at[d - 1], z_send.at[d - 1], z_recv.at[d - 1], at(row, q * 2 + core)
        )
        copy.start()
        lasts.append(copy)
    result = total(z)
    for d in range(1, 4):
        lasts[d - 1].wait_recv()
        result = result + tail[d - 1].astype(f32)
    final[...] = result
    for copy in rounds:
        copy.wait_recv()
    pltpu.make_async_copy(tokens, tokens, x_recv).wait()
    each_chunk(lambda copy: copy.wait_send(), False)
    small_out[...] = small_row[0] + small_row[1] + small_row[2] + small_row[3]
    for copy in sends + lasts + rounds:
        copy.wait_send()


def end_exchange(grads, small, rows, shape, deps):
    grain = 64
    height, lanes = grads.shape[3:]
    slab = lambda *n: pltpu.VMEM(n + (height, lanes), grads.dtype)
    dma = lambda n: pltpu.SemaphoreType.DMA((n,))
    return pl.pallas_call(
        partial(end_kernel, grain),
        in_specs=[HOLD, pl.BlockSpec(memory_space=pltpu.VMEM), HOLD] + [HOLD] * len(deps),
        out_specs=[pl.BlockSpec(memory_space=pltpu.VMEM)] * 2 + [HOLD],
        out_shape=[
            jax.ShapeDtypeStruct((height, lanes), jnp.float32),
            jax.ShapeDtypeStruct(small.shape, jnp.float32),
            jax.ShapeDtypeStruct(shape, rows.dtype),
        ],
        scratch_shapes=[
            slab(4, 4), slab(4, 4), slab(4), slab(4), slab(4), slab(3),
            pltpu.VMEM((8,) + small.shape, jnp.float32), pltpu.VMEM((4,) + small.shape, jnp.float32),
            pltpu.VMEM(small.shape, jnp.float32),
            pltpu.SemaphoreType.DMA, dma(4), dma(4), dma(6), dma(6), dma(3), dma(3),
            dma(7), dma(7), dma(3), dma(3), dma(1), dma(rows.shape[0] // grain), pltpu.SemaphoreType.DMA,
        ],
        compiler_params=pltpu.CompilerParams(
            collective_id=1, has_side_effects=True, vmem_limit_bytes=40 * 1024 * 1024
        ),
        cost_estimate=pl.CostEstimate(flops=100_000_000_000, bytes_accessed=0, transcendentals=0),
        name="end_exchange",
    )(grads, small, rows, *deps)


def lane_runs(width, padded, columns, qkv_cols, out_cols):
    runs = []
    for c in range(columns):
        start = c * qkv_cols
        while start < (c + 1) * qkv_cols:
            third = start // width
            stop = min((c + 1) * qkv_cols, (third + 1) * width)
            runs.append((0, third * padded + start - third * width, c, start - c * qkv_cols, stop - start))
            start = stop
        runs.append((1, c * out_cols, c, qkv_cols, out_cols))
    return runs


def assemble_kernel(runs, width, padded, full, triple, out):
    step = pl.program_id(0)
    height = full.shape[3]
    columns = 2 * full.shape[2]
    slabs = [full[c % 2, 0, c // 2].astype(jnp.float32) for c in range(columns)]
    piece = lambda run: slabs[run[2]][:, run[3] : run[3] + run[4]]
    gap = jnp.zeros((height, padded - width), jnp.float32)

    def line(which, third):
        low, high = third * padded, third * padded + padded
        chosen = [r for r in runs if r[0] == which and low <= r[1] < high]
        return jnp.concatenate([piece(r) for r in chosen] + [gap], axis=1).astype(triple.dtype)

    for third in range(3):
        triple[:, third * padded : (third + 1) * padded] = line(0, third)

    @pl.when(step == 0)
    def _():
        out[width:, :] = jnp.zeros((padded - width, padded), out.dtype)

    out[pl.ds(pl.multiple_of(step * height, 16), height), :] = line(1, 0)


def assemble(full, width, padded, qkv_cols):
    height, lanes = full.shape[3:]
    runs = lane_runs(width, padded, 2 * full.shape[2], qkv_cols, lanes - qkv_cols)
    return pl.pallas_call(
        partial(assemble_kernel, runs, width, padded),
        grid=(full.shape[1],),
        in_specs=[pl.BlockSpec((2, 1, full.shape[2], height, lanes), lambda r: (0, r, 0, 0, 0))],
        out_specs=[
            pl.BlockSpec((height, 3 * padded), lambda r: (r, 0)),
            pl.BlockSpec((padded, padded), lambda r: (0, 0)),
        ],
        out_shape=[
            jax.ShapeDtypeStruct((width, 3 * padded), full.dtype),
            jax.ShapeDtypeStruct((padded, padded), full.dtype),
        ],
        compiler_params=pltpu.CompilerParams(vmem_limit_bytes=48 * 1024 * 1024),
        cost_estimate=pl.CostEstimate(flops=12_000_000_000, bytes_accessed=0, transcendentals=0),
        name="assemble_weights",
    )(full)


def divide_kernel(runs, triple, out, full):
    wide = triple[...].astype(jnp.float32)
    last = out[...].astype(jnp.float32)
    for c in range(2 * full.shape[2]):
        parts = [
            (wide, last)[r[0]][:, r[1] : r[1] + r[4]] for r in runs if r[2] == c
        ]
        full[c % 2, 0, c // 2] = jnp.concatenate(parts, axis=1).astype(full.dtype)


def divide(triple, out, width, padded, qkv_cols, out_cols, columns, rows):
    height, lanes = width // rows, qkv_cols + out_cols
    runs = lane_runs(width, padded, columns, qkv_cols, out_cols)
    return pl.pallas_call(
        partial(divide_kernel, runs),
        grid=(rows,),
        in_specs=[
            pl.BlockSpec((height, 3 * padded), lambda r: (r, 0)),
            pl.BlockSpec((height, out.shape[1]), lambda r: (r, 0)),
        ],
        out_specs=pl.BlockSpec((2, 1, columns // 2, height, lanes), lambda r: (0, r, 0, 0, 0)),
        out_shape=jax.ShapeDtypeStruct((2, rows, columns // 2, height, lanes), jnp.bfloat16),
        compiler_params=pltpu.CompilerParams(vmem_limit_bytes=48 * 1024 * 1024),
        cost_estimate=pl.CostEstimate(flops=1_000_000_000, bytes_accessed=0, transcendentals=0),
        name="divide_gradients",
    )(triple, out)


def finish_kernel(own_trunk, dq, dk, dv, other_k, other_v, *refs):
    total, sums = refs[-2:]
    step = pl.program_id(0)
    each = pl.num_programs(0) // 3

    def deliver(value):
        total[...] = value
        sums[...] = jnp.sum(value.astype(jnp.float32), axis=0, keepdims=True)

    @pl.when(step < each)
    def _():
        deliver(dq[...])

    for index, (near, far) in enumerate(((dk, other_k), (dv, other_v))):

        @pl.when(step // each == index + 1)
        def _():
            value = near[:own_trunk, :].astype(jnp.float32)
            for start in range(0, far.shape[0], own_trunk):
                value = value + far[start : start + own_trunk, :].astype(jnp.float32)
            deliver(jnp.concatenate([value.astype(total.dtype), near[own_trunk:, :]], axis=0))


def finish_gradients(own_trunk, dq, dk, dv, other_k, other_v, deps):
    rows, padded = dq.shape
    block = 384
    each = padded // block

    def spec(count, third):
        return pl.BlockSpec((count, block), lambda j: (0, jnp.clip(j - third * each, 0, each - 1)))

    return pl.pallas_call(
        partial(finish_kernel, own_trunk),
        grid=(3 * each,),
        in_specs=[
            spec(rows, 0), spec(rows, 1), spec(rows, 2), spec(other_k.shape[0], 1), spec(other_v.shape[0], 2),
        ]
        + [HOLD] * len(deps),
        out_specs=[
            pl.BlockSpec((rows, block), lambda j: (0, j)), pl.BlockSpec((1, block), lambda j: (0, j)),
        ],
        out_shape=[
            jax.ShapeDtypeStruct((rows, 3 * padded), jnp.bfloat16),
            jax.ShapeDtypeStruct((1, 3 * padded), jnp.float32),
        ],
        compiler_params=pltpu.CompilerParams(vmem_limit_bytes=48 * 1024 * 1024),
        cost_estimate=pl.CostEstimate(flops=1_000_000_000, bytes_accessed=0, transcendentals=0),
        name="finish_gradients",
    )(dq, dk, dv, other_k, other_v, *deps)


def norm_parts(value):
    center = value - jnp.mean(value, axis=-1, keepdims=True)
    scale = lax.rsqrt(jnp.mean(center * center, axis=-1, keepdims=True) + 1e-05)
    return center * scale, scale


def norm_back(grad, value, gain):
    unit, scale = norm_parts(value)
    scaled = grad * gain
    back = scaled - jnp.mean(scaled, axis=-1, keepdims=True)
    back = scale * (back - unit * jnp.mean(scaled * unit, axis=-1, keepdims=True))
    return back, jnp.sum(grad * unit, axis=0, keepdims=True), jnp.sum(grad, axis=0, keepdims=True)


def out_kernel(mixed, weight, bias, rows, gain, shift, middle, second):
    width = rows.shape[1]
    attended = dot_nn(mixed[...], weight[...])[:, :width] + bias[...]
    total = rows[...].astype(jnp.float32) + attended.astype(jnp.bfloat16).astype(jnp.float32)
    middle[...] = total
    unit, _ = norm_parts(total)
    second[...] = (unit * gain[...] + shift[...]).astype(jnp.bfloat16)


def by_rows(kernel, name, count, chunked, fixed, outs, sums=(), scratch=(), flops=0, deps=()):
    chunk = count // 5
    block = lambda width: pl.BlockSpec((chunk, width), lambda i: (i, 0))
    whole = lambda shape: pl.BlockSpec(shape, lambda i: (0,) * len(shape))
    return pl.pallas_call(
        kernel,
        grid=(5,),
        in_specs=[block(v.shape[1]) for v in chunked] + [whole(v.shape) for v in fixed]
        + [HOLD] * len(deps),
        out_specs=[block(width) for width, _ in outs] + [whole(shape) for shape, _ in sums],
        out_shape=[jax.ShapeDtypeStruct((count, width), dtype) for width, dtype in outs]
        + [jax.ShapeDtypeStruct(shape, dtype) for shape, dtype in sums],
        scratch_shapes=list(scratch),
        compiler_params=pltpu.CompilerParams(vmem_limit_bytes=56 * 1024 * 1024),
        cost_estimate=pl.CostEstimate(flops=flops, bytes_accessed=0, transcendentals=0),
        name=name,
    )(*chunked, *fixed, *deps)


def project_out(mixed, rows, weight, bias, gain, shift):
    width = rows.shape[1]

    def kernel(mixed, rows, weight, bias, gain, shift, middle, second):
        out_kernel(mixed, weight, bias, rows, gain, shift, middle, second)

    line = lambda v: v.reshape(1, width)
    return by_rows(
        kernel, "project_out", rows.shape[0], (mixed, rows), (weight, line(bias), line(gain), line(shift)),
        ((width, jnp.float32), (width, jnp.bfloat16)), flops=12_000_000_000,
    )


def middle_kernel(held, second_grad, lowered, middle, seed, mixed, weight, gain, down_bias, *refs):
    result, middle_grad, mixed_grad, sums, out_grad, total = refs[held:]
    step = pl.program_id(0)
    width = middle.shape[1]
    value, up = middle[...], seed[...].astype(jnp.float32)
    result[...] = (value + lowered[...] + down_bias[...]).astype(jnp.bfloat16)
    back, gain_sum, shift_sum = norm_back(second_grad[...], value, gain[...])
    grad = up + back
    middle_grad[...] = grad
    low = grad.astype(jnp.bfloat16)
    mixed_grad[...] = dot_nt(low, weight[:, :width]).astype(jnp.bfloat16)
    part = dot_tn(mixed[...], low)
    low_sum = jnp.sum(low.astype(jnp.float32), axis=0, keepdims=True)
    up_sum = jnp.sum(up, axis=0, keepdims=True)
    lines = jnp.concatenate([low_sum, gain_sum, shift_sum, up_sum], axis=0)

    @pl.when(step == 0)
    def _():
        sums[...] = lines
        total[...] = part

    @pl.when(step > 0)
    def _():
        sums[...] += lines
        total[...] += part

    @pl.when(step == pl.num_programs(0) - 1)
    def _():
        out_grad[:, :width] = total[:width, :].astype(jnp.bfloat16)
        out_grad[:, width:] = jnp.zeros((width, out_grad.shape[1] - width), jnp.bfloat16)


def middle_back(second_grad, lowered, middle, seed, mixed, weight, gain, down_bias, deps):
    rows, width = middle.shape
    padded = weight.shape[0]
    line = lambda v: v.reshape(1, width)
    return by_rows(
        partial(middle_kernel, len(deps)), "middle_back", rows, (second_grad, lowered, middle, seed, mixed),
        (weight, line(gain), line(down_bias)),
        ((width, jnp.bfloat16), (width, jnp.float32), (padded, jnp.bfloat16)),
        (((4, width), jnp.float32), ((width, padded), jnp.bfloat16)),
        (pltpu.VMEM((padded, width), jnp.float32),), flops=25_000_000_000, deps=deps,
    )


def first_kernel(held, triple_grad, rows, middle_grad, weight, gain, *refs):
    input_grad, sums = refs[held:]
    step = pl.program_id(0)
    grad = dot_nt(triple_grad[...], weight[...])
    back, gain_sum, shift_sum = norm_back(grad, rows[...].astype(jnp.float32), gain[...])
    input_grad[...] = (middle_grad[...] + back).astype(jnp.bfloat16)
    lines = jnp.concatenate([gain_sum, shift_sum], axis=0)

    @pl.when(step == 0)
    def _():
        sums[...] = lines

    @pl.when(step > 0)
    def _():
        sums[...] += lines


def first_back(triple_grad, rows, middle_grad, weight, gain, deps):
    count, width = rows.shape
    return by_rows(
        partial(first_kernel, len(deps)), "first_back", count, (triple_grad, rows, middle_grad), (weight, gain.reshape(1, width)),
        ((width, jnp.bfloat16),), (((2, width), jnp.float32),), flops=4_000_000_000, deps=deps,
    )


def blocks_kernel(rest, core, total, other, total_tail, other_tail, out):
    quarter = pl.program_id(0)
    main = total.shape[1]
    out[0, :, :main] = total[...]
    out[0, :, main : 2 * main] = other[...]
    for shard in range(8):

        @pl.when(quarter + 4 * core[0] == shard)
        def _():
            cut = slice(shard * rest, (shard + 1) * rest)
            out[0, :, 2 * main : 2 * main + rest] = total_tail[:, cut]
            out[0, :, 2 * main + rest :] = other_tail[:, cut]


def pair_blocks(core, total, other, main, rest):
    rows = total.shape[0]
    spec = pl.BlockSpec((rows, main), lambda q, s: (0, q + 4 * s[0]))
    tail = pl.BlockSpec((rows, 8 * rest), lambda q, s: (0, main // rest))
    return pl.pallas_call(
        partial(blocks_kernel, rest),
        grid_spec=pltpu.PrefetchScalarGridSpec(
            num_scalar_prefetch=1,
            grid=(4,),
            in_specs=[spec, spec, tail, tail],
            out_specs=pl.BlockSpec((1, rows, 2 * (main + rest)), lambda q, s: (q, 0, 0)),
        ),
        out_shape=jax.ShapeDtypeStruct((4, rows, 2 * (main + rest)), total.dtype),
        cost_estimate=pl.CostEstimate(flops=1_000_000_000, bytes_accessed=0, transcendentals=0),
        name="pair_blocks",
    )(core, total, other, total, other)


def after(value, *deps):
    def kernel(*refs):
        pass

    return pl.pallas_call(
        kernel,
        in_specs=[HOLD] * (1 + len(deps)),
        out_specs=HOLD,
        out_shape=jax.ShapeDtypeStruct(value.shape, value.dtype),
        input_output_aliases={0: 0},
        name="after",
    )(value, *deps)


def order_kernel(table, *refs):
    pieces, out = refs[:-1], refs[-1]
    for index, piece in enumerate(pieces):
        out[table[index]] = piece[...]


def in_order(table, pieces):
    rows, width = pieces[0].shape
    whole = pl.BlockSpec((rows, width), lambda i, s: (0, 0))
    return pl.pallas_call(
        order_kernel,
        grid_spec=pltpu.PrefetchScalarGridSpec(
            num_scalar_prefetch=1,
            grid=(1,),
            in_specs=[whole] * len(pieces),
            out_specs=pl.BlockSpec((len(pieces), rows, width), lambda i, s: (0, 0, 0)),
        ),
        out_shape=jax.ShapeDtypeStruct((len(pieces), rows, width), pieces[0].dtype),
        compiler_params=pltpu.CompilerParams(vmem_limit_bytes=48 * 1024 * 1024),
        cost_estimate=pl.CostEstimate(flops=0, bytes_accessed=4 * len(pieces) * rows * width, transcendentals=0),
        name="in_order",
    )(table, *pieces)


def layer_norm(value, gain, bias):
    center = value - jnp.mean(value, axis=-1, keepdims=True)
    spread = jnp.mean(center * center, axis=-1, keepdims=True)
    return center * lax.rsqrt(spread + 1e-05) * gain + bias


def own_rows(parts, part):
    blocks = TRUNK // (128 * parts)
    starts = []
    for k in range(blocks):
        base = (k // 2) * 2 * parts
        starts.append(128 * (base + (part if k % 2 == 0 else 2 * parts - 1 - part)))
    rows = [np.arange(128) + s for s in starts]
    groups = (TRUNK // 256) // parts
    rows.append(TRUNK + part * groups * GROUP + np.arange(groups * GROUP))
    return np.concatenate(rows)


def spread_kernel(grain, table, *refs):
    pieces, out = refs[:-1], refs[-1]
    each = pieces[0].shape[0] // grain
    for index, piece in enumerate(pieces):
        for i in range(each):
            target = table[index * each + i]

            @pl.when(target >= 0)
            def _():
                rows = pl.ds(pl.multiple_of(target * grain, grain), grain)
                out[rows, :] = piece[i * grain : (i + 1) * grain, :]


def spread(table, pieces, grain, count):
    width = pieces[0].shape[1]
    whole = lambda rows: pl.BlockSpec((rows, width), lambda i, s: (0, 0))
    return pl.pallas_call(
        partial(spread_kernel, grain),
        grid_spec=pltpu.PrefetchScalarGridSpec(
            num_scalar_prefetch=1,
            grid=(1,),
            in_specs=[whole(p.shape[0]) for p in pieces],
            out_specs=whole(count),
        ),
        out_shape=jax.ShapeDtypeStruct((count, width), pieces[0].dtype),
        compiler_params=pltpu.CompilerParams(vmem_limit_bytes=48 * 1024 * 1024),
        cost_estimate=pl.CostEstimate(flops=0, bytes_accessed=6 * count * width, transcendentals=0),
        name="spread_rows",
    )(table, *pieces)


def collect_kernel(grain, count, table, *refs):
    sources, outs = refs[:-count], refs[-count:]
    each = outs[0].shape[0] // grain
    for index, out in enumerate(outs):
        for i in range(each):
            owner = table[2 * (index * each + i)]
            start = table[2 * (index * each + i) + 1]
            for which, source in enumerate(sources):

                @pl.when(owner == which)
                def _():
                    rows = pl.ds(pl.multiple_of(start * grain, grain), grain)
                    out[i * grain : (i + 1) * grain, :] = source[rows, :]


def collect(table, sources, grain, count, length):
    width = sources[0].shape[1]
    whole = lambda rows: pl.BlockSpec((rows, width), lambda i, s: (0, 0))
    return pl.pallas_call(
        partial(collect_kernel, grain, count),
        grid_spec=pltpu.PrefetchScalarGridSpec(
            num_scalar_prefetch=1,
            grid=(1,),
            in_specs=[whole(s.shape[0]) for s in sources],
            out_specs=[whole(length)] * count,
        ),
        out_shape=[jax.ShapeDtypeStruct((length, width), sources[0].dtype)] * count,
        compiler_params=pltpu.CompilerParams(vmem_limit_bytes=48 * 1024 * 1024),
        cost_estimate=pl.CostEstimate(flops=0, bytes_accessed=6 * count * length * width, transcendentals=0),
        name="collect_rows",
    )(table, *sources)


class Place:
    def __init__(self, micro, tree):
        self.columns = lax.axis_size("col")
        self.micro = micro
        self.parts = self.columns // micro
        self.tree = tree
        self.length = tree // self.columns
        self.grain = math.gcd(self.length, 128)
        me = lax.axis_index("col")
        self.quarter, self.part = me // self.parts, me % self.parts
        self.own = np.stack([own_rows(self.parts, part) for part in range(self.parts)])
        self.count = self.own.shape[1]

    def quarter_perm(self, shift):
        p = self.parts
        return [(c, ((c // p) ^ shift) * p + c % p) for c in range(self.columns)]

    def part_perm(self, shift):
        return [(c, c ^ shift) for c in range(self.columns)]

    def swap_quarters(self, value):
        groups = [
            [q * self.parts + part for q in range(self.micro)] for part in range(self.parts)
        ]
        return lax.all_to_all(value, "col", 0, 0, axis_index_groups=groups, tiled=True)

    def tree_sources(self, value):
        flat = (self.micro * self.length, value.shape[2])
        moved = [lax.ppermute(value, "col", self.part_perm(e)) for e in range(1, self.parts)]
        return [v.reshape(flat) for v in [value] + moved]

    def to_tree(self, sources):
        grain, each = self.grain, self.length // self.grain
        table = np.full((self.parts, self.tree // grain), -1, np.int32)
        for part in range(self.parts):
            table[part, self.own[part, ::grain] // grain] = np.arange(self.count // grain)
        mine = lax.dynamic_index_in_dim(jnp.asarray(table), self.part, 0, keepdims=False)
        e, rest = np.divmod(np.arange(self.tree // grain, dtype=np.int32), self.micro * each)
        quarter, inside = np.divmod(rest, each)
        chunk = (quarter * self.parts + (self.part ^ e)) * each + inside
        return spread(mine[chunk], sources, grain, self.count)

    def from_tree_sources(self, value):
        split = value.reshape(-1, self.grain, value.shape[1])
        moved = [lax.ppermute(split, "col", self.part_perm(e)) for e in range(1, self.parts)]
        return [value] + [v.reshape(value.shape) for v in moved]

    def from_tree_parts(self, sources):
        grain, each, parts = self.grain, self.length // self.grain, self.parts
        owner = np.zeros(self.tree // grain, np.int32)
        local = np.zeros(self.tree // grain, np.int32)
        for part in range(parts):
            owner[self.own[part, ::grain] // grain] = part
            local[self.own[part, ::grain] // grain] = np.arange(self.count // grain)
        quarter, inside = np.divmod(np.arange(self.micro * each, dtype=np.int32), each)
        chunk = (quarter * parts + self.part) * each + inside
        table = jnp.stack([jnp.asarray(owner)[chunk] ^ self.part, jnp.asarray(local)[chunk]], axis=1)
        (out,) = collect(table.reshape(-1), sources, grain, 1, self.micro * self.length)
        return out.reshape(self.micro, self.length, sources[0].shape[1])

    def masks(self, own_ids, parent_ids):
        parts = self.parts
        own = jnp.asarray(self.own, jnp.int32)
        mine = lax.dynamic_index_in_dim(own, self.part, 0, keepdims=False)
        trunk_rows = TRUNK // parts
        tiles = trunk_rows // QT
        trunk = []
        for tile in range(tiles):
            span = slice(tile * QT, (tile + 1) * QT)
            keys = jnp.concatenate(
                [
                    lax.dynamic_index_in_dim(own, self.part ^ e, 0, keepdims=False)[span]
                    for e in range(parts)
                ]
            )
            trunk.append(jnp.where(keys[None, :] <= mine[span][:, None], 0.0, -1e30))
        group = []
        groups = (TRUNK // 256) // parts
        places = jnp.arange(GROUP)
        for g in range(groups):
            start = TRUNK + (self.part * groups + g) * GROUP
            ids = lax.dynamic_slice_in_dim(own_ids, start, GROUP)
            parent = lax.dynamic_slice_in_dim(parent_ids, start, GROUP)
            seen = (places[None, :] <= places[:, None]) & (
                (ids[None, :] == 0) | (ids[None, :] == ids[:, None]) | (ids[None, :] == parent[:, None])
            )
            group.append(jnp.where(seen, 0.0, -1e30))
        return jnp.stack(trunk).astype(jnp.float32), jnp.stack(group).astype(jnp.float32)


BOTH = ("row", "col")
ROW_CUT = 144


def plain_gather(block):
    full = lax.all_gather(block, BOTH, axis=0, tiled=False)
    full = full.reshape(lax.axis_size("row"), lax.axis_size("col"), *block.shape)
    return full.transpose(0, 2, 1, 3).reshape(full.shape[0] * full.shape[2], full.shape[1] * full.shape[3])


def plain_scatter(grad):
    rows, cols = lax.axis_size("row"), lax.axis_size("col")
    blocks = grad.astype(jnp.bfloat16).reshape(rows, grad.shape[0] // rows, cols, grad.shape[1] // cols)
    blocks = blocks.transpose(0, 2, 1, 3).reshape(rows * cols, grad.shape[0] // rows, grad.shape[1] // cols)
    return lax.psum_scatter(blocks, BOTH, scatter_dimension=0, tiled=False).astype(jnp.float32)


def across(value, shift):
    return lax.ppermute(value, "row", [(r, r ^ shift) for r in range(lax.axis_size("row"))])


def row_gather(block):
    beside = across(block, 1)
    below = across(block, 2)
    return [block, beside, below, across(beside[:ROW_CUT], 2), across(below[ROW_CUT:], 1)]


def row_starts(rows):
    me = lax.axis_index("row")
    far = (me ^ 3) * rows
    return [me * rows, (me ^ 1) * rows, (me ^ 2) * rows, far, far + ROW_CUT]


def core_swap(place, value):
    return lax.ppermute(value, "col", place.part_perm(1))


def far_sums(own, swapped):
    f32, bf16 = jnp.float32, jnp.bfloat16
    total = (own[3].astype(f32) + swapped[3].astype(f32)).astype(bf16)
    return total[:ROW_CUT], total[ROW_CUT:]


def far_sends(sums):
    return across(sums[0], 2), across(sums[1], 1)


def near_sums(own, swapped, received):
    f32 = jnp.float32
    beside = own[1].astype(f32) + swapped[1].astype(f32)
    below = own[2].astype(f32) + swapped[2].astype(f32)
    beside = jnp.concatenate([beside[:ROW_CUT] + received[0].astype(f32), beside[ROW_CUT:]], axis=0)
    below = jnp.concatenate([below[:ROW_CUT], below[ROW_CUT:] + received[1].astype(f32)], axis=0)
    return beside.astype(jnp.bfloat16), below.astype(jnp.bfloat16)


def near_sends(sums):
    return across(sums[0], 1), across(sums[1], 2)


def row_total(own, swapped, last):
    f32 = jnp.float32
    base = own[0].astype(f32) + swapped[0].astype(f32)
    return (base + last[0].astype(f32) + last[1].astype(f32)).astype(jnp.bfloat16)


def pack_pair(w_up, w_down):
    main = w_up.shape[1] // 256 * 256
    down = w_down.T
    parts = []
    for start in range(0, main, FF_BLOCK):
        parts += [w_up[:, start : start + FF_BLOCK], down[:, start : start + FF_BLOCK]]
    return jnp.concatenate(parts + [w_up[:, main:], down[:, main:]], axis=1)


class QuickWeights:
    def __init__(self, place, w_qkv, w_out, w_up, w_down, padded):
        self.place, self.padded = place, padded
        self.rows = w_qkv.shape[0]
        self.cols = place.columns
        self.width = w_out.shape[1] * self.cols
        self.qkv_cols, self.out_cols, self.up_cols = w_qkv.shape[1], w_out.shape[1], w_up.shape[1]
        self.main = main = self.up_cols // 256 * 256
        self.rest = rest = self.up_cols - main
        self.role = place.part
        self.scalars = jnp.stack([self.role] + row_starts(self.rows)).astype(jnp.int32)
        self.pack = pack_pair(w_up, w_down)

    def start(self, w_qkv, w_out, value):
        full, rows, pack = start_exchange(
            jnp.concatenate([w_qkv, w_out], axis=1), self.pack, value, self.place.count
        )
        place = self.place
        pieces = [pack] + [
            lax.ppermute(pack, "col", place.quarter_perm(d)) for d in range(1, place.micro)
        ]
        self.own = in_order(place.quarter ^ jnp.arange(place.micro, dtype=jnp.int32), pieces)
        self.beside, self.below = across(self.own, 1), across(self.own, 2)
        self.far = (self.beside[:2], self.below[2:])
        mine = [self.own, self.beside, self.below, across(self.far[0], 2), across(self.far[1], 1)]
        self.pair = (mine, [core_swap(place, piece) for piece in mine])
        self.triple, self.out = assemble(full, self.width, self.padded, self.qkv_cols)
        return rows

    def end(self, triple_grad, out_grad, small, rows, shape, deps):
        blocks = divide(
            triple_grad, out_grad, self.width, self.padded, self.qkv_cols, self.out_cols, self.cols, 4
        )
        final, summed, tokens = end_exchange(blocks, small, rows, shape, deps)
        return final[:, : self.qkv_cols], final[:, self.qkv_cols :], summed, tokens

    def bias_order(self, bias):
        blocks = bias.reshape(self.place.micro, self.place.parts, self.up_cols).transpose(1, 0, 2)
        blocks = blocks.reshape(self.cols, self.up_cols)
        return jnp.concatenate([blocks[:, : self.main].reshape(-1), blocks[:, self.main :].reshape(-1)])

    def bias_back(self, grad):
        edge = self.cols * self.main
        blocks = jnp.concatenate(
            [grad[:edge].reshape(self.cols, self.main), grad[edge:].reshape(self.cols, self.rest)], axis=1
        )
        blocks = blocks.reshape(self.place.parts, self.place.micro, self.up_cols)
        return blocks.transpose(1, 0, 2).reshape(-1)

    def pair_final(self, parts):
        final = jnp.sum(parts.astype(jnp.float32), axis=0)
        main, rest = self.main, self.rest
        own = jnp.concatenate([final[:, :main], final[:, 2 * main : 2 * main + rest]], axis=1)
        far = jnp.concatenate([final[:, main : 2 * main], final[:, 2 * main + rest :]], axis=1)
        up = jnp.where(self.role == 0, own, far)
        down = jnp.where(self.role == 0, far, own)
        return up, down.T


class PlainWeights:
    def __init__(self, place, w_qkv, w_out, w_up, w_down, padded):
        self.place, self.padded = place, padded
        qkv, out = plain_gather(w_qkv), plain_gather(w_out)
        self.width = width = out.shape[1]
        pad = padded - width
        self.triple = jnp.pad(qkv.reshape(width, 3, width), ((0, 0), (0, 0), (0, pad))).reshape(
            width, 3 * padded
        )
        self.out = jnp.pad(out, ((0, pad), (0, pad)))
        self.rows, self.cols, self.up_cols = w_qkv.shape[0], place.columns, w_up.shape[1]
        self.main = self.up_cols // 256 * 256
        self.rest = self.up_cols - self.main
        full = lax.all_gather(pack_pair(w_up, w_down), BOTH, axis=0, tiled=False)
        full = full.reshape(lax.axis_size("row"), self.cols, self.rows, 2 * self.up_cols)
        self.pair = (full.transpose(1, 0, 2, 3).reshape(1, self.cols, width, 2 * self.up_cols),)
        self.scalars = jnp.zeros((2,), jnp.int32)

    def bias_order(self, bias):
        blocks = bias.reshape(self.cols, self.up_cols)
        return jnp.concatenate([blocks[:, : self.main].reshape(-1), blocks[:, self.main :].reshape(-1)])

    def bias_back(self, grad):
        edge = self.cols * self.main
        return jnp.concatenate(
            [grad[:edge].reshape(self.cols, self.main), grad[edge:].reshape(self.cols, self.rest)], axis=1
        ).reshape(-1)

    def natural(self, grad):
        edge = self.cols * self.main
        cut = lambda value: value.reshape(grad.shape[0], self.cols, -1)
        return jnp.concatenate([cut(grad[:, :edge]), cut(grad[:, edge:])], axis=2).reshape(grad.shape)

    def scatter_pair(self, mine, theirs):
        return plain_scatter(self.natural(mine)), plain_scatter(self.natural(theirs)).T

    def scatter_first(self, triple_grad, out_grad):
        width, padded = self.width, self.padded
        qkv = triple_grad.reshape(width, 3, padded)[:, :, :width].reshape(width, 3 * width)
        return plain_scatter(qkv), plain_scatter(out_grad[:, :width])


def cuts_of(pairs, count):
    edges = [round(i * pairs / count) for i in range(count + 1)]
    return list(zip(edges[:-1], edges[1:]))


def local(
    block_input, paths, ln1_gain, ln1_bias, w_qkv, q_bias, v_bias, w_out, out_bias,
    ln2_gain, ln2_bias, w_up, up_bias, w_down, down_bias, cotangent,
):
    micro, _, width = block_input.shape
    place = Place(micro, paths.shape[2])
    parts = place.parts
    heads = width // HEAD_DIM
    padded = (heads + 1) // 2 * 128
    pairs = padded // 128
    pad = padded - width
    own_trunk = TRUNK // parts
    f32, bf16 = jnp.float32, jnp.bfloat16

    quick = lax.axis_size("row") == 4 and parts == 2 and w_qkv.shape[0] == 272
    if quick:
        weights = QuickWeights(place, w_qkv, w_out, w_up, w_down, padded)
        rows_low = weights.start(w_qkv, w_out, block_input)
    else:
        weights = PlainWeights(place, w_qkv, w_out, w_up, w_down, padded)
        rows_low = place.to_tree(place.tree_sources(place.swap_quarters(block_input)))
    rows_in = rows_low.astype(f32)

    own_ids = lax.dynamic_index_in_dim(paths[0], place.quarter, 0, keepdims=False)
    parent_ids = lax.dynamic_index_in_dim(paths[1], place.quarter, 0, keepdims=False)
    mask_trunk, mask_group = place.masks(own_ids, parent_ids)

    seed_moved = place.swap_quarters(after(cotangent, weights.own) if quick else cotangent)

    q_scale = HEAD_DIM**-0.5 * LOG2E
    triple_bias = jnp.concatenate(
        [jnp.pad(q_bias * q_scale, (0, pad)), jnp.zeros((padded,), f32), jnp.pad(v_bias, (0, pad))]
    )
    triple_scale = jnp.concatenate([jnp.full((padded,), q_scale, f32), jnp.ones((2 * padded,), f32)])
    first = layer_norm(rows_in, ln1_gain, ln1_bias).astype(bf16)
    triple = (dot_nn(first, weights.triple) * triple_scale + triple_bias).astype(bf16)
    shared = triple[:own_trunk, padded:]
    others = jnp.concatenate(
        [lax.ppermute(shared, "col", place.part_perm(e)) for e in range(1, parts)], axis=0
    )
    cuts = [round(pairs * part / 9) for part in (0, 6, 8, 9)]
    before, gates = (), ((), (), ())
    if quick:
        gates = ((weights.own,), weights.far, tuple(weights.pair[0][3:]))
    for start, stop, deps in zip(cuts[:-1], cuts[1:], gates):
        before = attention_forward(
            parts, heads, triple, others, mask_trunk, mask_group, start, stop, before, deps
        )
    mixed, lse = before
    seed_rows = place.to_tree(place.tree_sources(after(seed_moved, mixed)))
    middle, second = project_out(mixed, rows_low, weights.out, out_bias, ln2_gain, ln2_bias)
    outs = 4 if quick else 1
    lowered, second_grad, up_bias_grad, *pair_grads = feed_forward(
        weights.scalars, weights.pair, second, seed_rows, weights.bias_order(up_bias), outs
    )
    pair_mine, pair_theirs = pair_grads[:outs], pair_grads[outs:]
    up_bias_grad = weights.bias_back(up_bias_grad.reshape(-1))
    far = ()
    if quick:
        pair_swapped = {d: core_swap(place, pair_theirs[d]) for d in (3, 1, 2, 0)}
        far = far_sums(pair_mine, pair_swapped)
        received = far_sends(far)
    result, middle_grad, mixed_grad, sums, out_padded = middle_back(
        second_grad, lowered, middle, seed_rows, mixed, weights.out, ln2_gain, down_bias, far
    )
    out_bias_grad, gain_two, shift_two, down_bias_grad = sums[0], sums[1], sums[2], sums[3]

    turned = jnp.swapaxes(mask_trunk, 1, 2), jnp.swapaxes(mask_group, 1, 2)
    result_sources = place.from_tree_sources(result)
    result_parts = place.from_tree_parts(result_sources)
    result_out = place.swap_quarters(result_parts)
    cut = 5 * pairs // 9
    deps = (result_parts,)
    if quick:
        near = near_sums(pair_mine, pair_swapped, received)
        last = near_sends(near)
        deps += near
    inputs = parts, heads, triple, others, mixed, mixed_grad, lse, *turned
    grads = attention_backward(*inputs, 0, cut, (), deps)
    deps = ()
    if quick:
        last = after(last[0], grads[0]), last[1]
        total = row_total(pair_mine, pair_swapped, last)
        deps = (total,)
    grads = attention_backward(*inputs, cut, pairs, grads, deps)
    finish_deps, first_deps = (), ()
    if quick:
        blocks = pair_blocks(
            place.part.reshape(1).astype(jnp.int32), total, core_swap(place, total), weights.main, weights.rest
        )
        pair_parts = place.swap_quarters(blocks)
        finish_deps = (blocks,)
    else:
        up_grad, down_grad = weights.scatter_pair(pair_mine[0], pair_theirs[0])
    dq, dk, dv, dko, dvo = grads
    other_k, other_v = (
        jnp.concatenate(
            [
                lax.ppermute(part[(e - 1) * own_trunk : e * own_trunk], "col", place.part_perm(e))
                for e in range(1, parts)
            ],
            axis=0,
        )
        for part in (dko, dvo)
    )
    triple_grad, triple_sums = finish_gradients(own_trunk, dq, dk, dv, other_k, other_v, finish_deps)
    q_bias_grad = triple_sums[0, :width]
    v_bias_grad = triple_sums[0, 2 * padded : 2 * padded + width]
    input_grad, sums = first_back(
        triple_grad, rows_low, middle_grad, weights.triple, ln1_gain, first_deps
    )
    gain_one, shift_one = sums[0], sums[1]
    triple_weight_grad = dot_tn(first, triple_grad).astype(bf16)
    small = [
        gain_one, shift_one, q_bias_grad, v_bias_grad, out_bias_grad, gain_two, shift_two, up_bias_grad,
        down_bias_grad,
    ]
    if quick:
        up_grad, down_grad = weights.pair_final(pair_parts)
        flat = jnp.concatenate(small)
        flat = jnp.pad(flat, (0, -flat.shape[0] % 1024)).reshape(-1, 128)
        qkv_grad, out_grad, flat, input_grad_out = weights.end(
            triple_weight_grad, out_padded, flat, input_grad, block_input.shape, (up_grad, down_grad)
        )
        edges = np.cumsum([0] + [v.shape[0] for v in small])
        flat = flat.reshape(-1)
        small = [flat[low:high] for low, high in zip(edges[:-1], edges[1:])]
    else:
        qkv_grad, out_grad = weights.scatter_first(triple_weight_grad, out_padded)
        small = lax.psum(small, BOTH)
        input_grad_out = place.swap_quarters(
            place.from_tree_parts(place.from_tree_sources(input_grad))
        )
    return (
        result_out, input_grad_out, small[0], small[1], qkv_grad, small[2], small[3],
        out_grad, small[4], small[5], small[6], up_grad, small[7], down_grad, small[8],
    )


def solution(mesh):
    rows = P(None, BOTH, None)
    placed = (
        rows, P(None, None, "row"), P(), P(), P("row", "col"), P(), P(), P("row", "col"), P(),
        P(), P(), P("row", "col"), P(), P("col", "row"), P(), rows,
    )
    out = (
        rows, rows, P(), P(), P("row", "col"), P(), P(), P("row", "col"), P(),
        P(), P(), P("row", "col"), P(), P("col", "row"), P(),
    )
    return jax.shard_map(local, mesh=mesh, in_specs=placed, out_specs=out, check_vma=False)
```
